32 devices in a mesh: dp: 2 (over core), seq: 4 (over y, x), tp: 4 (over z).
Axes of the slice: x: 2, y: 2, z: 4, core: 2. Of those that a mesh axis runs over, the one named last changes fastest.
Arguments:
- tokens: bfloat16 [4, 1024, 2048], P('dp', 'seq'), may hold values from -6 to 6
- w_query: bfloat16 [2048, 2048], P(('dp', 'seq'), 'tp'), as said below
- w_key: bfloat16 [2048, 2048], P(('dp', 'seq'), 'tp'), as said below
- w_value: bfloat16 [2048, 2048], P(('dp', 'seq'), 'tp'), may hold values from -0.125 to 0.125
- w_out: bfloat16 [2048, 2048], P('tp', ('dp', 'seq')), may hold values from -0.125 to 0.125
- w_gate: bfloat16 [2048, 8192], P(('dp', 'seq'), 'tp'), may hold values from -0.125 to 0.125
- w_up: bfloat16 [2048, 8192], P(('dp', 'seq'), 'tp'), may hold values from -0.125 to 0.125
- w_down: bfloat16 [8192, 2048], P('tp', ('dp', 'seq')), may hold values from -0.0625 to 0.0625
- q_gain: bfloat16 [16, 128], P('tp', ('dp', 'seq')), may hold values from 1 to 2
- k_gain: bfloat16 [16, 128], P('tp', ('dp', 'seq')), may hold values from 0.5 to 1.5
- attn_gain: bfloat16 [16, 128], P(None, ('dp', 'seq')), may hold values from 0.5 to 1.5
- mlp_gain: bfloat16 [16, 128], P(None, ('dp', 'seq')), may hold values from 0.5 to 1.5
- cotangent: bfloat16 [4, 1024, 2048], P('dp', ('seq', 'tp')), may hold values from -6 to 6
Outputs:
- outputs: bfloat16 [4, 1024, 2048], P('dp', ('seq', 'tp'))
- grad_tokens: float32 [4, 1024, 2048], P('dp', ('seq', 'tp'))
- grad_w_query: float32 [2048, 2048], P(('dp', 'seq'), 'tp')
- grad_w_key: float32 [2048, 2048], P(('dp', 'seq'), 'tp')
- grad_w_value: float32 [2048, 2048], P(('dp', 'seq'), 'tp')
- grad_w_out: float32 [2048, 2048], P('tp', ('dp', 'seq'))
- grad_w_gate: float32 [2048, 8192], P(('dp', 'seq'), 'tp')
- grad_w_up: float32 [2048, 8192], P(('dp', 'seq'), 'tp')
- grad_w_down: float32 [8192, 2048], P('tp', ('dp', 'seq'))
- grad_q_gain: float32 [16, 128], P('tp', ('dp', 'seq'))
- grad_k_gain: float32 [16, 128], P('tp', ('dp', 'seq'))
- grad_attn_gain: float32 [16, 128], P('tp', ('dp', 'seq'))
- grad_mlp_gain: float32 [16, 128], P('tp', ('dp', 'seq'))
The draws below stay inside these ranges and needn't reach their ends.
Inputs may be any that keep to these rules, and one draw needn't show every extreme that they name: `w_query`: entries at most 7 / sqrt(2048) in magnitude. `w_key`: entries at most 7 / sqrt(2048) in magnitude.
All inputs are finite; a program needn't handle non-finite values.
Results may differ from the reference program's by a relative error of at most 0.02.
Values may be sent and summed in bfloat16 or wider, within the bound.
No kernel may reach another device: no remote copies, remote signals or barrier semaphores. Data moves between devices by JAX's collectives and lax.ppermute only.
A program may use at most 192 MiB of HBM per device.

```python
import math
import jax
import jax.numpy as jnp
from jax import lax

D = 2048
HEADS = 16
HEAD_DIM = 128
FF = 8192
SEQLEN = 1024
SEQS = 4


def head_rising(entries, rise):
    heads = jnp.arange(D, dtype=jnp.int32) // HEAD_DIM
    factor = jnp.exp(heads.astype(jnp.float32) * (0.5 * math.log(rise) / (HEADS - 1)))
    return entries * factor[None, :] * D ** (-0.5)


def draw_w_query(key, part):
    key = jax.random.fold_in(key, 11)
    entries = jnp.clip(jax.random.normal(key, (D, D), jnp.float32), -4.0, 4.0)
    return head_rising(entries, 3.0).astype(jnp.bfloat16)


def draw_w_key(key, part):
    key = jax.random.fold_in(key, 12)
    entries = jnp.clip(jax.random.normal(key, (D, D), jnp.float32), -4.0, 4.0)
    return head_rising(entries, 3.0).astype(jnp.bfloat16)


def levels(key, dims, shards, low, largest):
    loudness, own = 1.0, jax.random.fold_in(key, 6)
    for position, blocks in shards:
        draws = jnp.exp(jax.random.uniform(jax.random.fold_in(own, position), (blocks,), jnp.float32, low / len(shards), largest / len(shards)))
        loudness = loudness * jnp.repeat(draws, dims[position] // blocks).reshape([-1 if axis == position else 1 for axis in range(len(dims))])
    return loudness


def bell_draw(stream_key, shape, spread, limit, split=(), held_as=jnp.bfloat16):
    result = jax.random.normal(stream_key, shape, jnp.float32) * spread
    if len(split) > 0:
        result = levels(stream_key, shape, split, -0.22, 0.18) * result
    return jnp.clip(result, min=-limit, max=limit).astype(held_as)


def setup_inputs(seed: int = 0) -> dict:
    splits = jax.random.split(jax.random.key(seed), 14)
    return {
        "tokens": bell_draw(splits[0], (SEQS, SEQLEN, D), 1.0, 6.0, ((0, 2), (1, 4))),
        "w_query": draw_w_query(jax.random.fold_in(splits[13], 71), 0),
        "w_key": draw_w_key(jax.random.fold_in(splits[13], 71), 0),
        "w_value": bell_draw(splits[3], (D, D), D ** -0.5, 0.125, ((0, 8), (1, 4))),
        "w_out": bell_draw(splits[4], (D, D), D ** -0.5, 0.125, ((0, 4), (1, 8))),
        "w_gate": bell_draw(splits[5], (D, FF), D ** -0.5, 0.125, ((0, 8), (1, 4))),
        "w_up": bell_draw(splits[6], (D, FF), D ** -0.5, 0.125, ((0, 8), (1, 4))),
        "w_down": bell_draw(splits[7], (FF, D), FF ** -0.5, 0.0625, ((0, 4), (1, 8))),
        "q_gain": jnp.clip(1.0 + 1.0 * jax.random.uniform(splits[8], (HEADS, HEAD_DIM), jnp.float32) ** levels(splits[8], (HEADS, HEAD_DIM), ((0, 4), (1, 8)), -0.2, 0.2), 1.0, 2.0).astype(jnp.bfloat16),
        "k_gain": jnp.clip(0.5 + 1.0 * jax.random.uniform(splits[9], (HEADS, HEAD_DIM), jnp.float32) ** levels(splits[9], (HEADS, HEAD_DIM), ((0, 4), (1, 8)), -0.2, 0.2), 0.5, 1.5).astype(jnp.bfloat16),
        "attn_gain": jnp.clip(1.0 + 0.1 * jax.random.normal(splits[10], (HEADS, HEAD_DIM), jnp.float32), 0.5, 1.5).astype(jnp.bfloat16),
        "mlp_gain": jnp.clip(1.0 + 0.1 * jax.random.normal(splits[11], (HEADS, HEAD_DIM), jnp.float32), 0.5, 1.5).astype(jnp.bfloat16),
        "cotangent": bell_draw(splits[12], (SEQS, SEQLEN, D), 1.0, 6.0, ((0, 2), (1, 16))),
    }


NORM_EPS = 1e-06
ROPE_BASE = 500000.0
MASKED = -1e+30
PRECISE = lax.Precision.HIGHEST

@jax.custom_vjp
def low(v):
    return lax.optimization_barrier(v.astype(jnp.bfloat16)).astype(jnp.float32)

@jax.custom_vjp
def low_back(v):
    return v

def low_keep(v):
    return (low(v), None)

def low_pass(kept, grad):
    return (grad,)

def back_keep(v):
    return (v, None)

def back_low(kept, grad):
    return (low(grad),)
low.defvjp(low_keep, low_pass)
low_back.defvjp(back_keep, back_low)

def matmul(left, right):
    return jnp.dot(left, right, precision=PRECISE, preferred_element_type=jnp.float32)

def rms_scale(values):
    return lax.rsqrt(lax.optimization_barrier(jnp.mean(values * values, axis=-1, keepdims=True)) + NORM_EPS)

def rope_tables(positions, head_dim):
    steps = jnp.arange(head_dim // 2, dtype=jnp.float32)
    freqs = jnp.exp(steps * (-2.0 * math.log(ROPE_BASE) / head_dim))
    angles = positions.astype(jnp.float32)[:, None] * freqs[None, :]
    return (jnp.cos(angles)[:, None, :], jnp.sin(angles)[:, None, :])

def rotate(values, cosines, sines):
    half = values.shape[-1] // 2
    first = values[..., :half]
    second = values[..., half:]
    return jnp.concatenate([first * cosines - second * sines, second * cosines + first * sines], axis=-1)

def sequence_layer(seq_tokens, weights):
    w_query, w_key, w_value, w_out, w_gate, w_up, w_down, q_gain, k_gain, attn_gain, mlp_gain = weights
    length = seq_tokens.shape[0]
    query_raw = low_back(matmul(seq_tokens, w_query))
    key_raw = low_back(matmul(seq_tokens, w_key))
    value_raw = low_back(matmul(seq_tokens, w_value))
    query_norm = query_raw * rms_scale(query_raw) * q_gain
    key_norm = key_raw * rms_scale(key_raw) * k_gain
    positions = jnp.arange(length, dtype=jnp.int32)
    cosines, sines = rope_tables(positions, HEAD_DIM)
    queries = low(rotate(query_norm.reshape(length, HEADS, HEAD_DIM), cosines, sines))
    keys = low(rotate(key_norm.reshape(length, HEADS, HEAD_DIM), cosines, sines))
    values = low(value_raw).reshape(length, HEADS, HEAD_DIM)
    block_rows = min(512, length)
    score_scale = HEAD_DIM ** (-0.5)

    def attend(block_index):
        first_row = block_index * block_rows
        query_block = lax.dynamic_slice_in_dim(queries, first_row, block_rows, 0)
        scores = jnp.einsum('qhd,khd->hqk', query_block, keys, precision=PRECISE) * score_scale
        scores = low_back(scores)
        query_pos = first_row + jnp.arange(block_rows, dtype=jnp.int32)
        allowed = positions[None, :] <= query_pos[:, None]
        scores = jnp.where(allowed[None], scores, MASKED)
        row_max = lax.optimization_barrier(jnp.max(scores, axis=-1, keepdims=True))
        log_total = row_max + jnp.log(lax.optimization_barrier(jnp.sum(jnp.exp(scores - row_max), axis=-1, keepdims=True)))
        probs = low(jnp.exp(scores - log_total))
        return jnp.einsum('hqk,khd->qhd', probs, values, precision=PRECISE)
    context = lax.map(jax.checkpoint(attend), jnp.arange(length // block_rows, dtype=jnp.int32))
    context = low(low_back(context.reshape(length, HEADS * HEAD_DIM)))
    attn_out = low_back(matmul(context, w_out))
    hidden = seq_tokens + attn_out * rms_scale(attn_out) * attn_gain
    hidden_low = low(hidden)
    gate = low_back(matmul(hidden_low, w_gate))
    up_act = low_back(matmul(hidden_low, w_up))
    mixed = low(jax.nn.silu(gate) * up_act)
    mlp_out = low_back(matmul(mixed, w_down))
    return hidden + mlp_out * rms_scale(mlp_out) * mlp_gain

def reference(tokens, w_query, w_key, w_value, w_out, w_gate, w_up, w_down, q_gain, k_gain, attn_gain, mlp_gain, cotangent):
    weights = (w_query.astype(jnp.float32), w_key.astype(jnp.float32), w_value.astype(jnp.float32), w_out.astype(jnp.float32), w_gate.astype(jnp.float32), w_up.astype(jnp.float32), w_down.astype(jnp.float32), q_gain.astype(jnp.float32).reshape(D), k_gain.astype(jnp.float32).reshape(D), attn_gain.astype(jnp.float32).reshape(D), mlp_gain.astype(jnp.float32).reshape(D))

    def layer_all(token_values, weight_values):

        def one_sequence(seq_tokens):
            return sequence_layer(seq_tokens, weight_values)
        return lax.map(jax.checkpoint(one_sequence), token_values)
    outputs, pullback = jax.vjp(layer_all, tokens.astype(jnp.float32), weights)
    grad_tokens, grads = pullback(cotangent.astype(jnp.float32))
    return (outputs.astype(jnp.bfloat16), grad_tokens, grads[0], grads[1], grads[2], grads[3], grads[4], grads[5], grads[6], grads[7].reshape(HEADS, HEAD_DIM), grads[8].reshape(HEADS, HEAD_DIM), grads[9].reshape(HEADS, HEAD_DIM), grads[10].reshape(HEADS, HEAD_DIM))
```

```python
import math

import jax
import jax.numpy as jnp
from jax import lax
from jax.experimental import pallas as pl
from jax.experimental.pallas import tpu as pltpu
from jax.sharding import PartitionSpec as P

NORM_EPS = 1e-06
ROPE_BASE = 500000.0
MASKED = -1e30


def project(left, right):
    return jnp.dot(left, right, preferred_element_type=jnp.float32)


def project_back(left, right):
    return lax.dot_general(
        left, right, (((left.ndim - 1,), (1,)), ((), ())), preferred_element_type=jnp.float32
    )


def outer_sum(left, right):
    return lax.dot_general(
        left, right, (((0, 1), (0, 1)), ((), ())), preferred_element_type=jnp.float32
    )


def rope_tables(positions, head_dim):
    steps = jnp.arange(head_dim // 2, dtype=jnp.float32)
    freqs = jnp.exp(steps * (-2.0 * math.log(ROPE_BASE) / head_dim))
    angles = positions.astype(jnp.float32)[:, None] * freqs[None, :]
    return (jnp.cos(angles)[:, None, :], jnp.sin(angles)[:, None, :])


def rotate(values, cosines, sines):
    half = values.shape[-1] // 2
    first = values[..., :half]
    second = values[..., half:]
    return jnp.concatenate(
        [first * cosines - second * sines, second * cosines + first * sines], axis=-1
    )


def unrotate(grads, cosines, sines):
    half = grads.shape[-1] // 2
    first = grads[..., :half]
    second = grads[..., half:]
    return jnp.concatenate(
        [first * cosines + second * sines, second * cosines - first * sines], axis=-1
    )


def norm_back(normed, grad_normed, inv_scale, total_dot, d_model):
    return inv_scale * (grad_normed - normed * (total_dot / d_model)[..., None])


def on_any_mesh(
    tokens,
    w_query,
    w_key,
    w_value,
    w_out,
    w_gate,
    w_up,
    w_down,
    q_gain,
    k_gain,
    attn_gain,
    mlp_gain,
    cotangent,
):
    seq_count, local_len, d_model = tokens.shape
    seq_rank = lax.axis_index("seq")
    tp_rank = lax.axis_index("tp")
    own_rows = local_len // lax.axis_size("tp")
    weights_in = (
        lax.all_gather(w_query, ("dp", "seq"), axis=0, tiled=True),
        lax.all_gather(w_key, ("dp", "seq"), axis=0, tiled=True),
        lax.all_gather(w_value, ("dp", "seq"), axis=0, tiled=True),
        lax.all_gather(w_out, ("dp", "seq"), axis=1, tiled=True),
        lax.all_gather(w_gate, ("dp", "seq"), axis=0, tiled=True),
        lax.all_gather(w_up, ("dp", "seq"), axis=0, tiled=True),
        lax.all_gather(w_down, ("dp", "seq"), axis=1, tiled=True),
        lax.all_gather(q_gain, ("dp", "seq"), axis=1, tiled=True),
        lax.all_gather(k_gain, ("dp", "seq"), axis=1, tiled=True),
        lax.all_gather(attn_gain, ("dp", "seq"), axis=1, tiled=True),
        lax.all_gather(mlp_gain, ("dp", "seq"), axis=1, tiled=True),
    )
    (
        full_query,
        full_key,
        full_value,
        full_out,
        full_gate,
        full_up,
        full_down,
        full_qgain,
        full_kgain,
        full_again,
        full_mgain,
    ) = weights_in
    local_heads = full_qgain.shape[0]
    head_dim = full_qgain.shape[1]
    head_span = local_heads * head_dim
    score_scale = head_dim ** (-0.5)
    query_gain = full_qgain.astype(jnp.float32).reshape(head_span)
    key_gain = full_kgain.astype(jnp.float32).reshape(head_span)
    attn_scale_gain = full_again.astype(jnp.float32).reshape(d_model)
    mlp_scale_gain = full_mgain.astype(jnp.float32).reshape(d_model)
    query_raw = project(tokens, full_query)
    key_raw = project(tokens, full_key)
    value_raw = project(tokens, full_value)
    query_sq, key_sq = lax.psum(
        (jnp.sum(query_raw * query_raw, axis=-1), jnp.sum(key_raw * key_raw, axis=-1)), "tp"
    )
    query_inv = lax.rsqrt(query_sq / d_model + NORM_EPS)[..., None]
    key_inv = lax.rsqrt(key_sq / d_model + NORM_EPS)[..., None]
    query_unit = query_raw * query_inv
    key_unit = key_raw * key_inv
    positions = seq_rank * local_len + jnp.arange(local_len, dtype=jnp.int32)
    cosines, sines = rope_tables(positions, head_dim)
    heads_shape = (seq_count, local_len, local_heads, head_dim)
    queries = rotate((query_unit * query_gain).reshape(heads_shape), cosines, sines).astype(
        jnp.bfloat16
    )
    keys_local = (
        rotate((key_unit * key_gain).reshape(heads_shape), cosines, sines)
        .astype(jnp.bfloat16)
        .reshape(seq_count, local_len, head_span)
    )
    values_local = value_raw.astype(jnp.bfloat16)
    all_keys, all_values = (
        lax.all_gather(keys_local, "seq", axis=1, tiled=True),
        lax.all_gather(values_local, "seq", axis=1, tiled=True),
    )
    length = all_keys.shape[1]
    keys_full = all_keys.reshape(seq_count, length, local_heads, head_dim)
    values_full = all_values.reshape(seq_count, length, local_heads, head_dim)
    key_rows = min(512, length)
    block_ids = jnp.arange(length // key_rows, dtype=jnp.int32)

    def key_block(block_index):
        first_key = block_index * key_rows
        key_part = lax.dynamic_slice_in_dim(keys_full, first_key, key_rows, 1)
        value_part = lax.dynamic_slice_in_dim(values_full, first_key, key_rows, 1)
        scores = (
            jnp.einsum("mqhd,mkhd->mhqk", queries, key_part, preferred_element_type=jnp.float32)
            * score_scale
        )
        allowed = (first_key + jnp.arange(key_rows, dtype=jnp.int32))[None, :] <= positions[:, None]
        return (key_part, value_part, jnp.where(allowed, scores, MASKED), allowed)

    def max_step(state, block_index):
        running_max, running_sum = state
        key_part, value_part, scores, allowed = key_block(block_index)
        new_max = jnp.maximum(running_max, jnp.max(scores, axis=-1))
        weights_now = jnp.where(allowed, jnp.exp(scores - new_max[..., None]), 0.0)
        return (
            (new_max, running_sum * jnp.exp(running_max - new_max) + jnp.sum(weights_now, axis=-1)),
            None,
        )

    stat_shape = (seq_count, local_heads, local_len)
    final_state, unused = lax.scan(
        max_step,
        (jnp.full(stat_shape, MASKED, jnp.float32), jnp.zeros(stat_shape, jnp.float32)),
        block_ids,
    )
    log_total = (final_state[0] + jnp.log(final_state[1]))[..., None]

    def context_step(context, block_index):
        key_part, value_part, scores, allowed = key_block(block_index)
        probs = jnp.where(allowed, jnp.exp(scores - log_total), 0.0).astype(jnp.bfloat16)
        return (
            context
            + jnp.einsum("mhqk,mkhd->mqhd", probs, value_part, preferred_element_type=jnp.float32),
            None,
        )

    context, unused = lax.scan(context_step, jnp.zeros(heads_shape, jnp.float32), block_ids)
    context_low = context.astype(jnp.bfloat16).reshape(seq_count, local_len, head_span)
    attn_out = lax.psum_scatter(
        project(context_low, full_out), "tp", scatter_dimension=1, tiled=True
    )
    attn_inv = lax.rsqrt(jnp.mean(attn_out * attn_out, axis=-1, keepdims=True) + NORM_EPS)
    attn_unit = attn_out * attn_inv
    own_tokens = lax.dynamic_slice_in_dim(tokens, tp_rank * own_rows, own_rows, 1).astype(
        jnp.float32
    )
    hidden = own_tokens + attn_unit * attn_scale_gain
    hidden_all = lax.all_gather(hidden.astype(jnp.bfloat16), "tp", axis=1, tiled=True)
    gate_act = project(hidden_all, full_gate)
    up_act = project(hidden_all, full_up)
    gate_sig = jax.nn.sigmoid(gate_act)
    mixed = (gate_act * gate_sig * up_act).astype(jnp.bfloat16)
    mlp_out = lax.psum_scatter(project(mixed, full_down), "tp", scatter_dimension=1, tiled=True)
    mlp_inv = lax.rsqrt(jnp.mean(mlp_out * mlp_out, axis=-1, keepdims=True) + NORM_EPS)
    mlp_unit = mlp_out * mlp_inv
    outputs = (hidden + mlp_unit * mlp_scale_gain).astype(jnp.bfloat16)
    weights_back = (
        lax.all_gather(w_query, ("dp", "seq"), axis=0, tiled=True),
        lax.all_gather(w_key, ("dp", "seq"), axis=0, tiled=True),
        lax.all_gather(w_value, ("dp", "seq"), axis=0, tiled=True),
        lax.all_gather(w_out, ("dp", "seq"), axis=1, tiled=True),
        lax.all_gather(w_gate, ("dp", "seq"), axis=0, tiled=True),
        lax.all_gather(w_up, ("dp", "seq"), axis=0, tiled=True),
        lax.all_gather(w_down, ("dp", "seq"), axis=1, tiled=True),
    )
    back_query, back_key, back_value, back_out, back_gate, back_up, back_down = weights_back
    grad_out = cotangent.astype(jnp.float32)
    grad_mgain = jnp.sum(grad_out * mlp_unit, axis=(0, 1))
    mlp_scaled = grad_out * mlp_scale_gain
    grad_mlp = norm_back(
        mlp_unit, mlp_scaled, mlp_inv, jnp.sum(mlp_scaled * mlp_unit, axis=-1), d_model
    ).astype(jnp.bfloat16)
    grad_mlp_all = lax.all_gather(grad_mlp, "tp", axis=1, tiled=True)
    grad_wdown = outer_sum(mixed, grad_mlp_all)
    grad_mixed = project_back(grad_mlp_all, back_down)
    grad_gate = (grad_mixed * up_act * gate_sig * (1.0 + gate_act * (1.0 - gate_sig))).astype(
        jnp.bfloat16
    )
    grad_up = (grad_mixed * gate_act * gate_sig).astype(jnp.bfloat16)
    grad_wgate = outer_sum(hidden_all, grad_gate)
    grad_wup = outer_sum(hidden_all, grad_up)
    hidden_part = project_back(grad_gate, back_gate) + project_back(grad_up, back_up)
    hidden_sum, grad_mgain_part = (
        lax.psum_scatter(hidden_part, "tp", scatter_dimension=1, tiled=True),
        lax.psum_scatter(grad_mgain.reshape(-1, head_dim), "tp", scatter_dimension=0, tiled=True),
    )
    grad_hidden = grad_out + hidden_sum
    grad_again = jnp.sum(grad_hidden * attn_unit, axis=(0, 1))
    attn_scaled = grad_hidden * attn_scale_gain
    grad_attn = norm_back(
        attn_unit, attn_scaled, attn_inv, jnp.sum(attn_scaled * attn_unit, axis=-1), d_model
    ).astype(jnp.bfloat16)
    grad_attn_all = lax.all_gather(grad_attn, "tp", axis=1, tiled=True)
    grad_wout = outer_sum(context_low, grad_attn_all)
    grad_context = project_back(grad_attn_all, back_out).astype(jnp.bfloat16).reshape(heads_shape)

    def delta_step(delta, block_index):
        key_part, value_part, scores, allowed = key_block(block_index)
        probs = jnp.exp(scores - log_total)
        grad_probs = jnp.einsum(
            "mqhd,mkhd->mhqk", grad_context, value_part, preferred_element_type=jnp.float32
        )
        return (delta + jnp.sum(probs * grad_probs, axis=-1), None)

    delta, unused = lax.scan(delta_step, jnp.zeros(stat_shape, jnp.float32), block_ids)

    def score_grads(block_index):
        key_part, value_part, scores, allowed = key_block(block_index)
        probs = jnp.exp(scores - log_total)
        grad_probs = jnp.einsum(
            "mqhd,mkhd->mhqk", grad_context, value_part, preferred_element_type=jnp.float32
        )
        grad_scores = (probs * (grad_probs - delta[..., None])).astype(jnp.bfloat16)
        return (key_part, probs, grad_scores)

    def grad_step(grad_queries, block_index):
        key_part, probs, grad_scores = score_grads(block_index)
        grad_queries = grad_queries + jnp.einsum(
            "mhqk,mkhd->mqhd", grad_scores, key_part, preferred_element_type=jnp.float32
        )
        grad_keys = (
            jnp.einsum("mhqk,mqhd->kmhd", grad_scores, queries, preferred_element_type=jnp.float32)
            * score_scale
        )
        grad_values = jnp.einsum(
            "mhqk,mqhd->kmhd",
            probs.astype(jnp.bfloat16),
            grad_context,
            preferred_element_type=jnp.float32,
        )
        both_terms = jnp.concatenate(
            [
                grad_keys.reshape(key_rows, seq_count, head_span),
                grad_values.reshape(key_rows, seq_count, head_span),
            ],
            axis=-1,
        )
        return (grad_queries, both_terms)

    grad_queries, key_terms = lax.scan(grad_step, jnp.zeros(heads_shape, jnp.float32), block_ids)
    key_value_grads = lax.psum_scatter(
        key_terms.reshape(length, seq_count, 2 * head_span).astype(jnp.bfloat16),
        "seq",
        scatter_dimension=0,
        tiled=True,
    ).astype(jnp.float32)
    key_value_grads = jnp.transpose(key_value_grads, (1, 0, 2))
    grad_keys_own = key_value_grads[..., :head_span].reshape(heads_shape)
    grad_values_own = key_value_grads[..., head_span:].astype(jnp.bfloat16)
    query_grad_unit = unrotate(grad_queries * score_scale, cosines, sines).reshape(
        seq_count, local_len, head_span
    )
    key_grad_unit = unrotate(grad_keys_own, cosines, sines).reshape(seq_count, local_len, head_span)
    grad_qgain = jnp.sum(query_grad_unit * query_unit, axis=(0, 1))
    grad_kgain = jnp.sum(key_grad_unit * key_unit, axis=(0, 1))
    query_scaled = query_grad_unit * query_gain
    key_scaled = key_grad_unit * key_gain
    query_dot, key_dot = lax.psum(
        (jnp.sum(query_scaled * query_unit, axis=-1), jnp.sum(key_scaled * key_unit, axis=-1)), "tp"
    )
    grad_qraw = norm_back(query_unit, query_scaled, query_inv, query_dot, d_model).astype(
        jnp.bfloat16
    )
    grad_kraw = norm_back(key_unit, key_scaled, key_inv, key_dot, d_model).astype(jnp.bfloat16)
    grad_wquery = outer_sum(tokens, grad_qraw)
    grad_wkey = outer_sum(tokens, grad_kraw)
    grad_wvalue = outer_sum(tokens, grad_values_own)
    token_part = (
        project_back(grad_qraw, back_query)
        + project_back(grad_kraw, back_key)
        + project_back(grad_values_own, back_value)
    )
    token_sum, grad_again_part = (
        lax.psum_scatter(
            token_part.astype(jnp.bfloat16), "tp", scatter_dimension=1, tiled=True
        ).astype(jnp.float32),
        lax.psum_scatter(
            grad_again.reshape(-1, head_dim).astype(jnp.bfloat16),
            "tp",
            scatter_dimension=0,
            tiled=True,
        ).astype(jnp.float32),
    )
    grad_tokens = grad_hidden + token_sum
    summed = (
        lax.psum_scatter(
            grad_wquery.astype(jnp.bfloat16), ("dp", "seq"), scatter_dimension=0, tiled=True
        ).astype(jnp.float32),
        lax.psum_scatter(
            grad_wkey.astype(jnp.bfloat16), ("dp", "seq"), scatter_dimension=0, tiled=True
        ).astype(jnp.float32),
        lax.psum_scatter(
            grad_wvalue.astype(jnp.bfloat16), ("dp", "seq"), scatter_dimension=0, tiled=True
        ).astype(jnp.float32),
        lax.psum_scatter(
            grad_wout.astype(jnp.bfloat16), ("dp", "seq"), scatter_dimension=1, tiled=True
        ).astype(jnp.float32),
        lax.psum_scatter(
            grad_wgate.astype(jnp.bfloat16), ("dp", "seq"), scatter_dimension=0, tiled=True
        ).astype(jnp.float32),
        lax.psum_scatter(
            grad_wup.astype(jnp.bfloat16), ("dp", "seq"), scatter_dimension=0, tiled=True
        ).astype(jnp.float32),
        lax.psum_scatter(
            grad_wdown.astype(jnp.bfloat16), ("dp", "seq"), scatter_dimension=1, tiled=True
        ).astype(jnp.float32),
        lax.psum_scatter(
            grad_qgain.reshape(local_heads, head_dim).astype(jnp.bfloat16),
            ("dp", "seq"),
            scatter_dimension=1,
            tiled=True,
        ).astype(jnp.float32),
        lax.psum_scatter(
            grad_kgain.reshape(local_heads, head_dim).astype(jnp.bfloat16),
            ("dp", "seq"),
            scatter_dimension=1,
            tiled=True,
        ).astype(jnp.float32),
        lax.psum_scatter(
            grad_again_part.astype(jnp.bfloat16), ("dp", "seq"), scatter_dimension=1, tiled=True
        ).astype(jnp.float32),
        lax.psum_scatter(
            grad_mgain_part.astype(jnp.bfloat16), ("dp", "seq"), scatter_dimension=1, tiled=True
        ).astype(jnp.float32),
    )
    (
        sum_query,
        sum_key,
        sum_value,
        sum_out,
        sum_gate,
        sum_up,
        sum_down,
        sum_qgain,
        sum_kgain,
        sum_again,
        sum_mgain,
    ) = summed
    return (
        outputs,
        grad_tokens,
        sum_query,
        sum_key,
        sum_value,
        sum_out,
        sum_gate,
        sum_up,
        sum_down,
        sum_qgain,
        sum_kgain,
        sum_again,
        sum_mgain,
    )


VMEM_LIMIT = 48 * 1024 * 1024


def to_neighbour(values, flip):
    return lax.ppermute(values, "seq", [(i, i ^ flip) for i in range(4)])


def to_core(values):
    return lax.ppermute(values, "dp", [(0, 1), (1, 0)])


def after(values, done):
    return lax.optimization_barrier((values, done))[0]


def gather_plane(shard, axis):
    half = shard.shape[0] // 2
    from_one = to_neighbour(shard, 1)
    from_two = to_neighbour(shard, 2)
    far_low = to_neighbour(from_two[:half], 1)
    far_high = to_neighbour(from_one[half:], 2)
    far = jnp.concatenate([far_low, far_high], axis=0)
    mine = jnp.concatenate([shard, from_one, from_two, far], axis=axis)
    return jnp.concatenate([mine, to_core(mine)], axis=axis)


def scatter_plane(kept, sent, axis):
    def blocks(values):
        return jnp.split(values.astype(jnp.float32), 4, axis=axis)

    low = jnp.bfloat16
    mine = [a + b for a, b in zip(blocks(kept), blocks(to_core(sent)))]
    half = mine[3].shape[0] // 2
    far_low = to_neighbour(mine[3][:half].astype(low), 1).astype(jnp.float32)
    far_high = to_neighbour(mine[3][half:].astype(low), 2).astype(jnp.float32)
    by_one = jnp.concatenate([mine[1][:half], mine[1][half:] + far_high], axis=0)
    by_two = jnp.concatenate([mine[2][:half] + far_low, mine[2][half:]], axis=0)
    from_one = to_neighbour(by_one.astype(low), 1).astype(jnp.float32)
    from_two = to_neighbour(by_two.astype(low), 2).astype(jnp.float32)
    return mine[0] + from_one + from_two


def reorder(values, order):
    rows, width = values.shape
    block = width // 8

    def body(order_ref, in_ref, out_ref):
        out_ref[...] = in_ref[...]

    return pl.pallas_call(
        body,
        grid_spec=pltpu.PrefetchScalarGridSpec(
            num_scalar_prefetch=1,
            grid=(8,),
            in_specs=[pl.BlockSpec((rows, block), lambda j, order_ref: (0, order_ref[j]))],
            out_specs=pl.BlockSpec((rows, block), lambda j, order_ref: (0, j)),
        ),
        out_shape=jax.ShapeDtypeStruct(values.shape, values.dtype),
        name="reorder",
    )(order, values)


def turned(values, cosines, sines):
    return values * cosines + pltpu.roll(values, values.shape[-1] // 2, axis=1) * sines


def prepare(raw, inv, gains, cosines, sines, heads, head_dim, seqs):
    rows = raw.shape[0]
    length = rows // seqs

    def body(raw_ref, inv_ref, gain_ref, cos_ref, sin_ref, out_ref):
        kind = pl.program_id(0)

        @pl.when(kind < 2)
        def _():
            normed = raw_ref[...] * inv_ref[0] * gain_ref[...]
            out_ref[0, 0] = (
                turned(normed, cos_ref[...], sin_ref[...])
                .astype(jnp.bfloat16)
                .reshape(seqs, length, head_dim)
            )

        @pl.when(kind == 2)
        def _():
            out_ref[0, 0] = raw_ref[...].astype(jnp.bfloat16).reshape(seqs, length, head_dim)

    return pl.pallas_call(
        body,
        grid=(3, heads),
        in_specs=[
            pl.BlockSpec((rows, head_dim), lambda t, h: (0, t * heads + h)),
            pl.BlockSpec((1, rows, 1), lambda t, h: (jnp.minimum(t, 1), 0, 0)),
            pl.BlockSpec((1, head_dim), lambda t, h: (0, jnp.minimum(t * heads + h, 2 * heads - 1))),
            pl.BlockSpec((rows, head_dim), lambda t, h: (0, 0)),
            pl.BlockSpec((rows, head_dim), lambda t, h: (0, 0)),
        ],
        out_specs=pl.BlockSpec((1, 1, seqs, length, head_dim), lambda t, h: (h, t, 0, 0, 0)),
        out_shape=jax.ShapeDtypeStruct((heads, 3, seqs, length, head_dim), jnp.bfloat16),
        name="prepare",
    )(raw, inv, gains, cosines, sines)


def scores_of(left, right):
    return lax.dot_general(
        left, right, (((1,), (1,)), ((), ())), preferred_element_type=jnp.float32
    )


def causal(scores, first):
    rows = lax.broadcasted_iota(jnp.int32, scores.shape, 0) + first
    columns = lax.broadcasted_iota(jnp.int32, scores.shape, 1)
    return columns <= rows


def attend(parts):
    blocks, _, seqs, length, head_dim = parts.shape
    score_scale = head_dim ** (-0.5)

    def body(parts_ref, out_ref, log_ref):
        for i in range(blocks):
            span = (i + 1) * length
            keys = parts_ref[: i + 1, 1, 0].reshape(span, head_dim)
            values = parts_ref[: i + 1, 2, 0].reshape(span, head_dim)
            scores = scores_of(parts_ref[i, 0, 0], keys) * score_scale
            scores = jnp.where(causal(scores, i * length), scores, MASKED)
            top = jnp.max(scores, axis=-1, keepdims=True)
            weights = jnp.exp(scores - top)
            total = jnp.sum(weights, axis=-1, keepdims=True)
            probs = (weights * (1.0 / total)).astype(jnp.bfloat16)
            out_ref[i, 0] = jnp.dot(probs, values, preferred_element_type=jnp.float32).astype(
                jnp.bfloat16
            )
            log_ref[i, 0] = top + jnp.log(total)

    return pl.pallas_call(
        body,
        grid=(seqs,),
        in_specs=[pl.BlockSpec((blocks, 3, 1, length, head_dim), lambda m: (0, 0, m, 0, 0))],
        out_specs=[
            pl.BlockSpec((blocks, 1, length, head_dim), lambda m: (0, m, 0, 0)),
            pl.BlockSpec((blocks, 1, length, 1), lambda m: (0, m, 0, 0)),
        ],
        out_shape=[
            jax.ShapeDtypeStruct((blocks, seqs, length, head_dim), jnp.bfloat16),
            jax.ShapeDtypeStruct((blocks, seqs, length, 1), jnp.float32),
        ],
        compiler_params=pltpu.CompilerParams(vmem_limit_bytes=VMEM_LIMIT),
        name="attend",
    )(parts)


def attend_back(parts, grad_context, log_total):
    blocks, _, seqs, length, head_dim = parts.shape
    score_scale = head_dim ** (-0.5)

    def body(parts_ref, grad_ref, log_ref, out_ref, keys_sum, values_sum):
        keys_sum[...] = jnp.zeros_like(keys_sum)
        values_sum[...] = jnp.zeros_like(values_sum)
        for i in range(blocks):
            span = (i + 1) * length
            queries = parts_ref[i, 0, 0]
            keys = parts_ref[: i + 1, 1, 0].reshape(span, head_dim)
            values = parts_ref[: i + 1, 2, 0].reshape(span, head_dim)
            grads = grad_ref[i, 0]
            scores = scores_of(queries, keys) * score_scale
            probs = jnp.where(
                causal(scores, i * length), jnp.exp(scores - log_ref[i, 0]), 0.0
            )
            grad_probs = scores_of(grads, values)
            delta = jnp.sum(probs * grad_probs, axis=-1, keepdims=True)
            grad_scores = (probs * (grad_probs - delta)).astype(jnp.bfloat16)
            out_ref[i, 0, 0] = (
                jnp.dot(grad_scores, keys, preferred_element_type=jnp.float32) * score_scale
            ).astype(jnp.bfloat16)
            over_rows = (((0,), (0,)), ((), ()))
            keys_sum[:span] += lax.dot_general(
                grad_scores, queries, over_rows, preferred_element_type=jnp.float32
            )
            values_sum[:span] += lax.dot_general(
                probs.astype(jnp.bfloat16), grads, over_rows, preferred_element_type=jnp.float32
            )
        out_ref[:, 1, 0] = (
            (keys_sum[...] * score_scale).astype(jnp.bfloat16).reshape(blocks, length, head_dim)
        )
        out_ref[:, 2, 0] = values_sum[...].astype(jnp.bfloat16).reshape(blocks, length, head_dim)

    whole = pl.BlockSpec((blocks, 3, 1, length, head_dim), lambda m: (0, 0, m, 0, 0))
    return pl.pallas_call(
        body,
        grid=(seqs,),
        in_specs=[
            whole,
            pl.BlockSpec((blocks, 1, length, head_dim), lambda m: (0, m, 0, 0)),
            pl.BlockSpec((blocks, 1, length, 1), lambda m: (0, m, 0, 0)),
        ],
        out_specs=whole,
        out_shape=jax.ShapeDtypeStruct(parts.shape, jnp.bfloat16),
        scratch_shapes=[
            pltpu.VMEM((blocks * length, head_dim), jnp.float32),
            pltpu.VMEM((blocks * length, head_dim), jnp.float32),
        ],
        compiler_params=pltpu.CompilerParams(vmem_limit_bytes=VMEM_LIMIT),
        name="attend_back",
    )(parts, grad_context, log_total)


def unprepare(grads, raw, inv, gains, cosines, sines, heads, head_dim):
    rows = raw.shape[0]

    def body(grad_ref, raw_ref, inv_ref, gain_ref, cos_ref, sin_ref, scaled_ref, dot_ref, sum_ref):
        turned_back = turned(
            grad_ref[0, 0].reshape(rows, head_dim).astype(jnp.float32), cos_ref[...], -sin_ref[...]
        )
        unit = raw_ref[...] * inv_ref[0]
        along = turned_back * unit
        sum_ref[...] = jnp.sum(along, axis=0, keepdims=True)
        scaled_ref[...] = turned_back * gain_ref[...]
        part = jnp.sum(along * gain_ref[...], axis=-1, keepdims=True)

        @pl.when(pl.program_id(1) == 0)
        def _():
            dot_ref[0] = part

        @pl.when(pl.program_id(1) > 0)
        def _():
            dot_ref[0] += part

    return pl.pallas_call(
        body,
        grid=(2, heads),
        in_specs=[
            pl.BlockSpec((1, 1) + grads.shape[2:], lambda t, h: (h, t, 0, 0, 0)),
            pl.BlockSpec((rows, head_dim), lambda t, h: (0, t * heads + h)),
            pl.BlockSpec((1, rows, 1), lambda t, h: (t, 0, 0)),
            pl.BlockSpec((1, head_dim), lambda t, h: (0, t * heads + h)),
            pl.BlockSpec((rows, head_dim), lambda t, h: (0, 0)),
            pl.BlockSpec((rows, head_dim), lambda t, h: (0, 0)),
        ],
        out_specs=[
            pl.BlockSpec((rows, head_dim), lambda t, h: (0, t * heads + h)),
            pl.BlockSpec((1, rows, 1), lambda t, h: (t, 0, 0)),
            pl.BlockSpec((1, head_dim), lambda t, h: (0, t * heads + h)),
        ],
        out_shape=[
            jax.ShapeDtypeStruct((rows, 2 * heads * head_dim), jnp.float32),
            jax.ShapeDtypeStruct((2, rows, 1), jnp.float32),
            jax.ShapeDtypeStruct((1, 2 * heads * head_dim), jnp.float32),
        ],
        name="unprepare",
    )(grads, raw, inv, gains, cosines, sines)


def raw_grads(grads, scaled, raw, inv, dots, heads, head_dim, d_model):
    rows = raw.shape[0]

    def body(grad_ref, scaled_ref, raw_ref, inv_ref, dot_ref, out_ref):
        @pl.when(pl.program_id(0) < 2)
        def _():
            unit = raw_ref[...] * inv_ref[0]
            out_ref[...] = (
                inv_ref[0] * (scaled_ref[...] - unit * (dot_ref[0] * (1.0 / d_model)))
            ).astype(jnp.bfloat16)

        @pl.when(pl.program_id(0) == 2)
        def _():
            out_ref[...] = grad_ref[0, 0].reshape(rows, head_dim)

    last = 2 * heads - 1
    return pl.pallas_call(
        body,
        grid=(3, heads),
        in_specs=[
            pl.BlockSpec(
                (1, 1) + grads.shape[2:], lambda t, h: (jnp.where(t == 2, h, 0), 2, 0, 0, 0)
            ),
            pl.BlockSpec((rows, head_dim), lambda t, h: (0, jnp.minimum(t * heads + h, last))),
            pl.BlockSpec((rows, head_dim), lambda t, h: (0, jnp.minimum(t * heads + h, last))),
            pl.BlockSpec((1, rows, 1), lambda t, h: (jnp.minimum(t, 1), 0, 0)),
            pl.BlockSpec((1, rows, 1), lambda t, h: (jnp.minimum(t, 1), 0, 0)),
        ],
        out_specs=pl.BlockSpec((rows, head_dim), lambda t, h: (0, t * heads + h)),
        out_shape=jax.ShapeDtypeStruct((rows, 3 * heads * head_dim), jnp.bfloat16),
        name="raw_grads",
    )(grads, scaled, raw, inv, dots)


def contract(left, right, left_dim, right_dim):
    return lax.dot_general(
        left, right, (((left_dim,), (right_dim,)), ((), ())), preferred_element_type=jnp.float32
    )


def on_plane(
    tokens,
    w_query,
    w_key,
    w_value,
    w_out,
    w_gate,
    w_up,
    w_down,
    q_gain,
    k_gain,
    attn_gain,
    mlp_gain,
    cotangent,
):
    low = jnp.bfloat16
    seqs, length, d_model = tokens.shape
    rows = seqs * length
    tp = lax.axis_size("tp")
    tp_rank = lax.axis_index("tp")
    seq_rank = lax.axis_index("seq")
    heads = q_gain.shape[0]
    head_dim = q_gain.shape[1] * 8
    head_span = heads * head_dim
    own_length = length // tp
    half = d_model // 2
    order = (lax.axis_index("dp") * 4 + seq_rank) ^ jnp.arange(8, dtype=jnp.int32)

    in_weights = gather_plane(jnp.concatenate([w_query, w_key, w_value], axis=1), 0)
    gain_rows = jnp.concatenate([q_gain, k_gain, attn_gain, mlp_gain], axis=0)
    all_gains = lax.all_gather(gain_rows.reshape(-1), ("dp", "seq"))
    all_gains = (
        jnp.transpose(all_gains.reshape((8,) + gain_rows.shape), (1, 0, 2))
        .reshape(gain_rows.shape[0], head_dim)
        .astype(jnp.float32)
    )
    qk_gain = all_gains[: 2 * heads].reshape(1, 2 * head_span)
    feature_rows = d_model // head_dim

    def features(first):
        return jnp.take(
            all_gains[first : first + feature_rows].reshape(8, d_model // 8), order, axis=0
        ).reshape(d_model)

    attn_gains = features(2 * heads)
    mlp_gains = features(2 * heads + feature_rows)
    rows_low = reorder(tokens.reshape(rows, d_model), order)
    grad_out = (
        reorder(cotangent.reshape(-1, d_model), order)
        .astype(jnp.float32)
        .reshape(seqs, own_length, d_model)
    )
    own_tokens = lax.dynamic_slice_in_dim(
        rows_low.reshape(seqs, length, d_model), tp_rank * own_length, own_length, 1
    ).astype(jnp.float32)

    raw = contract(rows_low, in_weights, 1, 0)
    squares = jnp.stack(
        [
            jnp.sum(jnp.square(raw[:, :head_span]), axis=-1),
            jnp.sum(jnp.square(raw[:, head_span : 2 * head_span]), axis=-1),
        ]
    )
    inv = lax.rsqrt(lax.psum(squares, "tp") / d_model + NORM_EPS)[..., None]
    positions = seq_rank * length + jnp.arange(length, dtype=jnp.int32)
    cosines, sines = rope_tables(positions, head_dim)
    cosines = jnp.tile(jnp.concatenate([cosines[:, 0], cosines[:, 0]], axis=-1), (seqs, 1))
    sines = jnp.tile(jnp.concatenate([-sines[:, 0], sines[:, 0]], axis=-1), (seqs, 1))
    parts = prepare(raw, inv, qk_gain, cosines, sines, heads, head_dim, seqs)
    parts = lax.all_to_all(parts, "seq", 0, 0, tiled=True)
    context, log_total = attend(parts)
    context = lax.all_to_all(context, "seq", 0, 0, tiled=True)
    context_low = jnp.transpose(context, (1, 2, 0, 3)).reshape(rows, head_span)

    out_weights = gather_plane(after(w_out, in_weights), 1)
    gate_weights = gather_plane(after(w_gate, in_weights), 0)
    up_weights = gather_plane(after(w_up, context), 0)
    down_weights = gather_plane(after(w_down, context), 1)

    def sum_rows(values):
        return lax.psum_scatter(
            values.astype(low).reshape(seqs, length, d_model),
            "tp",
            scatter_dimension=1,
            tiled=True,
        ).astype(jnp.float32)

    def all_rows(values):
        return lax.all_gather(values.astype(low), "tp", axis=1, tiled=True).reshape(rows, d_model)

    attn_out = sum_rows(contract(context_low, out_weights, 1, 0))
    attn_inv = lax.rsqrt(jnp.mean(attn_out * attn_out, axis=-1, keepdims=True) + NORM_EPS)
    attn_unit = attn_out * attn_inv
    hidden = own_tokens + attn_unit * attn_gains
    hidden_all = all_rows(hidden)
    gate = contract(hidden_all, gate_weights, 1, 0)
    up = contract(hidden_all, up_weights, 1, 0)
    gate_sig = jax.nn.sigmoid(gate)
    mixed = (gate * gate_sig * up).astype(low)
    mlp_out = sum_rows(contract(mixed, down_weights, 1, 0))
    mlp_inv = lax.rsqrt(jnp.mean(mlp_out * mlp_out, axis=-1, keepdims=True) + NORM_EPS)
    mlp_unit = mlp_out * mlp_inv
    outputs = (hidden + mlp_unit * mlp_gains).astype(low)

    grad_mgain = jnp.sum(grad_out * mlp_unit, axis=(0, 1))
    mlp_scaled = grad_out * mlp_gains
    grad_mlp = norm_back(
        mlp_unit, mlp_scaled, mlp_inv, jnp.sum(mlp_scaled * mlp_unit, axis=-1), d_model
    )
    grad_mlp_all = all_rows(grad_mlp)
    grad_mixed = contract(grad_mlp_all, down_weights, 1, 1)
    grad_gate = (grad_mixed * up * gate_sig * (1.0 + gate * (1.0 - gate_sig))).astype(low)
    grad_up = (grad_mixed * gate * gate_sig).astype(low)
    hidden_part = contract(grad_gate, gate_weights, 1, 1) + contract(grad_up, up_weights, 1, 1)
    hidden_sum = sum_rows(hidden_part)

    def weight_grad(left, right, axis):
        if axis == 0:
            sent = contract(left[:, half:], right, 0, 0)
            kept = contract(left[:, :half], right, 0, 0)
        else:
            sent = contract(left, right[:, half:], 0, 0)
            kept = contract(left, right[:, :half], 0, 0)
        return scatter_plane(kept.astype(low), sent.astype(low), axis)

    sum_down = weight_grad(mixed, grad_mlp_all, 1)
    sum_gate = weight_grad(hidden_all, grad_gate, 0)
    sum_up = weight_grad(hidden_all, grad_up, 0)

    grad_hidden = grad_out + hidden_sum
    grad_again = jnp.sum(grad_hidden * attn_unit, axis=(0, 1))
    attn_scaled = grad_hidden * attn_gains
    grad_attn = norm_back(
        attn_unit, attn_scaled, attn_inv, jnp.sum(attn_scaled * attn_unit, axis=-1), d_model
    )
    grad_attn_all = all_rows(grad_attn)
    grad_context = contract(grad_attn_all, out_weights, 1, 1).astype(low)
    grad_context = jnp.transpose(
        grad_context.reshape(seqs, length, heads, head_dim), (2, 0, 1, 3)
    )
    grad_context = lax.all_to_all(grad_context, "seq", 0, 0, tiled=True)
    sum_out = weight_grad(context_low, grad_attn_all, 1)
    part_grads = attend_back(parts, grad_context, log_total)
    part_grads = lax.all_to_all(part_grads, "seq", 0, 0, tiled=True)
    scaled, dots, qk_sums = unprepare(
        part_grads, raw, inv, qk_gain, cosines, sines, heads, head_dim
    )
    dots = lax.psum(dots.reshape(2, rows), "tp")[..., None]
    grad_raw = raw_grads(part_grads, scaled, raw, inv, dots, heads, head_dim, d_model)
    token_sum = sum_rows(contract(grad_raw, in_weights, 1, 1))
    sum_in = weight_grad(rows_low, grad_raw, 0)
    grad_tokens = grad_hidden + token_sum

    def by_owner(values):
        values = jnp.take(values.reshape(8, d_model // 8), order, axis=0)
        return jnp.transpose(values.reshape(tp, heads, 8, -1), (2, 0, 1, 3))

    head_sums = jnp.transpose(qk_sums.reshape(2, heads, 8, -1), (2, 0, 1, 3))[:, None]
    is_own = (jnp.arange(tp) == tp_rank)[None, :, None, None, None]
    payload = jnp.concatenate(
        [
            jnp.where(is_own, head_sums, 0.0),
            by_owner(grad_again)[:, :, None],
            by_owner(grad_mgain)[:, :, None],
        ],
        axis=2,
    ).reshape(8 * tp, -1)
    gain_sums = jnp.sum(
        lax.all_to_all(payload, ("dp", "seq", "tp"), 0, 0, tiled=True), axis=0
    ).reshape(4, heads, -1)

    def in_place(values):
        return reorder(values.reshape(-1, d_model), order).reshape(seqs, own_length, d_model)

    return (
        in_place(outputs),
        in_place(grad_tokens),
        sum_in[:, :head_span],
        sum_in[:, head_span : 2 * head_span],
        sum_in[:, 2 * head_span :],
        sum_out,
        sum_gate,
        sum_up,
        sum_down,
        gain_sums[0],
        gain_sums[1],
        gain_sums[2],
        gain_sums[3],
    )


def solution(mesh):
    by_plane = mesh.shape["dp"] == 2 and mesh.shape["seq"] == 4
    return jax.shard_map(
        on_plane if by_plane else on_any_mesh,
        mesh=mesh,
        in_specs=(
            P("dp", "seq", None),
            P(("dp", "seq"), "tp"),
            P(("dp", "seq"), "tp"),
            P(("dp", "seq"), "tp"),
            P("tp", ("dp", "seq")),
            P(("dp", "seq"), "tp"),
            P(("dp", "seq"), "tp"),
            P("tp", ("dp", "seq")),
            P("tp", ("dp", "seq")),
            P("tp", ("dp", "seq")),
            P(None, ("dp", "seq")),
            P(None, ("dp", "seq")),
            P("dp", ("seq", "tp"), None),
        ),
        out_specs=(
            P("dp", ("seq", "tp"), None),
            P("dp", ("seq", "tp"), None),
            P(("dp", "seq"), "tp"),
            P(("dp", "seq"), "tp"),
            P(("dp", "seq"), "tp"),
            P("tp", ("dp", "seq")),
            P(("dp", "seq"), "tp"),
            P(("dp", "seq"), "tp"),
            P("tp", ("dp", "seq")),
            P("tp", ("dp", "seq")),
            P("tp", ("dp", "seq")),
            P("tp", ("dp", "seq")),
            P("tp", ("dp", "seq")),
        ),
        check_vma=False,
    )
```

```python
import math

import jax
import jax.numpy as jnp
from jax import lax
from jax.experimental import pallas as pl
from jax.experimental.pallas import tpu as pltpu
from jax.sharding import PartitionSpec as P

NORM_EPS = 1e-06
ROPE_BASE = 500000.0
MASKED = -1e30


def project(left, right):
    return jnp.dot(left, right, preferred_element_type=jnp.float32)


def project_back(left, right):
    return lax.dot_general(
        left, right, (((left.ndim - 1,), (1,)), ((), ())), preferred_element_type=jnp.float32
    )


def outer_sum(left, right):
    return lax.dot_general(
        left, right, (((0, 1), (0, 1)), ((), ())), preferred_element_type=jnp.float32
    )


def rope_tables(positions, head_dim):
    steps = jnp.arange(head_dim // 2, dtype=jnp.float32)
    freqs = jnp.exp(steps * (-2.0 * math.log(ROPE_BASE) / head_dim))
    angles = positions.astype(jnp.float32)[:, None] * freqs[None, :]
    return (jnp.cos(angles)[:, None, :], jnp.sin(angles)[:, None, :])


def rotate(values, cosines, sines):
    half = values.shape[-1] // 2
    first = values[..., :half]
    second = values[..., half:]
    return jnp.concatenate(
        [first * cosines - second * sines, second * cosines + first * sines], axis=-1
    )


def unrotate(grads, cosines, sines):
    half = grads.shape[-1] // 2
    first = grads[..., :half]
    second = grads[..., half:]
    return jnp.concatenate(
        [first * cosines + second * sines, second * cosines - first * sines], axis=-1
    )


def norm_back(normed, grad_normed, inv_scale, total_dot, d_model):
    return inv_scale * (grad_normed - normed * (total_dot / d_model)[..., None])


def on_any_mesh(
    tokens,
    w_query,
    w_key,
    w_value,
    w_out,
    w_gate,
    w_up,
    w_down,
    q_gain,
    k_gain,
    attn_gain,
    mlp_gain,
    cotangent,
):
    seq_count, local_len, d_model = tokens.shape
    seq_rank = lax.axis_index("seq")
    tp_rank = lax.axis_index("tp")
    own_rows = local_len // lax.axis_size("tp")
    weights_in = (
        lax.all_gather(w_query, ("dp", "seq"), axis=0, tiled=True),
        lax.all_gather(w_key, ("dp", "seq"), axis=0, tiled=True),
        lax.all_gather(w_value, ("dp", "seq"), axis=0, tiled=True),
        lax.all_gather(w_out, ("dp", "seq"), axis=1, tiled=True),
        lax.all_gather(w_gate, ("dp", "seq"), axis=0, tiled=True),
        lax.all_gather(w_up, ("dp", "seq"), axis=0, tiled=True),
        lax.all_gather(w_down, ("dp", "seq"), axis=1, tiled=True),
        lax.all_gather(q_gain, ("dp", "seq"), axis=1, tiled=True),
        lax.all_gather(k_gain, ("dp", "seq"), axis=1, tiled=True),
        lax.all_gather(attn_gain, ("dp", "seq"), axis=1, tiled=True),
        lax.all_gather(mlp_gain, ("dp", "seq"), axis=1, tiled=True),
    )
    (
        full_query,
        full_key,
        full_value,
        full_out,
        full_gate,
        full_up,
        full_down,
        full_qgain,
        full_kgain,
        full_again,
        full_mgain,
    ) = weights_in
    local_heads = full_qgain.shape[0]
    head_dim = full_qgain.shape[1]
    head_span = local_heads * head_dim
    score_scale = head_dim ** (-0.5)
    query_gain = full_qgain.astype(jnp.float32).reshape(head_span)
    key_gain = full_kgain.astype(jnp.float32).reshape(head_span)
    attn_scale_gain = full_again.astype(jnp.float32).reshape(d_model)
    mlp_scale_gain = full_mgain.astype(jnp.float32).reshape(d_model)
    query_raw = project(tokens, full_query)
    key_raw = project(tokens, full_key)
    value_raw = project(tokens, full_value)
    query_sq, key_sq = lax.psum(
        (jnp.sum(query_raw * query_raw, axis=-1), jnp.sum(key_raw * key_raw, axis=-1)), "tp"
    )
    query_inv = lax.rsqrt(query_sq / d_model + NORM_EPS)[..., None]
    key_inv = lax.rsqrt(key_sq / d_model + NORM_EPS)[..., None]
    query_unit = query_raw * query_inv
    key_unit = key_raw * key_inv
    positions = seq_rank * local_len + jnp.arange(local_len, dtype=jnp.int32)
    cosines, sines = rope_tables(positions, head_dim)
    heads_shape = (seq_count, local_len, local_heads, head_dim)
    queries = rotate((query_unit * query_gain).reshape(heads_shape), cosines, sines).astype(
        jnp.bfloat16
    )
    keys_local = (
        rotate((key_unit * key_gain).reshape(heads_shape), cosines, sines)
        .astype(jnp.bfloat16)
        .reshape(seq_count, local_len, head_span)
    )
    values_local = value_raw.astype(jnp.bfloat16)
    all_keys, all_values = (
        lax.all_gather(keys_local, "seq", axis=1, tiled=True),
        lax.all_gather(values_local, "seq", axis=1, tiled=True),
    )
    length = all_keys.shape[1]
    keys_full = all_keys.reshape(seq_count, length, local_heads, head_dim)
    values_full = all_values.reshape(seq_count, length, local_heads, head_dim)
    key_rows = min(512, length)
    block_ids = jnp.arange(length // key_rows, dtype=jnp.int32)

    def key_block(block_index):
        first_key = block_index * key_rows
        key_part = lax.dynamic_slice_in_dim(keys_full, first_key, key_rows, 1)
        value_part = lax.dynamic_slice_in_dim(values_full, first_key, key_rows, 1)
        scores = (
            jnp.einsum("mqhd,mkhd->mhqk", queries, key_part, preferred_element_type=jnp.float32)
            * score_scale
        )
        allowed = (first_key + jnp.arange(key_rows, dtype=jnp.int32))[None, :] <= positions[:, None]
        return (key_part, value_part, jnp.where(allowed, scores, MASKED), allowed)

    def max_step(state, block_index):
        running_max, running_sum = state
        key_part, value_part, scores, allowed = key_block(block_index)
        new_max = jnp.maximum(running_max, jnp.max(scores, axis=-1))
        weights_now = jnp.where(allowed, jnp.exp(scores - new_max[..., None]), 0.0)
        return (
            (new_max, running_sum * jnp.exp(running_max - new_max) + jnp.sum(weights_now, axis=-1)),
            None,
        )

    stat_shape = (seq_count, local_heads, local_len)
    final_state, unused = lax.scan(
        max_step,
        (jnp.full(stat_shape, MASKED, jnp.float32), jnp.zeros(stat_shape, jnp.float32)),
        block_ids,
    )
    log_total = (final_state[0] + jnp.log(final_state[1]))[..., None]

    def context_step(context, block_index):
        key_part, value_part, scores, allowed = key_block(block_index)
        probs = jnp.where(allowed, jnp.exp(scores - log_total), 0.0).astype(jnp.bfloat16)
        return (
            context
            + jnp.einsum("mhqk,mkhd->mqhd", probs, value_part, preferred_element_type=jnp.float32),
            None,
        )

    context, unused = lax.scan(context_step, jnp.zeros(heads_shape, jnp.float32), block_ids)
    context_low = context.astype(jnp.bfloat16).reshape(seq_count, local_len, head_span)
    attn_out = lax.psum_scatter(
        project(context_low, full_out), "tp", scatter_dimension=1, tiled=True
    )
    attn_inv = lax.rsqrt(jnp.mean(attn_out * attn_out, axis=-1, keepdims=True) + NORM_EPS)
    attn_unit = attn_out * attn_inv
    own_tokens = lax.dynamic_slice_in_dim(tokens, tp_rank * own_rows, own_rows, 1).astype(
        jnp.float32
    )
    hidden = own_tokens + attn_unit * attn_scale_gain
    hidden_all = lax.all_gather(hidden.astype(jnp.bfloat16), "tp", axis=1, tiled=True)
    gate_act = project(hidden_all, full_gate)
    up_act = project(hidden_all, full_up)
    gate_sig = jax.nn.sigmoid(gate_act)
    mixed = (gate_act * gate_sig * up_act).astype(jnp.bfloat16)
    mlp_out = lax.psum_scatter(project(mixed, full_down), "tp", scatter_dimension=1, tiled=True)
    mlp_inv = lax.rsqrt(jnp.mean(mlp_out * mlp_out, axis=-1, keepdims=True) + NORM_EPS)
    mlp_unit = mlp_out * mlp_inv
    outputs = (hidden + mlp_unit * mlp_scale_gain).astype(jnp.bfloat16)
    weights_back = (
        lax.all_gather(w_query, ("dp", "seq"), axis=0, tiled=True),
        lax.all_gather(w_key, ("dp", "seq"), axis=0, tiled=True),
        lax.all_gather(w_value, ("dp", "seq"), axis=0, tiled=True),
        lax.all_gather(w_out, ("dp", "seq"), axis=1, tiled=True),
        lax.all_gather(w_gate, ("dp", "seq"), axis=0, tiled=True),
        lax.all_gather(w_up, ("dp", "seq"), axis=0, tiled=True),
        lax.all_gather(w_down, ("dp", "seq"), axis=1, tiled=True),
    )
    back_query, back_key, back_value, back_out, back_gate, back_up, back_down = weights_back
    grad_out = cotangent.astype(jnp.float32)
    grad_mgain = jnp.sum(grad_out * mlp_unit, axis=(0, 1))
    mlp_scaled = grad_out * mlp_scale_gain
    grad_mlp = norm_back(
        mlp_unit, mlp_scaled, mlp_inv, jnp.sum(mlp_scaled * mlp_unit, axis=-1), d_model
    ).astype(jnp.bfloat16)
    grad_mlp_all = lax.all_gather(grad_mlp, "tp", axis=1, tiled=True)
    grad_wdown = outer_sum(mixed, grad_mlp_all)
    grad_mixed = project_back(grad_mlp_all, back_down)
    grad_gate = (grad_mixed * up_act * gate_sig * (1.0 + gate_act * (1.0 - gate_sig))).astype(
        jnp.bfloat16
    )
    grad_up = (grad_mixed * gate_act * gate_sig).astype(jnp.bfloat16)
    grad_wgate = outer_sum(hidden_all, grad_gate)
    grad_wup = outer_sum(hidden_all, grad_up)
    hidden_part = project_back(grad_gate, back_gate) + project_back(grad_up, back_up)
    hidden_sum, grad_mgain_part = (
        lax.psum_scatter(hidden_part, "tp", scatter_dimension=1, tiled=True),
        lax.psum_scatter(grad_mgain.reshape(-1, head_dim), "tp", scatter_dimension=0, tiled=True),
    )
    grad_hidden = grad_out + hidden_sum
    grad_again = jnp.sum(grad_hidden * attn_unit, axis=(0, 1))
    attn_scaled = grad_hidden * attn_scale_gain
    grad_attn = norm_back(
        attn_unit, attn_scaled, attn_inv, jnp.sum(attn_scaled * attn_unit, axis=-1), d_model
    ).astype(jnp.bfloat16)
    grad_attn_all = lax.all_gather(grad_attn, "tp", axis=1, tiled=True)
    grad_wout = outer_sum(context_low, grad_attn_all)
    grad_context = project_back(grad_attn_all, back_out).astype(jnp.bfloat16).reshape(heads_shape)

    def delta_step(delta, block_index):
        key_part, value_part, scores, allowed = key_block(block_index)
        probs = jnp.exp(scores - log_total)
        grad_probs = jnp.einsum(
            "mqhd,mkhd->mhqk", grad_context, value_part, preferred_element_type=jnp.float32
        )
        return (delta + jnp.sum(probs * grad_probs, axis=-1), None)

    delta, unused = lax.scan(delta_step, jnp.zeros(stat_shape, jnp.float32), block_ids)

    def score_grads(block_index):
        key_part, value_part, scores, allowed = key_block(block_index)
        probs = jnp.exp(scores - log_total)
        grad_probs = jnp.einsum(
            "mqhd,mkhd->mhqk", grad_context, value_part, preferred_element_type=jnp.float32
        )
        grad_scores = (probs * (grad_probs - delta[..., None])).astype(jnp.bfloat16)
        return (key_part, probs, grad_scores)

    def grad_step(grad_queries, block_index):
        key_part, probs, grad_scores = score_grads(block_index)
        grad_queries = grad_queries + jnp.einsum(
            "mhqk,mkhd->mqhd", grad_scores, key_part, preferred_element_type=jnp.float32
        )
        grad_keys = (
            jnp.einsum("mhqk,mqhd->kmhd", grad_scores, queries, preferred_element_type=jnp.float32)
            * score_scale
        )
        grad_values = jnp.einsum(
            "mhqk,mqhd->kmhd",
            probs.astype(jnp.bfloat16),
            grad_context,
            preferred_element_type=jnp.float32,
        )
        both_terms = jnp.concatenate(
            [
                grad_keys.reshape(key_rows, seq_count, head_span),
                grad_values.reshape(key_rows, seq_count, head_span),
            ],
            axis=-1,
        )
        return (grad_queries, both_terms)

    grad_queries, key_terms = lax.scan(grad_step, jnp.zeros(heads_shape, jnp.float32), block_ids)
    key_value_grads = lax.psum_scatter(
        key_terms.reshape(length, seq_count, 2 * head_span).astype(jnp.bfloat16),
        "seq",
        scatter_dimension=0,
        tiled=True,
    ).astype(jnp.float32)
    key_value_grads = jnp.transpose(key_value_grads, (1, 0, 2))
    grad_keys_own = key_value_grads[..., :head_span].reshape(heads_shape)
    grad_values_own = key_value_grads[..., head_span:].astype(jnp.bfloat16)
    query_grad_unit = unrotate(grad_queries * score_scale, cosines, sines).reshape(
        seq_count, local_len, head_span
    )
    key_grad_unit = unrotate(grad_keys_own, cosines, sines).reshape(seq_count, local_len, head_span)
    grad_qgain = jnp.sum(query_grad_unit * query_unit, axis=(0, 1))
    grad_kgain = jnp.sum(key_grad_unit * key_unit, axis=(0, 1))
    query_scaled = query_grad_unit * query_gain
    key_scaled = key_grad_unit * key_gain
    query_dot, key_dot = lax.psum(
        (jnp.sum(query_scaled * query_unit, axis=-1), jnp.sum(key_scaled * key_unit, axis=-1)), "tp"
    )
    grad_qraw = norm_back(query_unit, query_scaled, query_inv, query_dot, d_model).astype(
        jnp.bfloat16
    )
    grad_kraw = norm_back(key_unit, key_scaled, key_inv, key_dot, d_model).astype(jnp.bfloat16)
    grad_wquery = outer_sum(tokens, grad_qraw)
    grad_wkey = outer_sum(tokens, grad_kraw)
    grad_wvalue = outer_sum(tokens, grad_values_own)
    token_part = (
        project_back(grad_qraw, back_query)
        + project_back(grad_kraw, back_key)
        + project_back(grad_values_own, back_value)
    )
    token_sum, grad_again_part = (
        lax.psum_scatter(
            token_part.astype(jnp.bfloat16), "tp", scatter_dimension=1, tiled=True
        ).astype(jnp.float32),
        lax.psum_scatter(
            grad_again.reshape(-1, head_dim).astype(jnp.bfloat16),
            "tp",
            scatter_dimension=0,
            tiled=True,
        ).astype(jnp.float32),
    )
    grad_tokens = grad_hidden + token_sum
    summed = (
        lax.psum_scatter(
            grad_wquery.astype(jnp.bfloat16), ("dp", "seq"), scatter_dimension=0, tiled=True
        ).astype(jnp.float32),
        lax.psum_scatter(
            grad_wkey.astype(jnp.bfloat16), ("dp", "seq"), scatter_dimension=0, tiled=True
        ).astype(jnp.float32),
        lax.psum_scatter(
            grad_wvalue.astype(jnp.bfloat16), ("dp", "seq"), scatter_dimension=0, tiled=True
        ).astype(jnp.float32),
        lax.psum_scatter(
            grad_wout.astype(jnp.bfloat16), ("dp", "seq"), scatter_dimension=1, tiled=True
        ).astype(jnp.float32),
        lax.psum_scatter(
            grad_wgate.astype(jnp.bfloat16), ("dp", "seq"), scatter_dimension=0, tiled=True
        ).astype(jnp.float32),
        lax.psum_scatter(
            grad_wup.astype(jnp.bfloat16), ("dp", "seq"), scatter_dimension=0, tiled=True
        ).astype(jnp.float32),
        lax.psum_scatter(
            grad_wdown.astype(jnp.bfloat16), ("dp", "seq"), scatter_dimension=1, tiled=True
        ).astype(jnp.float32),
        lax.psum_scatter(
            grad_qgain.reshape(local_heads, head_dim).astype(jnp.bfloat16),
            ("dp", "seq"),
            scatter_dimension=1,
            tiled=True,
        ).astype(jnp.float32),
        lax.psum_scatter(
            grad_kgain.reshape(local_heads, head_dim).astype(jnp.bfloat16),
            ("dp", "seq"),
            scatter_dimension=1,
            tiled=True,
        ).astype(jnp.float32),
        lax.psum_scatter(
            grad_again_part.astype(jnp.bfloat16), ("dp", "seq"), scatter_dimension=1, tiled=True
        ).astype(jnp.float32),
        lax.psum_scatter(
            grad_mgain_part.astype(jnp.bfloat16), ("dp", "seq"), scatter_dimension=1, tiled=True
        ).astype(jnp.float32),
    )
    (
        sum_query,
        sum_key,
        sum_value,
        sum_out,
        sum_gate,
        sum_up,
        sum_down,
        sum_qgain,
        sum_kgain,
        sum_again,
        sum_mgain,
    ) = summed
    return (
        outputs,
        grad_tokens,
        sum_query,
        sum_key,
        sum_value,
        sum_out,
        sum_gate,
        sum_up,
        sum_down,
        sum_qgain,
        sum_kgain,
        sum_again,
        sum_mgain,
    )


LOW = jnp.bfloat16
VMEM_LIMIT = 50 * 1024 * 1024
PARAMS = pltpu.CompilerParams(vmem_limit_bytes=VMEM_LIMIT)


def to_neighbour(values, flip):
    return lax.ppermute(values, "seq", [(i, i ^ flip) for i in range(4)])


def to_core(values):
    return lax.ppermute(values, "dp", [(0, 1), (1, 0)])


def after(values, done):
    return lax.optimization_barrier((values, done))[0]


def first_step(shard):
    return to_neighbour(shard, 1), to_neighbour(shard, 2)


def gather_plane(shard, firsts, meanwhile=()):
    half = shard.shape[0] // 2
    (from_one, from_two), meanwhile = lax.optimization_barrier((firsts, meanwhile))
    far_low = to_neighbour(from_two[:half], 1)
    far_high = to_neighbour(from_one[half:], 2)
    mine = [shard, from_one, from_two, far_low, far_high]
    return mine + [to_core(piece) for piece in mine], meanwhile


def place_piece(out_ref, order_ref, k, piece, axis):
    block = piece.shape[axis]
    if axis == 0 and k % 5 > 2:
        block *= 2
    first = piece.shape[0] if k % 5 == 4 else 0
    start = order_ref[(k // 5) * 4 + min(k % 5, 3)] * block
    if axis == 0:
        out_ref[pl.ds(pl.multiple_of(start + first, piece.shape[0]), piece.shape[0])] = piece
    else:
        out_ref[first : first + piece.shape[0], pl.ds(pl.multiple_of(start, block), block)] = piece


def assemble_columns(pieces, order):
    height, block = pieces[0].shape

    def body(order_ref, *refs):
        for k in range(10):
            place_piece(refs[10], order_ref, k, refs[k][...], 1)

    return pl.pallas_call(
        body,
        in_specs=[pl.BlockSpec(memory_space=pltpu.SMEM)]
        + [pl.BlockSpec(memory_space=pltpu.VMEM)] * 10,
        out_specs=pl.BlockSpec(memory_space=pltpu.VMEM),
        out_shape=jax.ShapeDtypeStruct((height, 8 * block), pieces[0].dtype),
        compiler_params=PARAMS,
        name="assemble_columns",
    )(order, *pieces)


def project_in(rows_low, pieces, order):
    rows, width = rows_low.shape
    columns = pieces[0].shape[1]
    tile = columns // 3

    def body(order_ref, rows_ref, *refs):
        for k in range(10):
            place_piece(refs[11], order_ref, k, refs[k][...], 0)
        refs[10][...] = jnp.dot(rows_ref[...], refs[11][...], preferred_element_type=jnp.float32)

    return pl.pallas_call(
        body,
        grid_spec=pltpu.PrefetchScalarGridSpec(
            num_scalar_prefetch=1,
            grid=(3,),
            in_specs=[pl.BlockSpec((rows, width), lambda j, o: (0, 0))]
            + [pl.BlockSpec((piece.shape[0], tile), lambda j, o: (0, j)) for piece in pieces],
            out_specs=[
                pl.BlockSpec((rows, tile), lambda j, o: (0, j)),
                pl.BlockSpec((width, tile), lambda j, o: (0, j)),
            ],
        ),
        out_shape=[
            jax.ShapeDtypeStruct((rows, columns), jnp.float32),
            jax.ShapeDtypeStruct((width, columns), LOW),
        ],
        compiler_params=PARAMS,
        name="project_in",
    )(order, rows_low, *pieces)


def grad_blocks(lefts, rights, groups, order, blocks, received=None):
    rows, d_model = lefts[0].shape
    block = d_model // 8
    half = block // 2
    count = len(blocks)
    width = sum(rights[right].shape[1] for _, right in groups[0])
    fresh = received is None

    def body(order_ref, *refs):
        left_refs, right_refs = refs[: len(lefts)], refs[len(lefts) : len(lefts) + len(rights)]
        rest = refs[len(lefts) + len(rights) :]
        for k, pairs in enumerate(groups):

            @pl.when(pl.program_id(1) == k)
            def _(pairs=pairs):
                first = 0
                for left, right in pairs:
                    total = contract(left_refs[left][...], right_refs[right][...], 0, 0)
                    columns = slice(first, first + total.shape[1])
                    first += total.shape[1]
                    if fresh:
                        rest[0][:, columns] = total.astype(LOW)
                        continue
                    total = (total + rest[0][:, columns].astype(jnp.float32)).astype(LOW)
                    for b in range(count):

                        @pl.when(pl.program_id(0) == b)
                        def _(total=total, columns=columns, b=b):
                            rest[1 + 2 * b][:, columns] = total[:half]
                            rest[2 + 2 * b][:, columns] = total[half:]

    def chosen(b, j, k):
        return jnp.where(j == b, k, jnp.where(j < b, 0, len(groups) - 1))

    def pick(j):
        value = blocks[0]
        for i, entry in enumerate(blocks[1:]):
            value = jnp.where(j > i, entry, value)
        return value

    in_specs = [pl.BlockSpec((rows, block), lambda j, k, o: (0, o[pick(j)])) for _ in lefts]
    in_specs += [pl.BlockSpec(right.shape, lambda j, k, o: (0, 0)) for right in rights]
    if fresh:
        out_specs = [pl.BlockSpec((block, width), lambda j, k, o: (j, k))]
        out_shape = [jax.ShapeDtypeStruct((count * block, len(groups) * width), LOW)]
    else:
        in_specs.append(pl.BlockSpec((block, width), lambda j, k, o: (pick(j), k)))
        out_specs = [
            pl.BlockSpec((half, width), lambda j, k, o, b=b: (0, chosen(b, j, k)))
            for b in range(count)
            for _ in range(2)
        ]
        out_shape = [jax.ShapeDtypeStruct((half, len(groups) * width), LOW)] * (2 * count)
    return pl.pallas_call(
        body,
        grid_spec=pltpu.PrefetchScalarGridSpec(
            num_scalar_prefetch=1, grid=(count, len(groups)), in_specs=in_specs, out_specs=out_specs
        ),
        out_shape=out_shape,
        compiler_params=PARAMS,
        name="grad_blocks",
    )(order, *lefts, *rights, *(() if fresh else (received,)))


def add_low(mine, got):
    return (mine.astype(jnp.float32) + got.astype(jnp.float32)).astype(LOW)


def sum_in_core(lefts, rights, groups, order):
    (sent,) = grad_blocks(lefts, rights, groups, order, (4, 5, 6, 7))
    received = to_core(sent)
    far = grad_blocks(lefts, rights, groups, order, (3,), received)
    near = grad_blocks(lefts, rights, groups, order, (1, 2, 0), received)
    return far, near


def send_first(far, near):
    one_low, _, _, two_high, _, _ = near
    return [to_neighbour(far[0], 1), to_neighbour(far[1], 2)], [
        to_neighbour(one_low, 1),
        to_neighbour(two_high, 2),
    ]


def send_second(far, near):
    return [
        to_neighbour(add_low(near[1], far[1]), 1),
        to_neighbour(add_low(near[2], far[0]), 2),
    ]


def halves_total(near, first, second):
    def total(*values):
        low, one, two = (value.astype(jnp.float32) for value in values)
        return low + one + two

    return total(near[4], first[0], second[1]), total(near[5], second[0], first[1])


def gather_line(own):
    up, down = own, own
    ups, downs = [], []
    for t in range(1, 4):
        up = lax.ppermute(up, "tp", [(i, i + 1) for i in range(t - 1, 3)])
        down = lax.ppermute(down, "tp", [(i, i - 1) for i in range(1, 5 - t)])
        ups.append(up)
        downs.append(down)
    return [own] + ups + downs


def scatter_line(slots, meanwhile=((), ())):
    meanwhile = list(meanwhile)
    def added(mine, got):
        return (mine.astype(jnp.float32) + got.astype(jnp.float32)).astype(LOW)

    up, down = slots[1], slots[3]
    for t in range(1, 4):
        up = lax.ppermute(up, "tp", [(i, i + 1) for i in range(t)])
        down = lax.ppermute(down, "tp", [(i, i - 1) for i in range(4 - t, 4)])
        if t < 3:
            up, down, meanwhile[t - 1] = lax.optimization_barrier((up, down, meanwhile[t - 1]))
            up = added(slots[t + 1], up)
            down = added(slots[3 - t], down)
    total = slots[0].astype(jnp.float32) + up.astype(jnp.float32) + down.astype(jnp.float32)
    return total, meanwhile


def sum_line(values):
    flat = lax.optimization_barrier(values.reshape(-1, 128))
    return lax.optimization_barrier(lax.psum(flat, "tp"))


def contract(left, right, left_dim, right_dim):
    return lax.dot_general(
        left, right, (((left_dim,), (right_dim,)), ((), ())), preferred_element_type=jnp.float32
    )


def turned(values, cosines, sines):
    return values * cosines + pltpu.roll(values, values.shape[-1] // 2, axis=1) * sines


def inverse_norm(squares, d_model):
    return lax.rsqrt(squares * (1.0 / d_model) + NORM_EPS)


def prepare(raw, squares, gains, cosines, sines, heads, head_dim, d_model):
    seqs, length, _ = raw.shape
    own = length // 4
    rows = seqs * own
    span = heads * head_dim

    def body(raw_ref, square_ref, gain_ref, cos_ref, sin_ref, out_ref):
        cosine = jnp.concatenate([cos_ref[...]] * seqs, axis=0)
        sine = jnp.concatenate([sin_ref[...]] * seqs, axis=0)
        for t in range(2):
            inv = inverse_norm(square_ref[t].reshape(rows, 1), d_model)
            for h in range(heads):
                columns = slice(t * span + h * head_dim, t * span + (h + 1) * head_dim)
                normed = raw_ref[:, :, columns].reshape(rows, head_dim) * inv * gain_ref[:, columns]
                out_ref[h, t] = (
                    turned(normed, cosine, sine).astype(LOW).reshape(seqs, own, head_dim)
                )
        for h in range(heads):
            columns = slice(2 * span + h * head_dim, 2 * span + (h + 1) * head_dim)
            out_ref[h, 2] = raw_ref[:, :, columns].astype(LOW)

    return pl.pallas_call(
        body,
        grid=(4,),
        in_specs=[
            pl.BlockSpec((seqs, own, 3 * span), lambda t: (0, t, 0)),
            pl.BlockSpec((2, seqs, own, 1), lambda t: (0, 0, t, 0)),
            pl.BlockSpec((1, 2 * span), lambda t: (0, 0)),
            pl.BlockSpec((own, head_dim), lambda t: (t, 0)),
            pl.BlockSpec((own, head_dim), lambda t: (t, 0)),
        ],
        out_specs=pl.BlockSpec((heads, 3, seqs, own, head_dim), lambda t: (0, 0, 0, t, 0)),
        out_shape=jax.ShapeDtypeStruct((heads, 3, seqs, length, head_dim), LOW),
        compiler_params=PARAMS,
        name="prepare",
    )(raw, squares, gains, cosines, sines)


def scores_of(left, right):
    return lax.dot_general(
        left, right, (((1,), (1,)), ((), ())), preferred_element_type=jnp.float32
    )


def causal(scores, first):
    rows = lax.broadcasted_iota(jnp.int32, scores.shape, 0) + first
    columns = lax.broadcasted_iota(jnp.int32, scores.shape, 1)
    return columns <= rows


def attend(parts):
    blocks, _, seqs, length, head_dim = parts.shape
    score_scale = head_dim ** (-0.5)

    def body(parts_ref, out_ref, log_ref):
        for i in range(blocks):
            span = (i + 1) * length
            keys = parts_ref[: i + 1, 1, 0].reshape(span, head_dim)
            values = parts_ref[: i + 1, 2, 0].reshape(span, head_dim)
            scores = scores_of(parts_ref[i, 0, 0], keys) * score_scale
            scores = jnp.where(causal(scores, i * length), scores, MASKED)
            top = jnp.max(scores, axis=-1, keepdims=True)
            weights = jnp.exp(scores - top)
            total = jnp.sum(weights, axis=-1, keepdims=True)
            probs = (weights * (1.0 / total)).astype(LOW)
            out_ref[i, 0] = jnp.dot(probs, values, preferred_element_type=jnp.float32).astype(LOW)
            log_ref[i, 0] = top + jnp.log(total)

    return pl.pallas_call(
        body,
        grid=(seqs,),
        in_specs=[pl.BlockSpec((blocks, 3, 1, length, head_dim), lambda m: (0, 0, m, 0, 0))],
        out_specs=[
            pl.BlockSpec((blocks, 1, length, head_dim), lambda m: (0, m, 0, 0)),
            pl.BlockSpec((blocks, 1, length, 1), lambda m: (0, m, 0, 0)),
        ],
        out_shape=[
            jax.ShapeDtypeStruct((blocks, seqs, length, head_dim), LOW),
            jax.ShapeDtypeStruct((blocks, seqs, length, 1), jnp.float32),
        ],
        compiler_params=PARAMS,
        name="attend",
    )(parts)


def attend_back(parts, grad_context, log_total):
    blocks, _, seqs, length, head_dim = parts.shape
    score_scale = head_dim ** (-0.5)

    def body(parts_ref, grad_ref, log_ref, out_ref, keys_sum, values_sum):
        keys_sum[...] = jnp.zeros_like(keys_sum)
        values_sum[...] = jnp.zeros_like(values_sum)
        for i in range(blocks):
            span = (i + 1) * length
            queries = parts_ref[i, 0, 0]
            keys = parts_ref[: i + 1, 1, 0].reshape(span, head_dim)
            values = parts_ref[: i + 1, 2, 0].reshape(span, head_dim)
            grads = grad_ref[i, 0]
            scores = scores_of(queries, keys) * score_scale
            probs = jnp.where(causal(scores, i * length), jnp.exp(scores - log_ref[i, 0]), 0.0)
            grad_probs = scores_of(grads, values)
            delta = jnp.sum(probs * grad_probs, axis=-1, keepdims=True)
            grad_scores = (probs * (grad_probs - delta)).astype(LOW)
            out_ref[i, 0, 0] = (
                jnp.dot(grad_scores, keys, preferred_element_type=jnp.float32) * score_scale
            ).astype(LOW)
            keys_sum[:span] += contract(grad_scores, queries, 0, 0)
            values_sum[:span] += contract(probs.astype(LOW), grads, 0, 0)
        out_ref[:, 1, 0] = (
            (keys_sum[...] * score_scale).astype(LOW).reshape(blocks, length, head_dim)
        )
        out_ref[:, 2, 0] = values_sum[...].astype(LOW).reshape(blocks, length, head_dim)

    whole = pl.BlockSpec((blocks, 3, 1, length, head_dim), lambda m: (0, 0, m, 0, 0))
    return pl.pallas_call(
        body,
        grid=(seqs,),
        in_specs=[
            whole,
            pl.BlockSpec((blocks, 1, length, head_dim), lambda m: (0, m, 0, 0)),
            pl.BlockSpec((blocks, 1, length, 1), lambda m: (0, m, 0, 0)),
        ],
        out_specs=whole,
        out_shape=jax.ShapeDtypeStruct(parts.shape, LOW),
        scratch_shapes=[
            pltpu.VMEM((blocks * length, head_dim), jnp.float32),
            pltpu.VMEM((blocks * length, head_dim), jnp.float32),
        ],
        compiler_params=PARAMS,
        name="attend_back",
    )(parts, grad_context, log_total)


def project_out(context, weights, slots):
    heads, seqs, length, head_dim = context.shape
    span, width = weights.shape
    own = length // 4
    own_rows = seqs * own
    tile = width // 2

    def body(slots_ref, context_ref, weight_ref, rows_ref, *outs):
        @pl.when(pl.program_id(0) == 0)
        def _():
            for t in range(4):
                place = pl.ds(pl.multiple_of(slots_ref[t] * own, own), own)
                for h in range(heads):
                    rows_ref[
                        t * own_rows : (t + 1) * own_rows, h * head_dim : (h + 1) * head_dim
                    ] = context_ref[h, :, place].reshape(own_rows, head_dim)

        product = jnp.dot(rows_ref[...], weight_ref[...], preferred_element_type=jnp.float32)
        for t in range(4):
            outs[t][...] = product[t * own_rows : (t + 1) * own_rows].astype(LOW)

    return pl.pallas_call(
        body,
        grid_spec=pltpu.PrefetchScalarGridSpec(
            num_scalar_prefetch=1,
            grid=(2,),
            in_specs=[
                pl.BlockSpec(context.shape, lambda j, s: (0, 0, 0, 0)),
                pl.BlockSpec((span, tile), lambda j, s: (0, j)),
            ],
            out_specs=[pl.BlockSpec((4 * own_rows, span), lambda j, s: (0, 0))]
            + [pl.BlockSpec((own_rows, tile), lambda j, s: (0, j))] * 4,
        ),
        out_shape=[jax.ShapeDtypeStruct((4 * own_rows, span), LOW)]
        + [jax.ShapeDtypeStruct((own_rows, width), LOW)] * 4,
        compiler_params=PARAMS,
        name="project_out",
    )(slots, context, weights)


def project_out_back(pieces, weights, slots, heads, seqs):
    own_rows, width = pieces[0].shape
    span = weights.shape[0]
    head_dim = span // heads
    own = own_rows // seqs
    rows = 4 * own_rows

    def body(slots_ref, *refs):
        ins, weight_ref, out_ref, rows_ref = refs[:7], refs[7], refs[8], refs[9]
        fill_slots(rows_ref, ins)
        product = scores_of(rows_ref[...], weight_ref[...]).astype(LOW)
        for t in range(4):
            place = pl.ds(pl.multiple_of(slots_ref[t] * own, own), own)
            for h in range(heads):
                out_ref[h, :, place] = product[
                    t * own_rows : (t + 1) * own_rows, h * head_dim : (h + 1) * head_dim
                ].reshape(seqs, own, head_dim)

    scalars = pl.BlockSpec(memory_space=pltpu.SMEM)
    whole = pl.BlockSpec(memory_space=pltpu.VMEM)
    return pl.pallas_call(
        body,
        in_specs=[scalars] + [whole] * 8,
        out_specs=[whole] * 2,
        out_shape=[
            jax.ShapeDtypeStruct((heads, seqs, 4 * own, head_dim), LOW),
            jax.ShapeDtypeStruct((rows, width), LOW),
        ],
        compiler_params=PARAMS,
        name="project_out_back",
    )(slots, *pieces, weights)


def unprepare(grads, raw, squares, gains, cosines, sines, d_model):
    heads, _, seqs, length, head_dim = grads.shape
    own = length // 4
    rows = seqs * own
    span = heads * head_dim

    def body(
        grad_ref, raw_ref, square_ref, gain_ref, cos_ref, sin_ref, scaled_ref, dot_ref, sum_ref
    ):
        cosine = jnp.concatenate([cos_ref[...]] * seqs, axis=0)
        sine = -jnp.concatenate([sin_ref[...]] * seqs, axis=0)

        @pl.when(pl.program_id(0) == 0)
        def _():
            sum_ref[...] = jnp.zeros_like(sum_ref)

        for t in range(2):
            inv = inverse_norm(square_ref[t].reshape(rows, 1), d_model)
            total = jnp.zeros((rows, head_dim), jnp.float32)
            for h in range(heads):
                columns = slice(t * span + h * head_dim, t * span + (h + 1) * head_dim)
                back = turned(
                    grad_ref[h, t].reshape(rows, head_dim).astype(jnp.float32), cosine, sine
                )
                along = back * (raw_ref[:, :, columns].reshape(rows, head_dim) * inv)
                sum_ref[:, columns] += jnp.sum(along, axis=0, keepdims=True)
                scaled_ref[:, :, columns] = (back * gain_ref[:, columns]).reshape(
                    seqs, own, head_dim
                )
                total += along * gain_ref[:, columns]
            dot_ref[t] = jnp.sum(total, axis=-1, keepdims=True).reshape(seqs, own, 1)

    return pl.pallas_call(
        body,
        grid=(4,),
        in_specs=[
            pl.BlockSpec((heads, 3, seqs, own, head_dim), lambda t: (0, 0, 0, t, 0)),
            pl.BlockSpec((seqs, own, 3 * span), lambda t: (0, t, 0)),
            pl.BlockSpec((2, seqs, own, 1), lambda t: (0, 0, t, 0)),
            pl.BlockSpec((1, 2 * span), lambda t: (0, 0)),
            pl.BlockSpec((own, head_dim), lambda t: (t, 0)),
            pl.BlockSpec((own, head_dim), lambda t: (t, 0)),
        ],
        out_specs=[
            pl.BlockSpec((seqs, own, 2 * span), lambda t: (0, t, 0)),
            pl.BlockSpec((2, seqs, own, 1), lambda t: (0, 0, t, 0)),
            pl.BlockSpec((1, 2 * span), lambda t: (0, 0)),
        ],
        out_shape=[
            jax.ShapeDtypeStruct((seqs, length, 2 * span), jnp.float32),
            jax.ShapeDtypeStruct((2, seqs, length, 1), jnp.float32),
            jax.ShapeDtypeStruct((1, 2 * span), jnp.float32),
        ],
        compiler_params=PARAMS,
        name="unprepare",
    )(grads, raw, squares, gains, cosines, sines)


def project_in_back(grads, scaled, raw, squares, dots, weights, slots):
    heads, _, seqs, length, head_dim = grads.shape
    own = length // 4
    own_rows = seqs * own
    rows = seqs * length
    span = heads * head_dim
    d_model = weights.shape[0]
    tile = d_model // 4

    def body(
        slots_ref, grad_ref, scaled_ref, raw_ref, square_ref, dot_ref, weight_ref, rows_ref, *refs
    ):
        outs, product = refs[:4], refs[4]

        @pl.when(pl.program_id(0) == 0)
        def _():
            for k in range(2):
                columns = slice(k * span, (k + 1) * span)
                inv = inverse_norm(square_ref[k].reshape(rows, 1), d_model)
                mean = dot_ref[k].reshape(rows, 1) * (1.0 / d_model)
                unit = raw_ref[:, :, columns].reshape(rows, span) * inv
                rows_ref[:, columns] = (
                    inv * (scaled_ref[:, :, columns].reshape(rows, span) - unit * mean)
                ).astype(LOW)
            for h in range(heads):
                columns = slice(2 * span + h * head_dim, 2 * span + (h + 1) * head_dim)
                rows_ref[:, columns] = grad_ref[h, 0].reshape(rows, head_dim)

        product[...] = scores_of(rows_ref[...], weight_ref[...]).reshape(seqs, length, tile)
        for t in range(4):
            place = pl.ds(pl.multiple_of(slots_ref[t] * own, own), own)
            outs[t][...] = product[:, place].reshape(own_rows, tile).astype(LOW)

    flat = pl.BlockSpec((2, seqs, length, 1), lambda j, s: (0, 0, 0, 0))
    return pl.pallas_call(
        body,
        grid_spec=pltpu.PrefetchScalarGridSpec(
            num_scalar_prefetch=1,
            grid=(4,),
            in_specs=[
                pl.BlockSpec((heads, 1, seqs, length, head_dim), lambda j, s: (0, 2, 0, 0, 0)),
                pl.BlockSpec((seqs, length, 2 * span), lambda j, s: (0, 0, 0)),
                pl.BlockSpec((seqs, length, 2 * span), lambda j, s: (0, 0, 0)),
                flat,
                flat,
                pl.BlockSpec((tile, 3 * span), lambda j, s: (j, 0)),
            ],
            out_specs=[pl.BlockSpec((rows, 3 * span), lambda j, s: (0, 0))]
            + [pl.BlockSpec((own_rows, tile), lambda j, s: (0, j))] * 4,
            scratch_shapes=[pltpu.VMEM((seqs, length, tile), jnp.float32)],
        ),
        out_shape=[jax.ShapeDtypeStruct((rows, 3 * span), LOW)]
        + [jax.ShapeDtypeStruct((own_rows, d_model), LOW)] * 4,
        compiler_params=PARAMS,
        name="project_in_back",
    )(slots, grads, scaled, raw, squares, dots, weights)


def fill_slots(rows_ref, refs):
    own = refs[0].shape[0]
    rows_ref[:own] = refs[0][...]
    for t in range(1, 4):
        rows_ref[t * own : (t + 1) * own] = refs[t][...] + refs[7 - t][...]


def weight_tiles(width, tile, tiles):
    return [pl.BlockSpec((width, tile), lambda j, k=k: (0, k * tiles + j)) for k in range(3)]


def feed_forward(pieces, weights):
    own, width = pieces[0].shape
    hidden_units = weights.shape[1] // 3
    tile = 512
    tiles = hidden_units // tile
    rows = 4 * own

    def body(*refs):
        ins, (gate_w, up_w, down_w) = refs[:7], refs[7:10]
        rows_ref, gate_ref, up_ref, mixed_ref = refs[10:14]
        outs, total = refs[14:18], refs[18]

        @pl.when(pl.program_id(0) == 0)
        def _():
            fill_slots(rows_ref, ins)

        gate = jnp.dot(rows_ref[...], gate_w[...], preferred_element_type=jnp.float32)
        up = jnp.dot(rows_ref[...], up_w[...], preferred_element_type=jnp.float32)
        mixed = (gate * jax.nn.sigmoid(gate) * up).astype(LOW)
        gate_ref[...] = gate.astype(LOW)
        up_ref[...] = up.astype(LOW)
        mixed_ref[...] = mixed
        part = scores_of(mixed, down_w[...])

        @pl.when(pl.program_id(0) == 0)
        def _():
            total[...] = part

        @pl.when((pl.program_id(0) > 0) & (pl.program_id(0) < tiles - 1))
        def _():
            total[...] += part

        @pl.when(pl.program_id(0) == tiles - 1)
        def _():
            for t in range(4):
                mine = slice(t * own, (t + 1) * own)
                outs[t][...] = (total[mine] + part[mine]).astype(LOW)

    fixed = pl.BlockSpec((own, width), lambda j: (0, 0))
    by_tile = pl.BlockSpec((rows, tile), lambda j: (0, j))
    return pl.pallas_call(
        body,
        grid=(tiles,),
        in_specs=[fixed] * 7 + weight_tiles(width, tile, tiles),
        out_specs=[pl.BlockSpec((rows, width), lambda j: (0, 0))] + [by_tile] * 3 + [fixed] * 4,
        out_shape=[jax.ShapeDtypeStruct((rows, width), LOW)]
        + [jax.ShapeDtypeStruct((rows, hidden_units), LOW)] * 3
        + [jax.ShapeDtypeStruct((own, width), LOW)] * 4,
        scratch_shapes=[pltpu.VMEM((rows, width), jnp.float32)],
        compiler_params=PARAMS,
        name="feed_forward",
    )(*pieces, weights, weights, weights)


def feed_forward_back(rows_low, gate, up, weights):
    rows, width = rows_low.shape
    own = rows // 4
    hidden_units = gate.shape[1]
    tile = 512
    tiles = hidden_units // tile

    def body(rows_ref, gate_ref, up_ref, gate_w, up_w, down_w, grad_gate_ref, grad_up_ref, *refs):
        outs, total = refs[:4], refs[4]
        grad_mixed = jnp.dot(rows_ref[...], down_w[...], preferred_element_type=jnp.float32)
        gate = gate_ref[...].astype(jnp.float32)
        up = up_ref[...].astype(jnp.float32)
        sig = jax.nn.sigmoid(gate)
        grad_gate = (grad_mixed * up * sig * (1.0 + gate * (1.0 - sig))).astype(LOW)
        grad_up = (grad_mixed * gate * sig).astype(LOW)
        grad_gate_ref[...] = grad_gate
        grad_up_ref[...] = grad_up
        part = scores_of(grad_gate, gate_w[...]) + scores_of(grad_up, up_w[...])

        @pl.when(pl.program_id(0) == 0)
        def _():
            total[...] = part

        @pl.when((pl.program_id(0) > 0) & (pl.program_id(0) < tiles - 1))
        def _():
            total[...] += part

        @pl.when(pl.program_id(0) == tiles - 1)
        def _():
            for t in range(4):
                mine = slice(t * own, (t + 1) * own)
                outs[t][...] = (total[mine] + part[mine]).astype(LOW)

    fixed = pl.BlockSpec((own, width), lambda j: (0, 0))
    by_tile = pl.BlockSpec((rows, tile), lambda j: (0, j))
    return pl.pallas_call(
        body,
        grid=(tiles,),
        in_specs=[pl.BlockSpec((rows, width), lambda j: (0, 0))]
        + [by_tile] * 2
        + weight_tiles(width, tile, tiles),
        out_specs=[by_tile] * 2 + [fixed] * 4,
        out_shape=[jax.ShapeDtypeStruct((rows, hidden_units), LOW)] * 2
        + [jax.ShapeDtypeStruct((own, width), LOW)] * 4,
        scratch_shapes=[pltpu.VMEM((rows, width), jnp.float32)],
        compiler_params=PARAMS,
        name="feed_forward_back",
    )(rows_low, gate, up, weights, weights, weights)


def down_grad(pieces, mixed):
    own, width = pieces[0].shape
    rows, columns = mixed.shape
    tile = 512

    def body(*refs):
        rows_ref, out_ref = refs[8], refs[9]

        @pl.when(pl.program_id(0) == 0)
        def _():
            fill_slots(rows_ref, refs[:7])

        place = pl.ds(pl.multiple_of(pl.program_id(0) * tile, tile), tile)
        out_ref[...] = contract(rows_ref[:, place], refs[7][...], 0, 0).astype(LOW)

    return pl.pallas_call(
        body,
        grid=(width // tile,),
        in_specs=[pl.BlockSpec((own, width), lambda j: (0, 0))] * 7
        + [pl.BlockSpec((rows, columns), lambda j: (0, 0))],
        out_specs=[
            pl.BlockSpec((rows, width), lambda j: (0, 0)),
            pl.BlockSpec((tile, columns), lambda j: (j, 0)),
        ],
        out_shape=[
            jax.ShapeDtypeStruct((rows, width), LOW),
            jax.ShapeDtypeStruct((width, columns), LOW),
        ],
        compiler_params=PARAMS,
        name="down_grad",
    )(*pieces, mixed)


def weight_grad(left, right, all_columns, place, others=None):
    rows, width = left.shape
    columns = right.shape[1]
    tile = 512

    def body(left_ref, right_ref, *refs):
        refs[-1][...] = contract(left_ref[...], right_ref[...], 0, 0).astype(LOW)

    given = () if others is None else (others,)
    return pl.pallas_call(
        body,
        grid=(width // tile,),
        in_specs=[
            pl.BlockSpec((rows, tile), lambda j: (0, j)),
            pl.BlockSpec((rows, columns), lambda j: (0, 0)),
        ]
        + [pl.BlockSpec(memory_space=pl.ANY)] * len(given),
        out_specs=pl.BlockSpec((tile, columns), lambda j: (j, place)),
        out_shape=jax.ShapeDtypeStruct((width, all_columns), LOW),
        input_output_aliases={2: 0} if given else {},
        compiler_params=PARAMS,
        name="weight_grad",
    )(left, right, *given)


def on_plane(
    tokens,
    w_query,
    w_key,
    w_value,
    w_out,
    w_gate,
    w_up,
    w_down,
    q_gain,
    k_gain,
    attn_gain,
    mlp_gain,
    cotangent,
):
    seqs, length, d_model = tokens.shape
    rows = seqs * length
    tp_rank = lax.axis_index("tp")
    seq_rank = lax.axis_index("seq")
    heads = q_gain.shape[0]
    head_dim = q_gain.shape[1] * 8
    head_span = heads * head_dim
    own_length = length // 4
    own_rows = seqs * own_length
    order = (lax.axis_index("dp") * 4 + seq_rank) ^ jnp.arange(8, dtype=jnp.int32)
    slots = (tp_rank + 4 - jnp.arange(4, dtype=jnp.int32)) % 4

    gain_rows = jnp.concatenate([q_gain, k_gain, attn_gain, mlp_gain], axis=0)
    all_gains = lax.all_to_all(
        jnp.broadcast_to(gain_rows.reshape(1, -1), (8, gain_rows.size)), ("dp", "seq"), 0, 0, tiled=True
    )
    packed = jnp.concatenate([w_gate, w_up, w_down.T], axis=1)
    in_shard = jnp.concatenate([w_query, w_key, w_value], axis=1)
    in_pieces, (all_gains, packed) = gather_plane(
        in_shard, first_step(in_shard), (all_gains, packed)
    )
    all_gains = (
        jnp.transpose(all_gains.reshape((8,) + gain_rows.shape), (1, 0, 2))
        .reshape(gain_rows.shape[0], head_dim)
        .astype(jnp.float32)
    )
    qk_gain = all_gains[: 2 * heads].reshape(1, 2 * head_span)
    feature_rows = d_model // head_dim
    attn_gains = all_gains[2 * heads : 2 * heads + feature_rows].reshape(d_model)
    mlp_gains = all_gains[2 * heads + feature_rows :].reshape(d_model)
    positions = seq_rank * length + jnp.arange(length, dtype=jnp.int32)
    cosines, sines = rope_tables(positions, head_dim)
    cosines = jnp.concatenate([cosines[:, 0], cosines[:, 0]], axis=-1)
    sines = jnp.concatenate([-sines[:, 0], sines[:, 0]], axis=-1)
    own_tokens = (
        lax.dynamic_slice_in_dim(tokens, tp_rank * own_length, own_length, 1)
        .astype(jnp.float32)
        .reshape(own_rows, d_model)
    )
    grad_out = cotangent.astype(jnp.float32).reshape(own_rows, d_model)

    raw, in_weights = project_in(tokens.reshape(rows, d_model), in_pieces, order)
    out_firsts = first_step(after(w_out, in_pieces[3:5]))
    weights = lax.all_gather(after(packed, in_pieces[3:5]), ("dp", "seq"), axis=0, tiled=True)

    squares = jnp.stack(
        [
            jnp.sum(jnp.square(raw[:, :head_span]), axis=-1),
            jnp.sum(jnp.square(raw[:, head_span : 2 * head_span]), axis=-1),
        ]
    )
    squares, out_firsts = lax.optimization_barrier((sum_line(squares), out_firsts))
    squares = squares.reshape(2, seqs, length, 1)
    out_pieces, _ = gather_plane(w_out, out_firsts)
    raw = raw.reshape(seqs, length, 3 * head_span)
    parts = prepare(raw, squares, qk_gain, cosines, sines, heads, head_dim, d_model)
    parts = lax.all_to_all(parts, "seq", 0, 0, tiled=True)
    parts, out_pieces = lax.optimization_barrier((parts, out_pieces))
    out_weights = assemble_columns(out_pieces, order)
    context, log_total = attend(parts)
    context = lax.all_to_all(context, "seq", 0, 0, tiled=True)
    context_rows, *attn_slots = project_out(context, out_weights, slots)
    attn_out, _ = scatter_line(attn_slots)
    attn_inv = lax.rsqrt(jnp.mean(attn_out * attn_out, axis=-1, keepdims=True) + NORM_EPS)
    attn_unit = attn_out * attn_inv
    hidden = own_tokens + attn_unit * attn_gains
    hidden_rows, gate, up, mixed, *mlp_slots = feed_forward(
        gather_line(hidden.astype(LOW)), weights
    )
    mlp_out, _ = scatter_line(mlp_slots)
    mlp_inv = lax.rsqrt(jnp.mean(mlp_out * mlp_out, axis=-1, keepdims=True) + NORM_EPS)
    mlp_unit = mlp_out * mlp_inv
    outputs = (hidden + mlp_unit * mlp_gains).astype(LOW)

    grad_mgain = jnp.sum(grad_out * mlp_unit, axis=0)
    mlp_scaled = grad_out * mlp_gains
    grad_mlp = norm_back(
        mlp_unit, mlp_scaled, mlp_inv, jnp.sum(mlp_scaled * mlp_unit, axis=-1), d_model
    )
    grad_mlp_rows, down_part = down_grad(gather_line(grad_mlp.astype(LOW)), mixed)
    grad_gate, grad_up, *hidden_slots = feed_forward_back(grad_mlp_rows, gate, up, weights)
    units = mixed.shape[1]
    gate_part = weight_grad(hidden_rows, grad_gate, 2 * units, 0)
    hidden_sum, (gate_part, _) = scatter_line(hidden_slots, (gate_part, ()))
    gate_up_part = weight_grad(hidden_rows, grad_up, 2 * units, 1, gate_part)
    hidden_sum, gate_up_part = lax.optimization_barrier((hidden_sum, gate_up_part))

    def sum_plane(part):
        return lax.optimization_barrier(
            lax.psum_scatter(part, ("dp", "seq"), scatter_dimension=0, tiled=True)
        )

    down_sum = sum_plane(down_part)
    gate_up_sum = sum_plane(gate_up_part)
    ff_sums = (
        gate_up_sum[:, :units].astype(jnp.float32),
        gate_up_sum[:, units:].astype(jnp.float32),
        down_sum.T.astype(jnp.float32),
    )

    def joined(halves, first, last):
        return jnp.concatenate([half[:, first:last] for half in halves], axis=0)

    grad_hidden = grad_out + hidden_sum
    grad_again = jnp.sum(grad_hidden * attn_unit, axis=0)
    attn_scaled = grad_hidden * attn_gains
    grad_attn = norm_back(
        attn_unit, attn_scaled, attn_inv, jnp.sum(attn_scaled * attn_unit, axis=-1), d_model
    ).astype(LOW)
    grad_context, grad_attn_rows = project_out_back(
        gather_line(grad_attn), out_weights, slots, heads, seqs
    )
    grad_context = lax.all_to_all(grad_context, "seq", 0, 0, tiled=True)
    part_grads = attend_back(parts, grad_context, log_total)
    part_grads = lax.all_to_all(part_grads, "seq", 0, 0, tiled=True)
    scaled, dots, qk_sums = unprepare(part_grads, raw, squares, qk_gain, cosines, sines, d_model)
    dots = sum_line(dots.reshape(2, rows)).reshape(2, seqs, length, 1)
    grad_raw, *token_slots = project_in_back(
        part_grads, scaled, raw, squares, dots, in_weights, slots
    )
    in_far, in_near = sum_in_core(
        (tokens.reshape(rows, d_model), grad_attn_rows),
        (grad_raw, context_rows),
        (((0, 0), (1, 1)),),
        order,
    )
    token_sum, (in_far, in_near) = scatter_line(token_slots, (in_far, in_near))
    in_far, in_first = send_first(in_far, in_near)
    in_second = send_second(in_far, in_near)
    in_second, ff_sums = lax.optimization_barrier((in_second, ff_sums))
    in_halves = halves_total(in_near, in_first, in_second)
    grad_tokens = grad_hidden + token_sum

    def by_owner(values):
        return jnp.transpose(values.reshape(4, feature_rows // 4, 8, -1), (2, 0, 1, 3))

    head_sums = jnp.transpose(qk_sums.reshape(2, heads, 8, -1), (2, 0, 1, 3))[:, None]
    is_own = (jnp.arange(4) == tp_rank)[None, :, None, None, None]
    payload = jnp.concatenate(
        [
            jnp.where(is_own, head_sums, 0.0),
            by_owner(grad_again)[:, :, None],
            by_owner(grad_mgain)[:, :, None],
        ],
        axis=2,
    ).reshape(32, -1)
    payload = after(payload, in_near)
    gain_sums = jnp.sum(
        lax.all_to_all(payload, ("dp", "seq", "tp"), 0, 0, tiled=True), axis=0
    ).reshape(4, heads, -1)
    return (
        outputs.reshape(seqs, own_length, d_model),
        grad_tokens.reshape(seqs, own_length, d_model),
        joined(in_halves, 0, head_span),
        joined(in_halves, head_span, 2 * head_span),
        joined(in_halves, 2 * head_span, 3 * head_span),
        joined(in_halves, 3 * head_span, 4 * head_span).T,
        ff_sums[0],
        ff_sums[1],
        ff_sums[2],
        gain_sums[0],
        gain_sums[1],
        gain_sums[2],
        gain_sums[3],
    )


def solution(mesh):
    by_plane = (mesh.shape["dp"], mesh.shape["seq"], mesh.shape["tp"]) == (2, 4, 4)
    return jax.shard_map(
        on_plane if by_plane else on_any_mesh,
        mesh=mesh,
        in_specs=(
            P("dp", "seq", None),
            P(("dp", "seq"), "tp"),
            P(("dp", "seq"), "tp"),
            P(("dp", "seq"), "tp"),
            P("tp", ("dp", "seq")),
            P(("dp", "seq"), "tp"),
            P(("dp", "seq"), "tp"),
            P("tp", ("dp", "seq")),
            P("tp", ("dp", "seq")),
            P("tp", ("dp", "seq")),
            P(None, ("dp", "seq")),
            P(None, ("dp", "seq")),
            P("dp", ("seq", "tp"), None),
        ),
        out_specs=(
            P("dp", ("seq", "tp"), None),
            P("dp", ("seq", "tp"), None),
            P(("dp", "seq"), "tp"),
            P(("dp", "seq"), "tp"),
            P(("dp", "seq"), "tp"),
            P("tp", ("dp", "seq")),
            P(("dp", "seq"), "tp"),
            P(("dp", "seq"), "tp"),
            P("tp", ("dp", "seq")),
            P("tp", ("dp", "seq")),
            P("tp", ("dp", "seq")),
            P("tp", ("dp", "seq")),
            P("tp", ("dp", "seq")),
        ),
        check_vma=False,
    )
```

```python
import math

import jax
import jax.numpy as jnp
from jax import lax
from jax.experimental import pallas as pl
from jax.experimental.pallas import tpu as pltpu
from jax.sharding import PartitionSpec as P

NORM_EPS = 1e-06
ROPE_BASE = 500000.0
MASKED = -1e30


def project(left, right):
    return jnp.dot(left, right, preferred_element_type=jnp.float32)


def project_back(left, right):
    return lax.dot_general(
        left, right, (((left.ndim - 1,), (1,)), ((), ())), preferred_element_type=jnp.float32
    )


def outer_sum(left, right):
    return lax.dot_general(
        left, right, (((0, 1), (0, 1)), ((), ())), preferred_element_type=jnp.float32
    )


def rope_tables(positions, head_dim):
    steps = jnp.arange(head_dim // 2, dtype=jnp.float32)
    freqs = jnp.exp(steps * (-2.0 * math.log(ROPE_BASE) / head_dim))
    angles = positions.astype(jnp.float32)[:, None] * freqs[None, :]
    return (jnp.cos(angles)[:, None, :], jnp.sin(angles)[:, None, :])


def rotate(values, cosines, sines):
    half = values.shape[-1] // 2
    first = values[..., :half]
    second = values[..., half:]
    return jnp.concatenate(
        [first * cosines - second * sines, second * cosines + first * sines], axis=-1
    )


def unrotate(grads, cosines, sines):
    half = grads.shape[-1] // 2
    first = grads[..., :half]
    second = grads[..., half:]
    return jnp.concatenate(
        [first * cosines + second * sines, second * cosines - first * sines], axis=-1
    )


def norm_back(normed, grad_normed, inv_scale, total_dot, d_model):
    return inv_scale * (grad_normed - normed * (total_dot / d_model)[..., None])


def on_any_mesh(
    tokens,
    w_query,
    w_key,
    w_value,
    w_out,
    w_gate,
    w_up,
    w_down,
    q_gain,
    k_gain,
    attn_gain,
    mlp_gain,
    cotangent,
):
    seq_count, local_len, d_model = tokens.shape
    seq_rank = lax.axis_index("seq")
    tp_rank = lax.axis_index("tp")
    own_rows = local_len // lax.axis_size("tp")
    weights_in = (
        lax.all_gather(w_query, ("dp", "seq"), axis=0, tiled=True),
        lax.all_gather(w_key, ("dp", "seq"), axis=0, tiled=True),
        lax.all_gather(w_value, ("dp", "seq"), axis=0, tiled=True),
        lax.all_gather(w_out, ("dp", "seq"), axis=1, tiled=True),
        lax.all_gather(w_gate, ("dp", "seq"), axis=0, tiled=True),
        lax.all_gather(w_up, ("dp", "seq"), axis=0, tiled=True),
        lax.all_gather(w_down, ("dp", "seq"), axis=1, tiled=True),
        lax.all_gather(q_gain, ("dp", "seq"), axis=1, tiled=True),
        lax.all_gather(k_gain, ("dp", "seq"), axis=1, tiled=True),
        lax.all_gather(attn_gain, ("dp", "seq"), axis=1, tiled=True),
        lax.all_gather(mlp_gain, ("dp", "seq"), axis=1, tiled=True),
    )
    (
        full_query,
        full_key,
        full_value,
        full_out,
        full_gate,
        full_up,
        full_down,
        full_qgain,
        full_kgain,
        full_again,
        full_mgain,
    ) = weights_in
    local_heads = full_qgain.shape[0]
    head_dim = full_qgain.shape[1]
    head_span = local_heads * head_dim
    score_scale = head_dim ** (-0.5)
    query_gain = full_qgain.astype(jnp.float32).reshape(head_span)
    key_gain = full_kgain.astype(jnp.float32).reshape(head_span)
    attn_scale_gain = full_again.astype(jnp.float32).reshape(d_model)
    mlp_scale_gain = full_mgain.astype(jnp.float32).reshape(d_model)
    query_raw = project(tokens, full_query)
    key_raw = project(tokens, full_key)
    value_raw = project(tokens, full_value)
    query_sq, key_sq = lax.psum(
        (jnp.sum(query_raw * query_raw, axis=-1), jnp.sum(key_raw * key_raw, axis=-1)), "tp"
    )
    query_inv = lax.rsqrt(query_sq / d_model + NORM_EPS)[..., None]
    key_inv = lax.rsqrt(key_sq / d_model + NORM_EPS)[..., None]
    query_unit = query_raw * query_inv
    key_unit = key_raw * key_inv
    positions = seq_rank * local_len + jnp.arange(local_len, dtype=jnp.int32)
    cosines, sines = rope_tables(positions, head_dim)
    heads_shape = (seq_count, local_len, local_heads, head_dim)
    queries = rotate((query_unit * query_gain).reshape(heads_shape), cosines, sines).astype(
        jnp.bfloat16
    )
    keys_local = (
        rotate((key_unit * key_gain).reshape(heads_shape), cosines, sines)
        .astype(jnp.bfloat16)
        .reshape(seq_count, local_len, head_span)
    )
    values_local = value_raw.astype(jnp.bfloat16)
    all_keys, all_values = (
        lax.all_gather(keys_local, "seq", axis=1, tiled=True),
        lax.all_gather(values_local, "seq", axis=1, tiled=True),
    )
    length = all_keys.shape[1]
    keys_full = all_keys.reshape(seq_count, length, local_heads, head_dim)
    values_full = all_values.reshape(seq_count, length, local_heads, head_dim)
    key_rows = min(512, length)
    block_ids = jnp.arange(length // key_rows, dtype=jnp.int32)

    def key_block(block_index):
        first_key = block_index * key_rows
        key_part = lax.dynamic_slice_in_dim(keys_full, first_key, key_rows, 1)
        value_part = lax.dynamic_slice_in_dim(values_full, first_key, key_rows, 1)
        scores = (
            jnp.einsum("mqhd,mkhd->mhqk", queries, key_part, preferred_element_type=jnp.float32)
            * score_scale
        )
        allowed = (first_key + jnp.arange(key_rows, dtype=jnp.int32))[None, :] <= positions[:, None]
        return (key_part, value_part, jnp.where(allowed, scores, MASKED), allowed)

    def max_step(state, block_index):
        running_max, running_sum = state
        key_part, value_part, scores, allowed = key_block(block_index)
        new_max = jnp.maximum(running_max, jnp.max(scores, axis=-1))
        weights_now = jnp.where(allowed, jnp.exp(scores - new_max[..., None]), 0.0)
        return (
            (new_max, running_sum * jnp.exp(running_max - new_max) + jnp.sum(weights_now, axis=-1)),
            None,
        )

    stat_shape = (seq_count, local_heads, local_len)
    final_state, unused = lax.scan(
        max_step,
        (jnp.full(stat_shape, MASKED, jnp.float32), jnp.zeros(stat_shape, jnp.float32)),
        block_ids,
    )
    log_total = (final_state[0] + jnp.log(final_state[1]))[..., None]

    def context_step(context, block_index):
        key_part, value_part, scores, allowed = key_block(block_index)
        probs = jnp.where(allowed, jnp.exp(scores - log_total), 0.0).astype(jnp.bfloat16)
        return (
            context
            + jnp.einsum("mhqk,mkhd->mqhd", probs, value_part, preferred_element_type=jnp.float32),
            None,
        )

    context, unused = lax.scan(context_step, jnp.zeros(heads_shape, jnp.float32), block_ids)
    context_low = context.astype(jnp.bfloat16).reshape(seq_count, local_len, head_span)
    attn_out = lax.psum_scatter(
        project(context_low, full_out), "tp", scatter_dimension=1, tiled=True
    )
    attn_inv = lax.rsqrt(jnp.mean(attn_out * attn_out, axis=-1, keepdims=True) + NORM_EPS)
    attn_unit = attn_out * attn_inv
    own_tokens = lax.dynamic_slice_in_dim(tokens, tp_rank * own_rows, own_rows, 1).astype(
        jnp.float32
    )
    hidden = own_tokens + attn_unit * attn_scale_gain
    hidden_all = lax.all_gather(hidden.astype(jnp.bfloat16), "tp", axis=1, tiled=True)
    gate_act = project(hidden_all, full_gate)
    up_act = project(hidden_all, full_up)
    gate_sig = jax.nn.sigmoid(gate_act)
    mixed = (gate_act * gate_sig * up_act).astype(jnp.bfloat16)
    mlp_out = lax.psum_scatter(project(mixed, full_down), "tp", scatter_dimension=1, tiled=True)
    mlp_inv = lax.rsqrt(jnp.mean(mlp_out * mlp_out, axis=-1, keepdims=True) + NORM_EPS)
    mlp_unit = mlp_out * mlp_inv
    outputs = (hidden + mlp_unit * mlp_scale_gain).astype(jnp.bfloat16)
    weights_back = (
        lax.all_gather(w_query, ("dp", "seq"), axis=0, tiled=True),
        lax.all_gather(w_key, ("dp", "seq"), axis=0, tiled=True),
        lax.all_gather(w_value, ("dp", "seq"), axis=0, tiled=True),
        lax.all_gather(w_out, ("dp", "seq"), axis=1, tiled=True),
        lax.all_gather(w_gate, ("dp", "seq"), axis=0, tiled=True),
        lax.all_gather(w_up, ("dp", "seq"), axis=0, tiled=True),
        lax.all_gather(w_down, ("dp", "seq"), axis=1, tiled=True),
    )
    back_query, back_key, back_value, back_out, back_gate, back_up, back_down = weights_back
    grad_out = cotangent.astype(jnp.float32)
    grad_mgain = jnp.sum(grad_out * mlp_unit, axis=(0, 1))
    mlp_scaled = grad_out * mlp_scale_gain
    grad_mlp = norm_back(
        mlp_unit, mlp_scaled, mlp_inv, jnp.sum(mlp_scaled * mlp_unit, axis=-1), d_model
    ).astype(jnp.bfloat16)
    grad_mlp_all = lax.all_gather(grad_mlp, "tp", axis=1, tiled=True)
    grad_wdown = outer_sum(mixed, grad_mlp_all)
    grad_mixed = project_back(grad_mlp_all, back_down)
    grad_gate = (grad_mixed * up_act * gate_sig * (1.0 + gate_act * (1.0 - gate_sig))).astype(
        jnp.bfloat16
    )
    grad_up = (grad_mixed * gate_act * gate_sig).astype(jnp.bfloat16)
    grad_wgate = outer_sum(hidden_all, grad_gate)
    grad_wup = outer_sum(hidden_all, grad_up)
    hidden_part = project_back(grad_gate, back_gate) + project_back(grad_up, back_up)
    hidden_sum, grad_mgain_part = (
        lax.psum_scatter(hidden_part, "tp", scatter_dimension=1, tiled=True),
        lax.psum_scatter(grad_mgain.reshape(-1, head_dim), "tp", scatter_dimension=0, tiled=True),
    )
    grad_hidden = grad_out + hidden_sum
    grad_again = jnp.sum(grad_hidden * attn_unit, axis=(0, 1))
    attn_scaled = grad_hidden * attn_scale_gain
    grad_attn = norm_back(
        attn_unit, attn_scaled, attn_inv, jnp.sum(attn_scaled * attn_unit, axis=-1), d_model
    ).astype(jnp.bfloat16)
    grad_attn_all = lax.all_gather(grad_attn, "tp", axis=1, tiled=True)
    grad_wout = outer_sum(context_low, grad_attn_all)
    grad_context = project_back(grad_attn_all, back_out).astype(jnp.bfloat16).reshape(heads_shape)

    def delta_step(delta, block_index):
        key_part, value_part, scores, allowed = key_block(block_index)
        probs = jnp.exp(scores - log_total)
        grad_probs = jnp.einsum(
            "mqhd,mkhd->mhqk", grad_context, value_part, preferred_element_type=jnp.float32
        )
        return (delta + jnp.sum(probs * grad_probs, axis=-1), None)

    delta, unused = lax.scan(delta_step, jnp.zeros(stat_shape, jnp.float32), block_ids)

    def score_grads(block_index):
        key_part, value_part, scores, allowed = key_block(block_index)
        probs = jnp.exp(scores - log_total)
        grad_probs = jnp.einsum(
            "mqhd,mkhd->mhqk", grad_context, value_part, preferred_element_type=jnp.float32
        )
        grad_scores = (probs * (grad_probs - delta[..., None])).astype(jnp.bfloat16)
        return (key_part, probs, grad_scores)

    def grad_step(grad_queries, block_index):
        key_part, probs, grad_scores = score_grads(block_index)
        grad_queries = grad_queries + jnp.einsum(
            "mhqk,mkhd->mqhd", grad_scores, key_part, preferred_element_type=jnp.float32
        )
        grad_keys = (
            jnp.einsum("mhqk,mqhd->kmhd", grad_scores, queries, preferred_element_type=jnp.float32)
            * score_scale
        )
        grad_values = jnp.einsum(
            "mhqk,mqhd->kmhd",
            probs.astype(jnp.bfloat16),
            grad_context,
            preferred_element_type=jnp.float32,
        )
        both_terms = jnp.concatenate(
            [
                grad_keys.reshape(key_rows, seq_count, head_span),
                grad_values.reshape(key_rows, seq_count, head_span),
            ],
            axis=-1,
        )
        return (grad_queries, both_terms)

    grad_queries, key_terms = lax.scan(grad_step, jnp.zeros(heads_shape, jnp.float32), block_ids)
    key_value_grads = lax.psum_scatter(
        key_terms.reshape(length, seq_count, 2 * head_span).astype(jnp.bfloat16),
        "seq",
        scatter_dimension=0,
        tiled=True,
    ).astype(jnp.float32)
    key_value_grads = jnp.transpose(key_value_grads, (1, 0, 2))
    grad_keys_own = key_value_grads[..., :head_span].reshape(heads_shape)
    grad_values_own = key_value_grads[..., head_span:].astype(jnp.bfloat16)
    query_grad_unit = unrotate(grad_queries * score_scale, cosines, sines).reshape(
        seq_count, local_len, head_span
    )
    key_grad_unit = unrotate(grad_keys_own, cosines, sines).reshape(seq_count, local_len, head_span)
    grad_qgain = jnp.sum(query_grad_unit * query_unit, axis=(0, 1))
    grad_kgain = jnp.sum(key_grad_unit * key_unit, axis=(0, 1))
    query_scaled = query_grad_unit * query_gain
    key_scaled = key_grad_unit * key_gain
    query_dot, key_dot = lax.psum(
        (jnp.sum(query_scaled * query_unit, axis=-1), jnp.sum(key_scaled * key_unit, axis=-1)), "tp"
    )
    grad_qraw = norm_back(query_unit, query_scaled, query_inv, query_dot, d_model).astype(
        jnp.bfloat16
    )
    grad_kraw = norm_back(key_unit, key_scaled, key_inv, key_dot, d_model).astype(jnp.bfloat16)
    grad_wquery = outer_sum(tokens, grad_qraw)
    grad_wkey = outer_sum(tokens, grad_kraw)
    grad_wvalue = outer_sum(tokens, grad_values_own)
    token_part = (
        project_back(grad_qraw, back_query)
        + project_back(grad_kraw, back_key)
        + project_back(grad_values_own, back_value)
    )
    token_sum, grad_again_part = (
        lax.psum_scatter(
            token_part.astype(jnp.bfloat16), "tp", scatter_dimension=1, tiled=True
        ).astype(jnp.float32),
        lax.psum_scatter(
            grad_again.reshape(-1, head_dim).astype(jnp.bfloat16),
            "tp",
            scatter_dimension=0,
            tiled=True,
        ).astype(jnp.float32),
    )
    grad_tokens = grad_hidden + token_sum
    summed = (
        lax.psum_scatter(
            grad_wquery.astype(jnp.bfloat16), ("dp", "seq"), scatter_dimension=0, tiled=True
        ).astype(jnp.float32),
        lax.psum_scatter(
            grad_wkey.astype(jnp.bfloat16), ("dp", "seq"), scatter_dimension=0, tiled=True
        ).astype(jnp.float32),
        lax.psum_scatter(
            grad_wvalue.astype(jnp.bfloat16), ("dp", "seq"), scatter_dimension=0, tiled=True
        ).astype(jnp.float32),
        lax.psum_scatter(
            grad_wout.astype(jnp.bfloat16), ("dp", "seq"), scatter_dimension=1, tiled=True
        ).astype(jnp.float32),
        lax.psum_scatter(
            grad_wgate.astype(jnp.bfloat16), ("dp", "seq"), scatter_dimension=0, tiled=True
        ).astype(jnp.float32),
        lax.psum_scatter(
            grad_wup.astype(jnp.bfloat16), ("dp", "seq"), scatter_dimension=0, tiled=True
        ).astype(jnp.float32),
        lax.psum_scatter(
            grad_wdown.astype(jnp.bfloat16), ("dp", "seq"), scatter_dimension=1, tiled=True
        ).astype(jnp.float32),
        lax.psum_scatter(
            grad_qgain.reshape(local_heads, head_dim).astype(jnp.bfloat16),
            ("dp", "seq"),
            scatter_dimension=1,
            tiled=True,
        ).astype(jnp.float32),
        lax.psum_scatter(
            grad_kgain.reshape(local_heads, head_dim).astype(jnp.bfloat16),
            ("dp", "seq"),
            scatter_dimension=1,
            tiled=True,
        ).astype(jnp.float32),
        lax.psum_scatter(
            grad_again_part.astype(jnp.bfloat16), ("dp", "seq"), scatter_dimension=1, tiled=True
        ).astype(jnp.float32),
        lax.psum_scatter(
            grad_mgain_part.astype(jnp.bfloat16), ("dp", "seq"), scatter_dimension=1, tiled=True
        ).astype(jnp.float32),
    )
    (
        sum_query,
        sum_key,
        sum_value,
        sum_out,
        sum_gate,
        sum_up,
        sum_down,
        sum_qgain,
        sum_kgain,
        sum_again,
        sum_mgain,
    ) = summed
    return (
        outputs,
        grad_tokens,
        sum_query,
        sum_key,
        sum_value,
        sum_out,
        sum_gate,
        sum_up,
        sum_down,
        sum_qgain,
        sum_kgain,
        sum_again,
        sum_mgain,
    )


LOW = jnp.bfloat16
VMEM_LIMIT = 50 * 1024 * 1024
PARAMS = pltpu.CompilerParams(vmem_limit_bytes=VMEM_LIMIT)


def to_neighbour(values, flip):
    return lax.ppermute(values, "seq", [(i, i ^ flip) for i in range(4)])


def to_core(values):
    return lax.ppermute(values, "dp", [(0, 1), (1, 0)])


def after(values, done):
    return lax.optimization_barrier((values, done))[0]


def first_step(shard):
    return to_neighbour(shard, 1), to_neighbour(shard, 2)


def gather_plane(shard, firsts, meanwhile=()):
    half = shard.shape[0] // 2
    (from_one, from_two), meanwhile = lax.optimization_barrier((firsts, meanwhile))
    far = [to_neighbour(from_two[:half], 1), to_neighbour(from_one[half:], 2)]
    near = [shard, from_one, from_two]
    far, other = lax.optimization_barrier((far, [to_core(piece) for piece in near]))
    return near + far + other + [to_core(piece) for piece in far], meanwhile


def place_piece(out_ref, order_ref, k, piece, axis):
    block = piece.shape[axis]
    if axis == 0 and k % 5 > 2:
        block *= 2
    first = piece.shape[0] if k % 5 == 4 else 0
    start = order_ref[(k // 5) * 4 + min(k % 5, 3)] * block
    if axis == 0:
        out_ref[pl.ds(pl.multiple_of(start + first, piece.shape[0]), piece.shape[0])] = piece
    else:
        out_ref[first : first + piece.shape[0], pl.ds(pl.multiple_of(start, block), block)] = piece


def assemble_columns(pieces, order):
    height, block = pieces[0].shape

    def body(order_ref, *refs):
        for k in range(10):
            place_piece(refs[10], order_ref, k, refs[k][...], 1)

    return pl.pallas_call(
        body,
        in_specs=[pl.BlockSpec(memory_space=pltpu.SMEM)]
        + [pl.BlockSpec(memory_space=pltpu.VMEM)] * 10,
        out_specs=pl.BlockSpec(memory_space=pltpu.VMEM),
        out_shape=jax.ShapeDtypeStruct((height, 8 * block), pieces[0].dtype),
        compiler_params=PARAMS,
        name="assemble_columns",
    )(order, *pieces)


def project_in(rows_low, pieces, order):
    rows, width = rows_low.shape
    columns = pieces[0].shape[1]
    tile = columns // 3

    def body(order_ref, rows_ref, *refs):
        for k in range(10):
            place_piece(refs[11], order_ref, k, refs[k][...], 0)
        refs[10][...] = jnp.dot(rows_ref[...], refs[11][...], preferred_element_type=jnp.float32)

    return pl.pallas_call(
        body,
        grid_spec=pltpu.PrefetchScalarGridSpec(
            num_scalar_prefetch=1,
            grid=(3,),
            in_specs=[pl.BlockSpec((rows, width), lambda j, o: (0, 0))]
            + [pl.BlockSpec((piece.shape[0], tile), lambda j, o: (0, j)) for piece in pieces],
            out_specs=[
                pl.BlockSpec((rows, tile), lambda j, o: (0, j)),
                pl.BlockSpec((width, tile), lambda j, o: (0, j)),
            ],
        ),
        out_shape=[
            jax.ShapeDtypeStruct((rows, columns), jnp.float32),
            jax.ShapeDtypeStruct((width, columns), LOW),
        ],
        compiler_params=PARAMS,
        name="project_in",
    )(order, rows_low, *pieces)


def grad_blocks(lefts, rights, extra, order, blocks, received=None, far=None):
    rows, d_model = lefts[0].shape
    block = d_model // 8
    half = block // 2
    count = len(blocks)
    width = sum(right.shape[1] for right in rights) + extra.shape[1]
    fresh = received is None

    def body(order_ref, *refs):
        left_refs, right_refs = refs[: len(lefts)], refs[len(lefts) : len(lefts) + len(rights)]
        extra_ref, rest = refs[len(lefts) + len(rights)], refs[len(lefts) + len(rights) + 1 :]
        first = 0
        for k in range(len(lefts) + 1):
            if k < len(lefts):
                total = contract(left_refs[k][...], right_refs[k][...], 0, 0)
            else:
                total = extra_ref[...]
            columns = slice(first, first + total.shape[1])
            first += total.shape[1]
            if fresh:
                rest[0][:, columns] = total.astype(LOW)
                continue
            total = total + rest[0][:, columns].astype(jnp.float32)
            if far is None:
                rest[1][:, columns] = total[:half].astype(LOW)
                rest[2][:, columns] = total[half:].astype(LOW)
                continue
            low, high, outs = rest[1], rest[2], rest[3:]

            @pl.when(pl.program_id(0) == 0)
            def _(total=total, columns=columns):
                outs[0][:half, columns] = total[:half].astype(LOW)
                outs[0][half:, columns] = (
                    total[half:] + high[:, columns].astype(jnp.float32)
                ).astype(LOW)

            @pl.when(pl.program_id(0) == 1)
            def _(total=total, columns=columns):
                outs[1][:half, columns] = (
                    total[:half] + low[:, columns].astype(jnp.float32)
                ).astype(LOW)
                outs[1][half:, columns] = total[half:].astype(LOW)

            @pl.when(pl.program_id(0) == 2)
            def _(total=total, columns=columns):
                outs[2][:, columns] = total.astype(LOW)

    def pick(j):
        value = blocks[0]
        for i, entry in enumerate(blocks[1:]):
            value = jnp.where(j > i, entry, value)
        return value

    def fixed(height):
        return pl.BlockSpec((height, width), lambda j, o: (0, 0))

    in_specs = [pl.BlockSpec((rows, block), lambda j, o: (0, o[pick(j)])) for _ in lefts]
    in_specs += [pl.BlockSpec(right.shape, lambda j, o: (0, 0)) for right in rights]
    in_specs.append(pl.BlockSpec((block, extra.shape[1]), lambda j, o: (o[pick(j)], 0)))
    more = ()
    if fresh:
        out_specs = [pl.BlockSpec((block, width), lambda j, o: (j, 0))]
        out_shape = [jax.ShapeDtypeStruct((count * block, width), LOW)]
    else:
        in_specs.append(pl.BlockSpec((block, width), lambda j, o: (pick(j), 0)))
        more = (received,)
        if far is None:
            out_specs = [fixed(half)] * 2
            out_shape = [jax.ShapeDtypeStruct((half, width), LOW)] * 2
        else:
            more += tuple(far)
            in_specs += [fixed(half)] * 2
            out_specs = [fixed(block)] * 3
            out_shape = [jax.ShapeDtypeStruct((block, width), LOW)] * 3
    return pl.pallas_call(
        body,
        grid_spec=pltpu.PrefetchScalarGridSpec(
            num_scalar_prefetch=1, grid=(count,), in_specs=in_specs, out_specs=out_specs
        ),
        out_shape=out_shape,
        compiler_params=PARAMS,
        name="grad_blocks",
    )(order, *lefts, *rights, extra, *more)


def sum_in_plane(*parts):
    (sent,) = grad_blocks(*parts, (4, 5, 6, 7))
    received = to_core(sent)
    sent = grad_blocks(*parts, (3,), received)
    far = [to_neighbour(sent[0], 1), to_neighbour(sent[1], 2)]
    return sent, grad_blocks(*parts, (1, 2, 0), received, far)


def gather_line(own):
    up, down = own, own
    ups, downs = [], []
    for t in range(1, 4):
        up = lax.ppermute(up, "tp", [(i, i + 1) for i in range(t - 1, 3)])
        down = lax.ppermute(down, "tp", [(i, i - 1) for i in range(1, 5 - t)])
        ups.append(up)
        downs.append(down)
    return [own] + ups + downs


def scatter_line(slots, meanwhile=((), ())):
    meanwhile = list(meanwhile)
    def added(mine, got):
        return (mine.astype(jnp.float32) + got.astype(jnp.float32)).astype(LOW)

    up, down = slots[1], slots[3]
    for t in range(1, 4):
        up = lax.ppermute(up, "tp", [(i, i + 1) for i in range(t)])
        down = lax.ppermute(down, "tp", [(i, i - 1) for i in range(4 - t, 4)])
        if t < 3:
            up, down, meanwhile[t - 1] = lax.optimization_barrier((up, down, meanwhile[t - 1]))
            up = added(slots[t + 1], up)
            down = added(slots[3 - t], down)
    return (slots[0], up, down), meanwhile


def sum_line(values):
    flat = lax.optimization_barrier(values.reshape(-1, 128))
    return lax.optimization_barrier(lax.psum(flat, "tp"))


def contract(left, right, left_dim, right_dim):
    return lax.dot_general(
        left, right, (((left_dim,), (right_dim,)), ((), ())), preferred_element_type=jnp.float32
    )


def turned(values, cosines, sines):
    return values * cosines + pltpu.roll(values, values.shape[-1] // 2, axis=1) * sines


def inverse_norm(squares, d_model):
    return lax.rsqrt(squares * (1.0 / d_model) + NORM_EPS)


def prepare(raw, squares, gains, cosines, sines, heads, head_dim, d_model):
    seqs, length, _ = raw.shape
    own = length // 4
    rows = seqs * own
    span = heads * head_dim

    def body(raw_ref, square_ref, gain_ref, cos_ref, sin_ref, out_ref):
        cosine = jnp.concatenate([cos_ref[...]] * seqs, axis=0)
        sine = jnp.concatenate([sin_ref[...]] * seqs, axis=0)
        for t in range(2):
            inv = inverse_norm(square_ref[t].reshape(rows, 1), d_model)
            for h in range(heads):
                columns = slice(t * span + h * head_dim, t * span + (h + 1) * head_dim)
                normed = raw_ref[:, :, columns].reshape(rows, head_dim) * inv * gain_ref[:, columns]
                out_ref[h, t] = (
                    turned(normed, cosine, sine).astype(LOW).reshape(seqs, own, head_dim)
                )
        for h in range(heads):
            columns = slice(2 * span + h * head_dim, 2 * span + (h + 1) * head_dim)
            out_ref[h, 2] = raw_ref[:, :, columns].astype(LOW)

    return pl.pallas_call(
        body,
        grid=(4,),
        in_specs=[
            pl.BlockSpec((seqs, own, 3 * span), lambda t: (0, t, 0)),
            pl.BlockSpec((2, seqs, own, 1), lambda t: (0, 0, t, 0)),
            pl.BlockSpec((1, 2 * span), lambda t: (0, 0)),
            pl.BlockSpec((own, head_dim), lambda t: (t, 0)),
            pl.BlockSpec((own, head_dim), lambda t: (t, 0)),
        ],
        out_specs=pl.BlockSpec((heads, 3, seqs, own, head_dim), lambda t: (0, 0, 0, t, 0)),
        out_shape=jax.ShapeDtypeStruct((heads, 3, seqs, length, head_dim), LOW),
        compiler_params=PARAMS,
        name="prepare",
    )(raw, squares, gains, cosines, sines)


def scores_of(left, right):
    return lax.dot_general(
        left, right, (((1,), (1,)), ((), ())), preferred_element_type=jnp.float32
    )


def causal(scores, first):
    rows = lax.broadcasted_iota(jnp.int32, scores.shape, 0) + first
    columns = lax.broadcasted_iota(jnp.int32, scores.shape, 1)
    return columns <= rows


def attend(parts):
    blocks, _, seqs, length, head_dim = parts.shape
    score_scale = head_dim ** (-0.5)

    def body(parts_ref, out_ref, log_ref):
        for i in range(blocks):
            span = (i + 1) * length
            keys = parts_ref[: i + 1, 1, 0].reshape(span, head_dim)
            values = parts_ref[: i + 1, 2, 0].reshape(span, head_dim)
            scores = scores_of(parts_ref[i, 0, 0], keys) * score_scale
            scores = jnp.where(causal(scores, i * length), scores, MASKED)
            top = jnp.max(scores, axis=-1, keepdims=True)
            weights = jnp.exp(scores - top)
            total = jnp.sum(weights, axis=-1, keepdims=True)
            probs = (weights * (1.0 / total)).astype(LOW)
            out_ref[i, 0] = jnp.dot(probs, values, preferred_element_type=jnp.float32).astype(LOW)
            log_ref[i, 0] = top + jnp.log(total)

    return pl.pallas_call(
        body,
        grid=(seqs,),
        in_specs=[pl.BlockSpec((blocks, 3, 1, length, head_dim), lambda m: (0, 0, m, 0, 0))],
        out_specs=[
            pl.BlockSpec((blocks, 1, length, head_dim), lambda m: (0, m, 0, 0)),
            pl.BlockSpec((blocks, 1, length, 1), lambda m: (0, m, 0, 0)),
        ],
        out_shape=[
            jax.ShapeDtypeStruct((blocks, seqs, length, head_dim), LOW),
            jax.ShapeDtypeStruct((blocks, seqs, length, 1), jnp.float32),
        ],
        compiler_params=PARAMS,
        name="attend",
    )(parts)


def attend_back(parts, grad_context, log_total):
    blocks, _, seqs, length, head_dim = parts.shape
    score_scale = head_dim ** (-0.5)

    def body(parts_ref, grad_ref, log_ref, out_ref, keys_sum, values_sum):
        keys_sum[...] = jnp.zeros_like(keys_sum)
        values_sum[...] = jnp.zeros_like(values_sum)
        for i in range(blocks):
            span = (i + 1) * length
            queries = parts_ref[i, 0, 0]
            keys = parts_ref[: i + 1, 1, 0].reshape(span, head_dim)
            values = parts_ref[: i + 1, 2, 0].reshape(span, head_dim)
            grads = grad_ref[i, :, 0].reshape(length, head_dim)
            scores = scores_of(queries, keys) * score_scale
            probs = jnp.where(causal(scores, i * length), jnp.exp(scores - log_ref[i, 0]), 0.0)
            grad_probs = scores_of(grads, values)
            delta = jnp.sum(probs * grad_probs, axis=-1, keepdims=True)
            grad_scores = (probs * (grad_probs - delta)).astype(LOW)
            out_ref[i, 0, 0] = (
                jnp.dot(grad_scores, keys, preferred_element_type=jnp.float32) * score_scale
            ).astype(LOW)
            keys_sum[:span] += contract(grad_scores, queries, 0, 0)
            values_sum[:span] += contract(probs.astype(LOW), grads, 0, 0)
        out_ref[:, 1, 0] = (
            (keys_sum[...] * score_scale).astype(LOW).reshape(blocks, length, head_dim)
        )
        out_ref[:, 2, 0] = values_sum[...].astype(LOW).reshape(blocks, length, head_dim)

    whole = pl.BlockSpec((blocks, 3, 1, length, head_dim), lambda m: (0, 0, m, 0, 0))
    return pl.pallas_call(
        body,
        grid=(seqs,),
        in_specs=[
            whole,
            pl.BlockSpec((blocks, 4, 1, length // 4, head_dim), lambda m: (0, 0, m, 0, 0)),
            pl.BlockSpec((blocks, 1, length, 1), lambda m: (0, m, 0, 0)),
        ],
        out_specs=whole,
        out_shape=jax.ShapeDtypeStruct(parts.shape, LOW),
        scratch_shapes=[
            pltpu.VMEM((blocks * length, head_dim), jnp.float32),
            pltpu.VMEM((blocks * length, head_dim), jnp.float32),
        ],
        compiler_params=PARAMS,
        name="attend_back",
    )(parts, grad_context, log_total)


def project_out(context, weights, slots):
    heads, seqs, length, head_dim = context.shape
    span, width = weights.shape
    own = length // 4
    own_rows = seqs * own
    tile = width // 2

    def body(slots_ref, context_ref, weight_ref, rows_ref, *outs):
        @pl.when(pl.program_id(0) == 0)
        def _():
            for t in range(4):
                place = pl.ds(pl.multiple_of(slots_ref[t] * own, own), own)
                for h in range(heads):
                    rows_ref[
                        t * own_rows : (t + 1) * own_rows, h * head_dim : (h + 1) * head_dim
                    ] = context_ref[h, :, place].reshape(own_rows, head_dim)

        product = jnp.dot(rows_ref[...], weight_ref[...], preferred_element_type=jnp.float32)
        for t in range(4):
            outs[t][...] = product[t * own_rows : (t + 1) * own_rows].astype(LOW)

    return pl.pallas_call(
        body,
        grid_spec=pltpu.PrefetchScalarGridSpec(
            num_scalar_prefetch=1,
            grid=(2,),
            in_specs=[
                pl.BlockSpec(context.shape, lambda j, s: (0, 0, 0, 0)),
                pl.BlockSpec((span, tile), lambda j, s: (0, j)),
            ],
            out_specs=[pl.BlockSpec((4 * own_rows, span), lambda j, s: (0, 0))]
            + [pl.BlockSpec((own_rows, tile), lambda j, s: (0, j))] * 4,
        ),
        out_shape=[jax.ShapeDtypeStruct((4 * own_rows, span), LOW)]
        + [jax.ShapeDtypeStruct((own_rows, width), LOW)] * 4,
        compiler_params=PARAMS,
        name="project_out",
    )(slots, context, weights)


def project_out_back(grads, weights, heads, head_dim, seqs):
    rows, width = grads.shape
    own = rows // seqs
    span = heads * head_dim

    def body(grad_ref, weight_ref, out_ref):
        product = jnp.dot(grad_ref[...], weight_ref[...], preferred_element_type=jnp.float32)
        for h in range(heads):
            out_ref[h, 0] = (
                product[:, h * head_dim : (h + 1) * head_dim].astype(LOW).reshape(seqs, own, head_dim)
            )

    return pl.pallas_call(
        body,
        grid=(4,),
        in_specs=[
            pl.BlockSpec((rows, width), lambda j: (0, 0)),
            pl.BlockSpec((width, span), lambda j: (0, j)),
        ],
        out_specs=pl.BlockSpec((heads, 1, seqs, own, head_dim), lambda j: (0, j, 0, 0, 0)),
        out_shape=jax.ShapeDtypeStruct((heads, 4, seqs, own, head_dim), LOW),
        compiler_params=PARAMS,
        name="project_out_back",
    )(grads, weights)


def rows_of(pieces):
    own, width = pieces[0].shape

    def body(*refs):
        fill_slots(refs[7], refs[:7])

    return pl.pallas_call(
        body,
        out_shape=jax.ShapeDtypeStruct((4 * own, width), LOW),
        compiler_params=PARAMS,
        name="rows_of",
    )(*pieces)


def unprepare(grads, raw, squares, gains, cosines, sines, d_model):
    heads, _, seqs, length, head_dim = grads.shape
    own = length // 4
    rows = seqs * own
    span = heads * head_dim

    def body(
        grad_ref, raw_ref, square_ref, gain_ref, cos_ref, sin_ref, scaled_ref, dot_ref, sum_ref
    ):
        cosine = jnp.concatenate([cos_ref[...]] * seqs, axis=0)
        sine = -jnp.concatenate([sin_ref[...]] * seqs, axis=0)

        @pl.when(pl.program_id(0) == 0)
        def _():
            sum_ref[...] = jnp.zeros_like(sum_ref)

        for t in range(2):
            inv = inverse_norm(square_ref[t].reshape(rows, 1), d_model)
            total = jnp.zeros((rows, head_dim), jnp.float32)
            for h in range(heads):
                columns = slice(t * span + h * head_dim, t * span + (h + 1) * head_dim)
                back = turned(
                    grad_ref[h, t].reshape(rows, head_dim).astype(jnp.float32), cosine, sine
                )
                along = back * (raw_ref[:, :, columns].reshape(rows, head_dim) * inv)
                sum_ref[:, columns] += jnp.sum(along, axis=0, keepdims=True)
                scaled_ref[:, :, columns] = (back * gain_ref[:, columns]).reshape(
                    seqs, own, head_dim
                )
                total += along * gain_ref[:, columns]
            dot_ref[t] = jnp.sum(total, axis=-1, keepdims=True).reshape(seqs, own, 1)

    return pl.pallas_call(
        body,
        grid=(4,),
        in_specs=[
            pl.BlockSpec((heads, 3, seqs, own, head_dim), lambda t: (0, 0, 0, t, 0)),
            pl.BlockSpec((seqs, own, 3 * span), lambda t: (0, t, 0)),
            pl.BlockSpec((2, seqs, own, 1), lambda t: (0, 0, t, 0)),
            pl.BlockSpec((1, 2 * span), lambda t: (0, 0)),
            pl.BlockSpec((own, head_dim), lambda t: (t, 0)),
            pl.BlockSpec((own, head_dim), lambda t: (t, 0)),
        ],
        out_specs=[
            pl.BlockSpec((seqs, own, 2 * span), lambda t: (0, t, 0)),
            pl.BlockSpec((2, seqs, own, 1), lambda t: (0, 0, t, 0)),
            pl.BlockSpec((1, 2 * span), lambda t: (0, 0)),
        ],
        out_shape=[
            jax.ShapeDtypeStruct((seqs, length, 2 * span), jnp.float32),
            jax.ShapeDtypeStruct((2, seqs, length, 1), jnp.float32),
            jax.ShapeDtypeStruct((1, 2 * span), jnp.float32),
        ],
        compiler_params=PARAMS,
        name="unprepare",
    )(grads, raw, squares, gains, cosines, sines)


def project_in_back(grads, scaled, raw, squares, dots, weights, slots):
    heads, _, seqs, length, head_dim = grads.shape
    own = length // 4
    own_rows = seqs * own
    rows = seqs * length
    span = heads * head_dim
    d_model = weights.shape[0]
    tile = d_model // 4

    def body(
        slots_ref, grad_ref, scaled_ref, raw_ref, square_ref, dot_ref, weight_ref, rows_ref, *refs
    ):
        outs, product = refs[:4], refs[4]

        @pl.when(pl.program_id(0) == 0)
        def _():
            for k in range(2):
                columns = slice(k * span, (k + 1) * span)
                inv = inverse_norm(square_ref[k].reshape(rows, 1), d_model)
                mean = dot_ref[k].reshape(rows, 1) * (1.0 / d_model)
                unit = raw_ref[:, :, columns].reshape(rows, span) * inv
                rows_ref[:, columns] = (
                    inv * (scaled_ref[:, :, columns].reshape(rows, span) - unit * mean)
                ).astype(LOW)
            for h in range(heads):
                columns = slice(2 * span + h * head_dim, 2 * span + (h + 1) * head_dim)
                rows_ref[:, columns] = grad_ref[h, 0].reshape(rows, head_dim)

        product[...] = scores_of(rows_ref[...], weight_ref[...]).reshape(seqs, length, tile)
        for t in range(4):
            place = pl.ds(pl.multiple_of(slots_ref[t] * own, own), own)
            outs[t][...] = product[:, place].reshape(own_rows, tile).astype(LOW)

    flat = pl.BlockSpec((2, seqs, length, 1), lambda j, s: (0, 0, 0, 0))
    return pl.pallas_call(
        body,
        grid_spec=pltpu.PrefetchScalarGridSpec(
            num_scalar_prefetch=1,
            grid=(4,),
            in_specs=[
                pl.BlockSpec((heads, 1, seqs, length, head_dim), lambda j, s: (0, 2, 0, 0, 0)),
                pl.BlockSpec((seqs, length, 2 * span), lambda j, s: (0, 0, 0)),
                pl.BlockSpec((seqs, length, 2 * span), lambda j, s: (0, 0, 0)),
                flat,
                flat,
                pl.BlockSpec((tile, 3 * span), lambda j, s: (j, 0)),
            ],
            out_specs=[pl.BlockSpec((rows, 3 * span), lambda j, s: (0, 0))]
            + [pl.BlockSpec((own_rows, tile), lambda j, s: (0, j))] * 4,
            scratch_shapes=[pltpu.VMEM((seqs, length, tile), jnp.float32)],
        ),
        out_shape=[jax.ShapeDtypeStruct((rows, 3 * span), LOW)]
        + [jax.ShapeDtypeStruct((own_rows, d_model), LOW)] * 4,
        compiler_params=PARAMS,
        name="project_in_back",
    )(slots, grads, scaled, raw, squares, dots, weights)


def fill_slots(rows_ref, refs):
    own = refs[0].shape[0]
    seqs = len(refs) // 7
    for m in range(seqs):
        mine = refs[7 * m : 7 * m + 7]
        rows_ref[m * own : (m + 1) * own] = mine[0][...]
        for t in range(1, 4):
            first = (t * seqs + m) * own
            rows_ref[first : first + own] = mine[t][...] + mine[7 - t][...]


def attn_norm(parts, tokens, gains):
    rows, width = tokens.shape

    def body(own_ref, up_ref, down_ref, token_ref, gain_ref, hidden_ref, low_ref, unit_ref, inv_ref):
        total = (
            own_ref[...].astype(jnp.float32)
            + up_ref[...].astype(jnp.float32)
            + down_ref[...].astype(jnp.float32)
        )
        inv = lax.rsqrt(jnp.mean(total * total, axis=-1, keepdims=True) + NORM_EPS)
        unit = total * inv
        hidden = token_ref[...].astype(jnp.float32) + unit * gain_ref[...]
        hidden_ref[...] = hidden
        low_ref[...] = hidden.astype(LOW)
        unit_ref[...] = unit
        inv_ref[...] = inv

    full = jax.ShapeDtypeStruct((rows, width), jnp.float32)
    return pl.pallas_call(
        body,
        out_shape=[
            full,
            jax.ShapeDtypeStruct((rows, width), LOW),
            full,
            jax.ShapeDtypeStruct((rows, 1), jnp.float32),
        ],
        compiler_params=PARAMS,
        name="attn_norm",
    )(*parts, tokens, gains)


def mlp_norm(parts, hidden, cotangent, gains):
    rows, width = hidden.shape

    def body(own_ref, up_ref, down_ref, hidden_ref, grad_ref, gain_ref, out_ref, back_ref, sum_ref):
        total = (
            own_ref[...].astype(jnp.float32)
            + up_ref[...].astype(jnp.float32)
            + down_ref[...].astype(jnp.float32)
        )
        inv = lax.rsqrt(jnp.mean(total * total, axis=-1, keepdims=True) + NORM_EPS)
        unit = total * inv
        out_ref[...] = (hidden_ref[...] + unit * gain_ref[...]).astype(LOW)
        grad = grad_ref[...].astype(jnp.float32)
        sum_ref[...] = jnp.sum(grad * unit, axis=0, keepdims=True)
        scaled = grad * gain_ref[...]
        mean = jnp.mean(scaled * unit, axis=-1, keepdims=True)
        back_ref[...] = (inv * (scaled - unit * mean)).astype(LOW)

    return pl.pallas_call(
        body,
        out_shape=[jax.ShapeDtypeStruct((rows, width), LOW)] * 2
        + [jax.ShapeDtypeStruct((1, width), jnp.float32)],
        compiler_params=PARAMS,
        name="mlp_norm",
    )(*parts, hidden, cotangent, gains)


def attn_norm_back(parts, cotangent, unit, inv, gains):
    rows, width = unit.shape

    def body(
        own_ref, up_ref, down_ref, grad_ref, unit_ref, inv_ref, gain_ref, hidden_ref, back_ref, sum_ref
    ):
        grad = (
            grad_ref[...].astype(jnp.float32)
            + own_ref[...].astype(jnp.float32)
            + up_ref[...].astype(jnp.float32)
            + down_ref[...].astype(jnp.float32)
        )
        hidden_ref[...] = grad
        unit = unit_ref[...]
        sum_ref[...] = jnp.sum(grad * unit, axis=0, keepdims=True)
        scaled = grad * gain_ref[...]
        mean = jnp.mean(scaled * unit, axis=-1, keepdims=True)
        back_ref[...] = (inv_ref[...] * (scaled - unit * mean)).astype(LOW)

    return pl.pallas_call(
        body,
        out_shape=[
            jax.ShapeDtypeStruct((rows, width), jnp.float32),
            jax.ShapeDtypeStruct((rows, width), LOW),
            jax.ShapeDtypeStruct((1, width), jnp.float32),
        ],
        compiler_params=PARAMS,
        name="attn_norm_back",
    )(*parts, cotangent, unit, inv, gains)


def ff_totals(gate_up, down):
    height, units = down.shape
    steps = 4

    def body(gate_ref, up_ref, down_ref, gate_out, up_out, down_out):
        gate_out[...] = gate_ref[...].astype(jnp.float32)
        up_out[...] = up_ref[...].astype(jnp.float32)
        down_out[...] = down_ref[...].astype(jnp.float32).T

    tile = units // steps
    return pl.pallas_call(
        body,
        grid=(steps,),
        in_specs=[
            pl.BlockSpec((height, tile), lambda j: (0, j)),
            pl.BlockSpec((height, tile), lambda j: (0, steps + j)),
            pl.BlockSpec((height, tile), lambda j: (0, j)),
        ],
        out_specs=[pl.BlockSpec((height, tile), lambda j: (0, j))] * 2
        + [pl.BlockSpec((tile, height), lambda j: (j, 0))],
        out_shape=[jax.ShapeDtypeStruct((height, units), jnp.float32)] * 2
        + [jax.ShapeDtypeStruct((units, height), jnp.float32)],
        compiler_params=PARAMS,
        name="ff_totals",
    )(gate_up, gate_up, down)


def plane_totals(sums, span):
    height, width = sums[0].shape
    more = width - 4 * span

    def body(*refs):
        outs = refs[3:]
        for k in range(5):
            columns = slice(k * span, min((k + 1) * span, width))
            total = (
                refs[0][:, columns].astype(jnp.float32)
                + refs[1][:, columns].astype(jnp.float32)
                + refs[2][:, columns].astype(jnp.float32)
            )
            outs[k][...] = total.T if k == 3 else total

    return pl.pallas_call(
        body,
        out_shape=[jax.ShapeDtypeStruct((height, span), jnp.float32)] * 3
        + [
            jax.ShapeDtypeStruct((span, height), jnp.float32),
            jax.ShapeDtypeStruct((height, more), jnp.float32),
        ],
        compiler_params=PARAMS,
        name="plane_totals",
    )(*sums)


def weight_tiles(width, tile, tiles):
    return [pl.BlockSpec((width, tile), lambda j, k=k: (0, k * tiles + j)) for k in range(3)]


def feed_forward(pieces, weights):
    count = len(pieces)
    own, width = pieces[0].shape
    hidden_units = weights.shape[1] // 3
    tile = 512
    tiles = hidden_units // tile
    parts = 4 * count // 7
    rows = parts * own

    def body(*refs):
        ins, (gate_w, up_w, down_w) = refs[:count], refs[count : count + 3]
        rows_ref, gate_ref, up_ref, mixed_ref, *outs = refs[count + 3 : -1]
        total = refs[-1]

        @pl.when(pl.program_id(0) == 0)
        def _():
            fill_slots(rows_ref, ins)

        gate = jnp.dot(rows_ref[...], gate_w[...], preferred_element_type=jnp.float32)
        up = jnp.dot(rows_ref[...], up_w[...], preferred_element_type=jnp.float32)
        mixed = (gate * jax.nn.sigmoid(gate) * up).astype(LOW)
        gate_ref[...] = gate.astype(LOW)
        up_ref[...] = up.astype(LOW)
        mixed_ref[...] = mixed
        part = scores_of(mixed, down_w[...])

        @pl.when(pl.program_id(0) == 0)
        def _():
            total[...] = part

        @pl.when((pl.program_id(0) > 0) & (pl.program_id(0) < tiles - 1))
        def _():
            total[...] += part

        @pl.when(pl.program_id(0) == tiles - 1)
        def _():
            for t in range(parts):
                mine = slice(t * own, (t + 1) * own)
                outs[t][...] = (total[mine] + part[mine]).astype(LOW)

    fixed = pl.BlockSpec((own, width), lambda j: (0, 0))
    by_tile = pl.BlockSpec((rows, tile), lambda j: (0, j))
    return pl.pallas_call(
        body,
        grid=(tiles,),
        in_specs=[fixed] * count + weight_tiles(width, tile, tiles),
        out_specs=[pl.BlockSpec((rows, width), lambda j: (0, 0))] + [by_tile] * 3 + [fixed] * parts,
        out_shape=[jax.ShapeDtypeStruct((rows, width), LOW)]
        + [jax.ShapeDtypeStruct((rows, hidden_units), LOW)] * 3
        + [jax.ShapeDtypeStruct((own, width), LOW)] * parts,
        scratch_shapes=[pltpu.VMEM((rows, width), jnp.float32)],
        compiler_params=PARAMS,
        name="feed_forward",
    )(*pieces, weights, weights, weights)


def feed_forward_back(rows_low, gate, up, weights, parts):
    rows, width = rows_low.shape
    own = rows // parts
    hidden_units = gate.shape[1]
    tile = 512
    tiles = hidden_units // tile

    def body(rows_ref, gate_ref, up_ref, gate_w, up_w, down_w, grad_gate_ref, grad_up_ref, *refs):
        outs, total = refs[:parts], refs[parts]
        grad_mixed = jnp.dot(rows_ref[...], down_w[...], preferred_element_type=jnp.float32)
        gate = gate_ref[...].astype(jnp.float32)
        up = up_ref[...].astype(jnp.float32)
        sig = jax.nn.sigmoid(gate)
        grad_gate = (grad_mixed * up * sig * (1.0 + gate * (1.0 - sig))).astype(LOW)
        grad_up = (grad_mixed * gate * sig).astype(LOW)
        grad_gate_ref[...] = grad_gate
        grad_up_ref[...] = grad_up
        part = scores_of(grad_gate, gate_w[...]) + scores_of(grad_up, up_w[...])

        @pl.when(pl.program_id(0) == 0)
        def _():
            total[...] = part

        @pl.when((pl.program_id(0) > 0) & (pl.program_id(0) < tiles - 1))
        def _():
            total[...] += part

        @pl.when(pl.program_id(0) == tiles - 1)
        def _():
            for t in range(parts):
                mine = slice(t * own, (t + 1) * own)
                outs[t][...] = (total[mine] + part[mine]).astype(LOW)

    fixed = pl.BlockSpec((own, width), lambda j: (0, 0))
    by_tile = pl.BlockSpec((rows, tile), lambda j: (0, j))
    return pl.pallas_call(
        body,
        grid=(tiles,),
        in_specs=[pl.BlockSpec((rows, width), lambda j: (0, 0))]
        + [by_tile] * 2
        + weight_tiles(width, tile, tiles),
        out_specs=[by_tile] * 2 + [fixed] * parts,
        out_shape=[jax.ShapeDtypeStruct((rows, hidden_units), LOW)] * 2
        + [jax.ShapeDtypeStruct((own, width), LOW)] * parts,
        scratch_shapes=[pltpu.VMEM((rows, width), jnp.float32)],
        compiler_params=PARAMS,
        name="feed_forward_back",
    )(rows_low, gate, up, weights, weights, weights)


def down_grad(pieces, mixed):
    count = len(pieces)
    own, width = pieces[0].shape
    rows, columns = mixed.shape
    tile = 512

    def body(*refs):
        rows_ref, out_ref = refs[count + 1], refs[count + 2]

        @pl.when(pl.program_id(0) == 0)
        def _():
            fill_slots(rows_ref, refs[:count])

        place = pl.ds(pl.multiple_of(pl.program_id(0) * tile, tile), tile)
        out_ref[...] = contract(rows_ref[:, place], refs[count][...], 0, 0).astype(LOW)

    return pl.pallas_call(
        body,
        grid=(width // tile,),
        in_specs=[pl.BlockSpec((own, width), lambda j: (0, 0))] * count
        + [pl.BlockSpec((rows, columns), lambda j: (0, 0))],
        out_specs=[
            pl.BlockSpec((rows, width), lambda j: (0, 0)),
            pl.BlockSpec((tile, columns), lambda j: (j, 0)),
        ],
        out_shape=[
            jax.ShapeDtypeStruct((rows, width), LOW),
            jax.ShapeDtypeStruct((width, columns), LOW),
        ],
        compiler_params=PARAMS,
        name="down_grad",
    )(*pieces, mixed)


def weight_grad(left, right, all_columns, place, others=None):
    rows, width = left.shape
    columns = right.shape[1]
    tile = 512

    def body(left_ref, right_ref, *refs):
        refs[-1][...] = contract(left_ref[...], right_ref[...], 0, 0).astype(LOW)

    given = () if others is None else (others,)
    return pl.pallas_call(
        body,
        grid=(width // tile,),
        in_specs=[
            pl.BlockSpec((rows, tile), lambda j: (0, j)),
            pl.BlockSpec((rows, columns), lambda j: (0, 0)),
        ]
        + [pl.BlockSpec(memory_space=pl.ANY)] * len(given),
        out_specs=pl.BlockSpec((tile, columns), lambda j: (j, place)),
        out_shape=jax.ShapeDtypeStruct((width, all_columns), LOW),
        input_output_aliases={2: 0} if given else {},
        compiler_params=PARAMS,
        name="weight_grad",
    )(left, right, *given)


def on_plane(
    tokens,
    w_query,
    w_key,
    w_value,
    w_out,
    w_gate,
    w_up,
    w_down,
    q_gain,
    k_gain,
    attn_gain,
    mlp_gain,
    cotangent,
):
    seqs, length, d_model = tokens.shape
    rows = seqs * length
    tp_rank = lax.axis_index("tp")
    seq_rank = lax.axis_index("seq")
    heads = q_gain.shape[0]
    head_dim = q_gain.shape[1] * 8
    head_span = heads * head_dim
    own_length = length // 4
    own_rows = seqs * own_length
    order = (lax.axis_index("dp") * 4 + seq_rank) ^ jnp.arange(8, dtype=jnp.int32)
    slots = (tp_rank + 4 - jnp.arange(4, dtype=jnp.int32)) % 4

    gain_rows = jnp.concatenate([q_gain, k_gain, attn_gain, mlp_gain], axis=0)
    all_gains = lax.all_to_all(
        jnp.broadcast_to(gain_rows.reshape(1, -1), (8, gain_rows.size)), ("dp", "seq"), 0, 0, tiled=True
    )
    packed = jnp.concatenate([w_gate, w_up, w_down.T], axis=1)
    in_shard = jnp.concatenate([w_query, w_key, w_value], axis=1)
    in_pieces, (all_gains, packed) = gather_plane(
        in_shard, first_step(in_shard), (all_gains, packed)
    )
    all_gains = (
        jnp.transpose(all_gains.reshape((8,) + gain_rows.shape), (1, 0, 2))
        .reshape(gain_rows.shape[0], head_dim)
        .astype(jnp.float32)
    )
    qk_gain = all_gains[: 2 * heads].reshape(1, 2 * head_span)
    feature_rows = d_model // head_dim
    attn_gains = all_gains[2 * heads : 2 * heads + feature_rows].reshape(1, d_model)
    mlp_gains = all_gains[2 * heads + feature_rows :].reshape(1, d_model)
    positions = seq_rank * length + jnp.arange(length, dtype=jnp.int32)
    cosines, sines = rope_tables(positions, head_dim)
    cosines = jnp.concatenate([cosines[:, 0], cosines[:, 0]], axis=-1)
    sines = jnp.concatenate([-sines[:, 0], sines[:, 0]], axis=-1)
    own_tokens = lax.dynamic_slice_in_dim(tokens, tp_rank * own_length, own_length, 1).reshape(
        own_rows, d_model
    )
    grad_out = cotangent.reshape(own_rows, d_model)
    out_rows = lax.all_gather(w_out, "tp", axis=0, tiled=True)

    raw, in_weights = project_in(tokens.reshape(rows, d_model), in_pieces, order)
    out_firsts = first_step(after(w_out, in_pieces[3:5]))
    weights = lax.all_gather(after(packed, (in_pieces[3:5], out_rows)), ("dp", "seq"), axis=0, tiled=True)

    squares = jnp.stack(
        [
            jnp.sum(jnp.square(raw[:, :head_span]), axis=-1),
            jnp.sum(jnp.square(raw[:, head_span : 2 * head_span]), axis=-1),
        ]
    )
    squares, out_firsts = lax.optimization_barrier((sum_line(squares), out_firsts))
    squares = squares.reshape(2, seqs, length, 1)
    out_pieces, _ = gather_plane(w_out, out_firsts)
    raw = raw.reshape(seqs, length, 3 * head_span)
    parts = prepare(raw, squares, qk_gain, cosines, sines, heads, head_dim, d_model)
    parts, out_pieces[3:5] = lax.optimization_barrier((parts, out_pieces[3:5]))
    parts = lax.all_to_all(parts, "seq", 0, 0, tiled=True)
    parts, out_pieces = lax.optimization_barrier((parts, out_pieces))
    out_weights = assemble_columns(out_pieces, order)
    context, log_total = attend(parts)
    context = lax.all_to_all(context, "seq", 0, 0, tiled=True)
    context_rows, *attn_slots = project_out(context, out_weights, slots)
    hidden, hidden_low, attn_unit, attn_inv = attn_norm(
        scatter_line(attn_slots)[0], own_tokens, attn_gains
    )
    out_columns = after(out_rows, hidden_low).T
    out_columns = lax.all_gather(out_columns, ("dp", "seq"), axis=0, tiled=True)
    hidden_rows, gate, up, mixed, *mlp_slots = feed_forward(gather_line(hidden_low), weights)
    outputs, grad_mlp, grad_mgain = mlp_norm(
        scatter_line(mlp_slots)[0], hidden, grad_out, mlp_gains
    )
    grad_mlp, out_columns = lax.optimization_barrier((grad_mlp, out_columns))
    grad_mlp_rows, down_part = down_grad(gather_line(grad_mlp), mixed)
    grad_gate, grad_up, *hidden_slots = feed_forward_back(grad_mlp_rows, gate, up, weights, 4)
    units = mixed.shape[1]
    gate_part = weight_grad(hidden_rows, grad_gate, 2 * units, 0)
    gate_up_part = weight_grad(hidden_rows, grad_up, 2 * units, 1, gate_part)
    hidden_sum, (gate_part, gate_up_part) = scatter_line(hidden_slots, (gate_part, gate_up_part))

    def sum_plane(part):
        return lax.optimization_barrier(
            lax.psum_scatter(part, ("dp", "seq"), scatter_dimension=0, tiled=True)
        )

    down_sum = sum_plane(down_part)
    gate_up_sum = sum_plane(gate_up_part)
    ff_sums = ff_totals(gate_up_sum, down_sum)

    grad_hidden, grad_attn, grad_again = attn_norm_back(
        hidden_sum, grad_out, attn_unit, attn_inv, attn_gains
    )
    grad_context = project_out_back(grad_attn, out_columns, heads, head_dim, seqs)
    grad_context = lax.all_to_all(
        grad_context.reshape((16,) + grad_context.shape[2:]), ("seq", "tp"), 0, 0, tiled=True
    ).reshape(grad_context.shape)
    part_grads = attend_back(parts, grad_context, log_total)
    part_grads = lax.all_to_all(part_grads, "seq", 0, 0, tiled=True)
    grad_attn_rows = rows_of(gather_line(grad_attn))
    own_gains = lax.all_to_all(
        jnp.concatenate([grad_again.reshape(4, 4, -1), grad_mgain.reshape(4, 4, -1)], axis=1),
        "tp",
        0,
        0,
        tiled=True,
    )
    part_grads, grad_attn_rows, own_gains = lax.optimization_barrier(
        (part_grads, grad_attn_rows, own_gains)
    )
    own_gains = jnp.sum(own_gains, axis=0)
    scaled, dots, qk_sums = unprepare(part_grads, raw, squares, qk_gain, cosines, sines, d_model)
    dots = sum_line(dots.reshape(2, rows)).reshape(2, seqs, length, 1)
    grad_raw, *token_slots = project_in_back(
        part_grads, scaled, raw, squares, dots, in_weights, slots
    )
    gain_parts = jnp.concatenate([qk_sums.reshape(2, heads, 8, -1), own_gains.reshape(2, heads, 8, -1)])
    gain_parts = jnp.transpose(gain_parts, (2, 0, 1, 3)).reshape(8, -1, 128)
    gain_rows_used = gain_parts.shape[1]
    gain_parts = jnp.pad(
        gain_parts, ((0, 0), (0, d_model // 8 - gain_rows_used), (0, 0))
    ).reshape(d_model, 128)
    far_sent, near = sum_in_plane(
        (tokens.reshape(rows, d_model), grad_attn_rows),
        (grad_raw, context_rows),
        gain_parts,
        order,
    )
    token_sums, (_, near) = scatter_line(token_slots, (far_sent, near))
    in_sums = [near[2], to_neighbour(near[0], 1), to_neighbour(near[1], 2)]
    in_sums, ff_sums = lax.optimization_barrier((in_sums, ff_sums))
    *in_sums, gain_sums = plane_totals(in_sums, head_span)
    grad_tokens = grad_hidden
    for part in token_sums:
        grad_tokens = grad_tokens + part.astype(jnp.float32)

    gain_sums = gain_sums[:gain_rows_used].reshape(4, heads, -1)
    return (
        outputs.reshape(cotangent.shape),
        grad_tokens.reshape(cotangent.shape),
        *in_sums,
        ff_sums[0],
        ff_sums[1],
        ff_sums[2],
        gain_sums[0],
        gain_sums[1],
        gain_sums[2],
        gain_sums[3],
    )


def solution(mesh):
    by_plane = (mesh.shape["dp"], mesh.shape["seq"], mesh.shape["tp"]) == (2, 4, 4)
    return jax.shard_map(
        on_plane if by_plane else on_any_mesh,
        mesh=mesh,
        in_specs=(
            P("dp", "seq", None),
            P(("dp", "seq"), "tp"),
            P(("dp", "seq"), "tp"),
            P(("dp", "seq"), "tp"),
            P("tp", ("dp", "seq")),
            P(("dp", "seq"), "tp"),
            P(("dp", "seq"), "tp"),
            P("tp", ("dp", "seq")),
            P("tp", ("dp", "seq")),
            P("tp", ("dp", "seq")),
            P(None, ("dp", "seq")),
            P(None, ("dp", "seq")),
            P("dp", ("seq", "tp"), None),
        ),
        out_specs=(
            P("dp", ("seq", "tp"), None),
            P("dp", ("seq", "tp"), None),
            P(("dp", "seq"), "tp"),
            P(("dp", "seq"), "tp"),
            P(("dp", "seq"), "tp"),
            P("tp", ("dp", "seq")),
            P(("dp", "seq"), "tp"),
            P(("dp", "seq"), "tp"),
            P("tp", ("dp", "seq")),
            P("tp", ("dp", "seq")),
            P("tp", ("dp", "seq")),
            P("tp", ("dp", "seq")),
            P("tp", ("dp", "seq")),
        ),
        check_vma=False,
    )
```

```python
import math

import jax
import jax.numpy as jnp
from jax import lax
from jax.experimental import pallas as pl
from jax.experimental.pallas import tpu as pltpu
from jax.sharding import PartitionSpec as P

NORM_EPS = 1e-06
ROPE_BASE = 500000.0
MASKED = -1e30


def project(left, right):
    return jnp.dot(left, right, preferred_element_type=jnp.float32)


def project_back(left, right):
    return lax.dot_general(
        left, right, (((left.ndim - 1,), (1,)), ((), ())), preferred_element_type=jnp.float32
    )


def outer_sum(left, right):
    return lax.dot_general(
        left, right, (((0, 1), (0, 1)), ((), ())), preferred_element_type=jnp.float32
    )


def rope_tables(positions, head_dim):
    steps = jnp.arange(head_dim // 2, dtype=jnp.float32)
    freqs = jnp.exp(steps * (-2.0 * math.log(ROPE_BASE) / head_dim))
    angles = positions.astype(jnp.float32)[:, None] * freqs[None, :]
    return (jnp.cos(angles)[:, None, :], jnp.sin(angles)[:, None, :])


def rotate(values, cosines, sines):
    half = values.shape[-1] // 2
    first = values[..., :half]
    second = values[..., half:]
    return jnp.concatenate(
        [first * cosines - second * sines, second * cosines + first * sines], axis=-1
    )


def unrotate(grads, cosines, sines):
    half = grads.shape[-1] // 2
    first = grads[..., :half]
    second = grads[..., half:]
    return jnp.concatenate(
        [first * cosines + second * sines, second * cosines - first * sines], axis=-1
    )


def norm_back(normed, grad_normed, inv_scale, total_dot, d_model):
    return inv_scale * (grad_normed - normed * (total_dot / d_model)[..., None])


def on_any_mesh(
    tokens,
    w_query,
    w_key,
    w_value,
    w_out,
    w_gate,
    w_up,
    w_down,
    q_gain,
    k_gain,
    attn_gain,
    mlp_gain,
    cotangent,
):
    seq_count, local_len, d_model = tokens.shape
    seq_rank = lax.axis_index("seq")
    tp_rank = lax.axis_index("tp")
    own_rows = local_len // lax.axis_size("tp")
    weights_in = (
        lax.all_gather(w_query, ("dp", "seq"), axis=0, tiled=True),
        lax.all_gather(w_key, ("dp", "seq"), axis=0, tiled=True),
        lax.all_gather(w_value, ("dp", "seq"), axis=0, tiled=True),
        lax.all_gather(w_out, ("dp", "seq"), axis=1, tiled=True),
        lax.all_gather(w_gate, ("dp", "seq"), axis=0, tiled=True),
        lax.all_gather(w_up, ("dp", "seq"), axis=0, tiled=True),
        lax.all_gather(w_down, ("dp", "seq"), axis=1, tiled=True),
        lax.all_gather(q_gain, ("dp", "seq"), axis=1, tiled=True),
        lax.all_gather(k_gain, ("dp", "seq"), axis=1, tiled=True),
        lax.all_gather(attn_gain, ("dp", "seq"), axis=1, tiled=True),
        lax.all_gather(mlp_gain, ("dp", "seq"), axis=1, tiled=True),
    )
    (
        full_query,
        full_key,
        full_value,
        full_out,
        full_gate,
        full_up,
        full_down,
        full_qgain,
        full_kgain,
        full_again,
        full_mgain,
    ) = weights_in
    local_heads = full_qgain.shape[0]
    head_dim = full_qgain.shape[1]
    head_span = local_heads * head_dim
    score_scale = head_dim ** (-0.5)
    query_gain = full_qgain.astype(jnp.float32).reshape(head_span)
    key_gain = full_kgain.astype(jnp.float32).reshape(head_span)
    attn_scale_gain = full_again.astype(jnp.float32).reshape(d_model)
    mlp_scale_gain = full_mgain.astype(jnp.float32).reshape(d_model)
    query_raw = project(tokens, full_query)
    key_raw = project(tokens, full_key)
    value_raw = project(tokens, full_value)
    query_sq, key_sq = lax.psum(
        (jnp.sum(query_raw * query_raw, axis=-1), jnp.sum(key_raw * key_raw, axis=-1)), "tp"
    )
    query_inv = lax.rsqrt(query_sq / d_model + NORM_EPS)[..., None]
    key_inv = lax.rsqrt(key_sq / d_model + NORM_EPS)[..., None]
    query_unit = query_raw * query_inv
    key_unit = key_raw * key_inv
    positions = seq_rank * local_len + jnp.arange(local_len, dtype=jnp.int32)
    cosines, sines = rope_tables(positions, head_dim)
    heads_shape = (seq_count, local_len, local_heads, head_dim)
    queries = rotate((query_unit * query_gain).reshape(heads_shape), cosines, sines).astype(
        jnp.bfloat16
    )
    keys_local = (
        rotate((key_unit * key_gain).reshape(heads_shape), cosines, sines)
        .astype(jnp.bfloat16)
        .reshape(seq_count, local_len, head_span)
    )
    values_local = value_raw.astype(jnp.bfloat16)
    all_keys, all_values = (
        lax.all_gather(keys_local, "seq", axis=1, tiled=True),
        lax.all_gather(values_local, "seq", axis=1, tiled=True),
    )
    length = all_keys.shape[1]
    keys_full = all_keys.reshape(seq_count, length, local_heads, head_dim)
    values_full = all_values.reshape(seq_count, length, local_heads, head_dim)
    key_rows = min(512, length)
    block_ids = jnp.arange(length // key_rows, dtype=jnp.int32)

    def key_block(block_index):
        first_key = block_index * key_rows
        key_part = lax.dynamic_slice_in_dim(keys_full, first_key, key_rows, 1)
        value_part = lax.dynamic_slice_in_dim(values_full, first_key, key_rows, 1)
        scores = (
            jnp.einsum("mqhd,mkhd->mhqk", queries, key_part, preferred_element_type=jnp.float32)
            * score_scale
        )
        allowed = (first_key + jnp.arange(key_rows, dtype=jnp.int32))[None, :] <= positions[:, None]
        return (key_part, value_part, jnp.where(allowed, scores, MASKED), allowed)

    def max_step(state, block_index):
        running_max, running_sum = state
        key_part, value_part, scores, allowed = key_block(block_index)
        new_max = jnp.maximum(running_max, jnp.max(scores, axis=-1))
        weights_now = jnp.where(allowed, jnp.exp(scores - new_max[..., None]), 0.0)
        return (
            (new_max, running_sum * jnp.exp(running_max - new_max) + jnp.sum(weights_now, axis=-1)),
            None,
        )

    stat_shape = (seq_count, local_heads, local_len)
    final_state, unused = lax.scan(
        max_step,
        (jnp.full(stat_shape, MASKED, jnp.float32), jnp.zeros(stat_shape, jnp.float32)),
        block_ids,
    )
    log_total = (final_state[0] + jnp.log(final_state[1]))[..., None]

    def context_step(context, block_index):
        key_part, value_part, scores, allowed = key_block(block_index)
        probs = jnp.where(allowed, jnp.exp(scores - log_total), 0.0).astype(jnp.bfloat16)
        return (
            context
            + jnp.einsum("mhqk,mkhd->mqhd", probs, value_part, preferred_element_type=jnp.float32),
            None,
        )

    context, unused = lax.scan(context_step, jnp.zeros(heads_shape, jnp.float32), block_ids)
    context_low = context.astype(jnp.bfloat16).reshape(seq_count, local_len, head_span)
    attn_out = lax.psum_scatter(
        project(context_low, full_out), "tp", scatter_dimension=1, tiled=True
    )
    attn_inv = lax.rsqrt(jnp.mean(attn_out * attn_out, axis=-1, keepdims=True) + NORM_EPS)
    attn_unit = attn_out * attn_inv
    own_tokens = lax.dynamic_slice_in_dim(tokens, tp_rank * own_rows, own_rows, 1).astype(
        jnp.float32
    )
    hidden = own_tokens + attn_unit * attn_scale_gain
    hidden_all = lax.all_gather(hidden.astype(jnp.bfloat16), "tp", axis=1, tiled=True)
    gate_act = project(hidden_all, full_gate)
    up_act = project(hidden_all, full_up)
    gate_sig = jax.nn.sigmoid(gate_act)
    mixed = (gate_act * gate_sig * up_act).astype(jnp.bfloat16)
    mlp_out = lax.psum_scatter(project(mixed, full_down), "tp", scatter_dimension=1, tiled=True)
    mlp_inv = lax.rsqrt(jnp.mean(mlp_out * mlp_out, axis=-1, keepdims=True) + NORM_EPS)
    mlp_unit = mlp_out * mlp_inv
    outputs = (hidden + mlp_unit * mlp_scale_gain).astype(jnp.bfloat16)
    weights_back = (
        lax.all_gather(w_query, ("dp", "seq"), axis=0, tiled=True),
        lax.all_gather(w_key, ("dp", "seq"), axis=0, tiled=True),
        lax.all_gather(w_value, ("dp", "seq"), axis=0, tiled=True),
        lax.all_gather(w_out, ("dp", "seq"), axis=1, tiled=True),
        lax.all_gather(w_gate, ("dp", "seq"), axis=0, tiled=True),
        lax.all_gather(w_up, ("dp", "seq"), axis=0, tiled=True),
        lax.all_gather(w_down, ("dp", "seq"), axis=1, tiled=True),
    )
    back_query, back_key, back_value, back_out, back_gate, back_up, back_down = weights_back
    grad_out = cotangent.astype(jnp.float32)
    grad_mgain = jnp.sum(grad_out * mlp_unit, axis=(0, 1))
    mlp_scaled = grad_out * mlp_scale_gain
    grad_mlp = norm_back(
        mlp_unit, mlp_scaled, mlp_inv, jnp.sum(mlp_scaled * mlp_unit, axis=-1), d_model
    ).astype(jnp.bfloat16)
    grad_mlp_all = lax.all_gather(grad_mlp, "tp", axis=1, tiled=True)
    grad_wdown = outer_sum(mixed, grad_mlp_all)
    grad_mixed = project_back(grad_mlp_all, back_down)
    grad_gate = (grad_mixed * up_act * gate_sig * (1.0 + gate_act * (1.0 - gate_sig))).astype(
        jnp.bfloat16
    )
    grad_up = (grad_mixed * gate_act * gate_sig).astype(jnp.bfloat16)
    grad_wgate = outer_sum(hidden_all, grad_gate)
    grad_wup = outer_sum(hidden_all, grad_up)
    hidden_part = project_back(grad_gate, back_gate) + project_back(grad_up, back_up)
    hidden_sum, grad_mgain_part = (
        lax.psum_scatter(hidden_part, "tp", scatter_dimension=1, tiled=True),
        lax.psum_scatter(grad_mgain.reshape(-1, head_dim), "tp", scatter_dimension=0, tiled=True),
    )
    grad_hidden = grad_out + hidden_sum
    grad_again = jnp.sum(grad_hidden * attn_unit, axis=(0, 1))
    attn_scaled = grad_hidden * attn_scale_gain
    grad_attn = norm_back(
        attn_unit, attn_scaled, attn_inv, jnp.sum(attn_scaled * attn_unit, axis=-1), d_model
    ).astype(jnp.bfloat16)
    grad_attn_all = lax.all_gather(grad_attn, "tp", axis=1, tiled=True)
    grad_wout = outer_sum(context_low, grad_attn_all)
    grad_context = project_back(grad_attn_all, back_out).astype(jnp.bfloat16).reshape(heads_shape)

    def delta_step(delta, block_index):
        key_part, value_part, scores, allowed = key_block(block_index)
        probs = jnp.exp(scores - log_total)
        grad_probs = jnp.einsum(
            "mqhd,mkhd->mhqk", grad_context, value_part, preferred_element_type=jnp.float32
        )
        return (delta + jnp.sum(probs * grad_probs, axis=-1), None)

    delta, unused = lax.scan(delta_step, jnp.zeros(stat_shape, jnp.float32), block_ids)

    def score_grads(block_index):
        key_part, value_part, scores, allowed = key_block(block_index)
        probs = jnp.exp(scores - log_total)
        grad_probs = jnp.einsum(
            "mqhd,mkhd->mhqk", grad_context, value_part, preferred_element_type=jnp.float32
        )
        grad_scores = (probs * (grad_probs - delta[..., None])).astype(jnp.bfloat16)
        return (key_part, probs, grad_scores)

    def grad_step(grad_queries, block_index):
        key_part, probs, grad_scores = score_grads(block_index)
        grad_queries = grad_queries + jnp.einsum(
            "mhqk,mkhd->mqhd", grad_scores, key_part, preferred_element_type=jnp.float32
        )
        grad_keys = (
            jnp.einsum("mhqk,mqhd->kmhd", grad_scores, queries, preferred_element_type=jnp.float32)
            * score_scale
        )
        grad_values = jnp.einsum(
            "mhqk,mqhd->kmhd",
            probs.astype(jnp.bfloat16),
            grad_context,
            preferred_element_type=jnp.float32,
        )
        both_terms = jnp.concatenate(
            [
                grad_keys.reshape(key_rows, seq_count, head_span),
                grad_values.reshape(key_rows, seq_count, head_span),
            ],
            axis=-1,
        )
        return (grad_queries, both_terms)

    grad_queries, key_terms = lax.scan(grad_step, jnp.zeros(heads_shape, jnp.float32), block_ids)
    key_value_grads = lax.psum_scatter(
        key_terms.reshape(length, seq_count, 2 * head_span).astype(jnp.bfloat16),
        "seq",
        scatter_dimension=0,
        tiled=True,
    ).astype(jnp.float32)
    key_value_grads = jnp.transpose(key_value_grads, (1, 0, 2))
    grad_keys_own = key_value_grads[..., :head_span].reshape(heads_shape)
    grad_values_own = key_value_grads[..., head_span:].astype(jnp.bfloat16)
    query_grad_unit = unrotate(grad_queries * score_scale, cosines, sines).reshape(
        seq_count, local_len, head_span
    )
    key_grad_unit = unrotate(grad_keys_own, cosines, sines).reshape(seq_count, local_len, head_span)
    grad_qgain = jnp.sum(query_grad_unit * query_unit, axis=(0, 1))
    grad_kgain = jnp.sum(key_grad_unit * key_unit, axis=(0, 1))
    query_scaled = query_grad_unit * query_gain
    key_scaled = key_grad_unit * key_gain
    query_dot, key_dot = lax.psum(
        (jnp.sum(query_scaled * query_unit, axis=-1), jnp.sum(key_scaled * key_unit, axis=-1)), "tp"
    )
    grad_qraw = norm_back(query_unit, query_scaled, query_inv, query_dot, d_model).astype(
        jnp.bfloat16
    )
    grad_kraw = norm_back(key_unit, key_scaled, key_inv, key_dot, d_model).astype(jnp.bfloat16)
    grad_wquery = outer_sum(tokens, grad_qraw)
    grad_wkey = outer_sum(tokens, grad_kraw)
    grad_wvalue = outer_sum(tokens, grad_values_own)
    token_part = (
        project_back(grad_qraw, back_query)
        + project_back(grad_kraw, back_key)
        + project_back(grad_values_own, back_value)
    )
    token_sum, grad_again_part = (
        lax.psum_scatter(
            token_part.astype(jnp.bfloat16), "tp", scatter_dimension=1, tiled=True
        ).astype(jnp.float32),
        lax.psum_scatter(
            grad_again.reshape(-1, head_dim).astype(jnp.bfloat16),
            "tp",
            scatter_dimension=0,
            tiled=True,
        ).astype(jnp.float32),
    )
    grad_tokens = grad_hidden + token_sum
    summed = (
        lax.psum_scatter(
            grad_wquery.astype(jnp.bfloat16), ("dp", "seq"), scatter_dimension=0, tiled=True
        ).astype(jnp.float32),
        lax.psum_scatter(
            grad_wkey.astype(jnp.bfloat16), ("dp", "seq"), scatter_dimension=0, tiled=True
        ).astype(jnp.float32),
        lax.psum_scatter(
            grad_wvalue.astype(jnp.bfloat16), ("dp", "seq"), scatter_dimension=0, tiled=True
        ).astype(jnp.float32),
        lax.psum_scatter(
            grad_wout.astype(jnp.bfloat16), ("dp", "seq"), scatter_dimension=1, tiled=True
        ).astype(jnp.float32),
        lax.psum_scatter(
            grad_wgate.astype(jnp.bfloat16), ("dp", "seq"), scatter_dimension=0, tiled=True
        ).astype(jnp.float32),
        lax.psum_scatter(
            grad_wup.astype(jnp.bfloat16), ("dp", "seq"), scatter_dimension=0, tiled=True
        ).astype(jnp.float32),
        lax.psum_scatter(
            grad_wdown.astype(jnp.bfloat16), ("dp", "seq"), scatter_dimension=1, tiled=True
        ).astype(jnp.float32),
        lax.psum_scatter(
            grad_qgain.reshape(local_heads, head_dim).astype(jnp.bfloat16),
            ("dp", "seq"),
            scatter_dimension=1,
            tiled=True,
        ).astype(jnp.float32),
        lax.psum_scatter(
            grad_kgain.reshape(local_heads, head_dim).astype(jnp.bfloat16),
            ("dp", "seq"),
            scatter_dimension=1,
            tiled=True,
        ).astype(jnp.float32),
        lax.psum_scatter(
            grad_again_part.astype(jnp.bfloat16), ("dp", "seq"), scatter_dimension=1, tiled=True
        ).astype(jnp.float32),
        lax.psum_scatter(
            grad_mgain_part.astype(jnp.bfloat16), ("dp", "seq"), scatter_dimension=1, tiled=True
        ).astype(jnp.float32),
    )
    (
        sum_query,
        sum_key,
        sum_value,
        sum_out,
        sum_gate,
        sum_up,
        sum_down,
        sum_qgain,
        sum_kgain,
        sum_again,
        sum_mgain,
    ) = summed
    return (
        outputs,
        grad_tokens,
        sum_query,
        sum_key,
        sum_value,
        sum_out,
        sum_gate,
        sum_up,
        sum_down,
        sum_qgain,
        sum_kgain,
        sum_again,
        sum_mgain,
    )


LOW = jnp.bfloat16


def vmem(mebibytes):
    return pltpu.CompilerParams(vmem_limit_bytes=mebibytes * 1024 * 1024)


def to_neighbour(values, flip):
    return lax.ppermute(values, "seq", [(i, i ^ flip) for i in range(4)])


def to_core(values):
    return lax.ppermute(values, "dp", [(0, 1), (1, 0)])


def after(values, done):
    return lax.optimization_barrier((values, done))[0]


def first_step(shard):
    return to_neighbour(shard, 1), to_neighbour(shard, 2)


def gather_plane(shard, firsts, meanwhile=()):
    half = shard.shape[0] // 2
    (from_one, from_two), meanwhile = lax.optimization_barrier((firsts, meanwhile))
    far = [to_neighbour(from_two[:half], 1), to_neighbour(from_one[half:], 2)]
    near = [shard, from_one, from_two]
    far, other = lax.optimization_barrier((far, [to_core(piece) for piece in near]))
    return near + far + other + [to_core(piece) for piece in far], meanwhile


def place_piece(out_ref, order_ref, k, piece, axis):
    block = piece.shape[axis]
    if axis == 0 and k % 5 > 2:
        block *= 2
    first = piece.shape[0] if k % 5 == 4 else 0
    start = order_ref[(k // 5) * 4 + min(k % 5, 3)] * block
    if axis == 0:
        out_ref[pl.ds(pl.multiple_of(start + first, piece.shape[0]), piece.shape[0])] = piece
    else:
        out_ref[first : first + piece.shape[0], pl.ds(pl.multiple_of(start, block), block)] = piece


def assemble_columns(pieces, order):
    height, block = pieces[0].shape

    def body(order_ref, *refs):
        for k in range(10):
            place_piece(refs[10], order_ref, k, refs[k][...], 1)

    return pl.pallas_call(
        body,
        in_specs=[pl.BlockSpec(memory_space=pltpu.SMEM)]
        + [pl.BlockSpec(memory_space=pltpu.VMEM)] * 10,
        out_specs=pl.BlockSpec(memory_space=pltpu.VMEM),
        out_shape=jax.ShapeDtypeStruct((height, 8 * block), pieces[0].dtype),
        compiler_params=vmem(50),
        name="assemble_columns",
    )(order, *pieces)


def project_in(rows_low, pieces, order):
    rows, width = rows_low.shape
    columns = pieces[0].shape[1]
    tile = columns // 3

    def body(order_ref, rows_ref, *refs):
        for k in range(10):
            place_piece(refs[11], order_ref, k, refs[k][...], 0)
        refs[10][...] = jnp.dot(rows_ref[...], refs[11][...], preferred_element_type=jnp.float32)

    return pl.pallas_call(
        body,
        grid_spec=pltpu.PrefetchScalarGridSpec(
            num_scalar_prefetch=1,
            grid=(3,),
            in_specs=[pl.BlockSpec((rows, width), lambda j, o: (0, 0))]
            + [pl.BlockSpec((piece.shape[0], tile), lambda j, o: (0, j)) for piece in pieces],
            out_specs=[
                pl.BlockSpec((rows, tile), lambda j, o: (0, j)),
                pl.BlockSpec((width, tile), lambda j, o: (0, j)),
            ],
        ),
        out_shape=[
            jax.ShapeDtypeStruct((rows, columns), jnp.float32),
            jax.ShapeDtypeStruct((width, columns), LOW),
        ],
        compiler_params=vmem(50),
        name="project_in",
    )(order, rows_low, *pieces)


def grad_blocks(lefts, rights, extra, order, blocks, received=None, far=None):
    rows, d_model = lefts[0].shape
    block = d_model // 8
    half = block // 2
    count = len(blocks)
    width = sum(right.shape[1] for right in rights) + extra.shape[1]
    fresh = received is None

    def body(order_ref, *refs):
        left_refs, right_refs = refs[: len(lefts)], refs[len(lefts) : len(lefts) + len(rights)]
        extra_ref, rest = refs[len(lefts) + len(rights)], refs[len(lefts) + len(rights) + 1 :]
        first = 0
        for k in range(len(lefts) + 1):
            if k < len(lefts):
                total = contract(left_refs[k][...], right_refs[k][...], 0, 0)
            else:
                total = extra_ref[...]
            columns = slice(first, first + total.shape[1])
            first += total.shape[1]
            if fresh:
                rest[0][:, columns] = total.astype(LOW)
                continue
            total = total + rest[0][:, columns].astype(jnp.float32)
            if far is None:
                rest[1][:, columns] = total[:half].astype(LOW)
                rest[2][:, columns] = total[half:].astype(LOW)
                continue
            low, high, outs = rest[1], rest[2], rest[3:]

            @pl.when(pl.program_id(0) == 0)
            def _(total=total, columns=columns):
                outs[0][:half, columns] = total[:half].astype(LOW)
                outs[0][half:, columns] = (
                    total[half:] + high[:, columns].astype(jnp.float32)
                ).astype(LOW)

            @pl.when(pl.program_id(0) == 1)
            def _(total=total, columns=columns):
                outs[1][:half, columns] = (
                    total[:half] + low[:, columns].astype(jnp.float32)
                ).astype(LOW)
                outs[1][half:, columns] = total[half:].astype(LOW)

            @pl.when(pl.program_id(0) == 2)
            def _(total=total, columns=columns):
                outs[2][:, columns] = total.astype(LOW)

    def pick(j):
        value = blocks[0]
        for i, entry in enumerate(blocks[1:]):
            value = jnp.where(j > i, entry, value)
        return value

    def fixed(height):
        return pl.BlockSpec((height, width), lambda j, o: (0, 0))

    in_specs = [pl.BlockSpec((rows, block), lambda j, o: (0, o[pick(j)])) for _ in lefts]
    in_specs += [pl.BlockSpec(right.shape, lambda j, o: (0, 0)) for right in rights]
    in_specs.append(pl.BlockSpec((block, extra.shape[1]), lambda j, o: (o[pick(j)], 0)))
    more = ()
    if fresh:
        out_specs = [pl.BlockSpec((block, width), lambda j, o: (j, 0))]
        out_shape = [jax.ShapeDtypeStruct((count * block, width), LOW)]
    else:
        in_specs.append(pl.BlockSpec((block, width), lambda j, o: (pick(j), 0)))
        more = (received,)
        if far is None:
            out_specs = [fixed(half)] * 2
            out_shape = [jax.ShapeDtypeStruct((half, width), LOW)] * 2
        else:
            more += tuple(far)
            in_specs += [fixed(half)] * 2
            out_specs = [fixed(block)] * 3
            out_shape = [jax.ShapeDtypeStruct((block, width), LOW)] * 3
    return pl.pallas_call(
        body,
        grid_spec=pltpu.PrefetchScalarGridSpec(
            num_scalar_prefetch=1, grid=(count,), in_specs=in_specs, out_specs=out_specs
        ),
        out_shape=out_shape,
        compiler_params=vmem(24),
        name="grad_blocks",
    )(order, *lefts, *rights, extra, *more)


def sum_in_plane(*parts):
    (sent,) = grad_blocks(*parts, (4, 5, 6, 7))
    received = to_core(sent)
    sent = grad_blocks(*parts, (3,), received)
    far = [to_neighbour(sent[0], 1), to_neighbour(sent[1], 2)]
    return sent, grad_blocks(*parts, (1, 2, 0), received, far)


def gather_line(own):
    up, down = own, own
    ups, downs = [], []
    for t in range(1, 4):
        up = lax.ppermute(up, "tp", [(i, i + 1) for i in range(t - 1, 3)])
        down = lax.ppermute(down, "tp", [(i, i - 1) for i in range(1, 5 - t)])
        ups.append(up)
        downs.append(down)
    return [own] + ups + downs


def scatter_line(slots, meanwhile=((), ())):
    meanwhile = list(meanwhile)
    def added(mine, got):
        return (mine.astype(jnp.float32) + got.astype(jnp.float32)).astype(LOW)

    up, down = slots[1], slots[3]
    for t in range(1, 4):
        up = lax.ppermute(up, "tp", [(i, i + 1) for i in range(t)])
        down = lax.ppermute(down, "tp", [(i, i - 1) for i in range(4 - t, 4)])
        if t < 3:
            up, down, meanwhile[t - 1] = lax.optimization_barrier((up, down, meanwhile[t - 1]))
            up = added(slots[t + 1], up)
            down = added(slots[3 - t], down)
    return (slots[0], up, down), meanwhile


def sum_line(values):
    flat = lax.optimization_barrier(values.reshape(1, -1, 128))
    flat = lax.all_to_all(jnp.broadcast_to(flat, (4,) + flat.shape[1:]), "tp", 0, 0, tiled=True)
    return jnp.sum(lax.optimization_barrier(flat), axis=0)


def contract(left, right, left_dim, right_dim):
    return lax.dot_general(
        left, right, (((left_dim,), (right_dim,)), ((), ())), preferred_element_type=jnp.float32
    )


def turned(values, cosines, sines):
    return values * cosines + pltpu.roll(values, values.shape[-1] // 2, axis=1) * sines


def inverse_norm(squares, d_model):
    return lax.rsqrt(squares * (1.0 / d_model) + NORM_EPS)


def prepare(raw, squares, gains, cosines, sines, heads, head_dim, d_model):
    seqs, length, _ = raw.shape
    own = length // 4
    rows = seqs * own
    span = heads * head_dim

    def body(raw_ref, square_ref, gain_ref, cos_ref, sin_ref, out_ref):
        cosine = jnp.concatenate([cos_ref[...]] * seqs, axis=0)
        sine = jnp.concatenate([sin_ref[...]] * seqs, axis=0)
        for t in range(2):
            inv = inverse_norm(square_ref[t].reshape(rows, 1), d_model)
            for h in range(heads):
                columns = slice(t * span + h * head_dim, t * span + (h + 1) * head_dim)
                normed = raw_ref[:, :, columns].reshape(rows, head_dim) * inv * gain_ref[:, columns]
                out_ref[h, t] = (
                    turned(normed, cosine, sine).astype(LOW).reshape(seqs, own, head_dim)
                )
        for h in range(heads):
            columns = slice(2 * span + h * head_dim, 2 * span + (h + 1) * head_dim)
            out_ref[h, 2] = raw_ref[:, :, columns].astype(LOW)

    return pl.pallas_call(
        body,
        grid=(4,),
        in_specs=[
            pl.BlockSpec((seqs, own, 3 * span), lambda t: (0, t, 0)),
            pl.BlockSpec((2, seqs, own, 1), lambda t: (0, 0, t, 0)),
            pl.BlockSpec((1, 2 * span), lambda t: (0, 0)),
            pl.BlockSpec((own, head_dim), lambda t: (t, 0)),
            pl.BlockSpec((own, head_dim), lambda t: (t, 0)),
        ],
        out_specs=pl.BlockSpec((heads, 3, seqs, own, head_dim), lambda t: (0, 0, 0, t, 0)),
        out_shape=jax.ShapeDtypeStruct((heads, 3, seqs, length, head_dim), LOW),
        compiler_params=vmem(50),
        name="prepare",
    )(raw, squares, gains, cosines, sines)


def scores_of(left, right):
    return lax.dot_general(
        left, right, (((1,), (1,)), ((), ())), preferred_element_type=jnp.float32
    )


def causal(scores, first):
    rows = lax.broadcasted_iota(jnp.int32, scores.shape, 0) + first
    columns = lax.broadcasted_iota(jnp.int32, scores.shape, 1)
    return columns <= rows


def attend(parts):
    blocks, _, seqs, length, head_dim = parts.shape
    score_scale = head_dim ** (-0.5)

    def body(parts_ref, out_ref, log_ref):
        for i in range(blocks):
            span = (i + 1) * length
            keys = parts_ref[: i + 1, 1, 0].reshape(span, head_dim)
            values = parts_ref[: i + 1, 2, 0].reshape(span, head_dim)
            scores = scores_of(parts_ref[i, 0, 0], keys) * score_scale
            scores = jnp.where(causal(scores, i * length), scores, MASKED)
            top = jnp.max(scores, axis=-1, keepdims=True)
            weights = jnp.exp(scores - top)
            total = jnp.sum(weights, axis=-1, keepdims=True)
            probs = (weights * (1.0 / total)).astype(LOW)
            out_ref[i, 0] = jnp.dot(probs, values, preferred_element_type=jnp.float32).astype(LOW)
            log_ref[i, 0] = top + jnp.log(total)

    return pl.pallas_call(
        body,
        grid=(seqs,),
        in_specs=[pl.BlockSpec((blocks, 3, 1, length, head_dim), lambda m: (0, 0, m, 0, 0))],
        out_specs=[
            pl.BlockSpec((blocks, 1, length, head_dim), lambda m: (0, m, 0, 0)),
            pl.BlockSpec((blocks, 1, length, 1), lambda m: (0, m, 0, 0)),
        ],
        out_shape=[
            jax.ShapeDtypeStruct((blocks, seqs, length, head_dim), LOW),
            jax.ShapeDtypeStruct((blocks, seqs, length, 1), jnp.float32),
        ],
        compiler_params=vmem(50),
        name="attend",
    )(parts)


def attend_back(parts, grad_context, log_total):
    blocks, _, seqs, length, head_dim = parts.shape
    score_scale = head_dim ** (-0.5)

    def body(parts_ref, grad_ref, log_ref, out_ref, keys_sum, values_sum):
        keys_sum[...] = jnp.zeros_like(keys_sum)
        values_sum[...] = jnp.zeros_like(values_sum)
        for i in range(blocks):
            span = (i + 1) * length
            queries = parts_ref[i, 0, 0]
            keys = parts_ref[: i + 1, 1, 0].reshape(span, head_dim)
            values = parts_ref[: i + 1, 2, 0].reshape(span, head_dim)
            grads = grad_ref[i, :, 0].reshape(length, head_dim)
            scores = scores_of(queries, keys) * score_scale
            probs = jnp.where(causal(scores, i * length), jnp.exp(scores - log_ref[i, 0]), 0.0)
            grad_probs = scores_of(grads, values)
            delta = jnp.sum(probs * grad_probs, axis=-1, keepdims=True)
            grad_scores = (probs * (grad_probs - delta)).astype(LOW)
            out_ref[i, 0, 0] = (
                jnp.dot(grad_scores, keys, preferred_element_type=jnp.float32) * score_scale
            ).astype(LOW)
            keys_sum[:span] += contract(grad_scores, queries, 0, 0)
            values_sum[:span] += contract(probs.astype(LOW), grads, 0, 0)
        out_ref[:, 1, 0] = (
            (keys_sum[...] * score_scale).astype(LOW).reshape(blocks, length, head_dim)
        )
        out_ref[:, 2, 0] = values_sum[...].astype(LOW).reshape(blocks, length, head_dim)

    whole = pl.BlockSpec((blocks, 3, 1, length, head_dim), lambda m: (0, 0, m, 0, 0))
    return pl.pallas_call(
        body,
        grid=(seqs,),
        in_specs=[
            whole,
            pl.BlockSpec((blocks, 4, 1, length // 4, head_dim), lambda m: (0, 0, m, 0, 0)),
            pl.BlockSpec((blocks, 1, length, 1), lambda m: (0, m, 0, 0)),
        ],
        out_specs=whole,
        out_shape=jax.ShapeDtypeStruct(parts.shape, LOW),
        scratch_shapes=[
            pltpu.VMEM((blocks * length, head_dim), jnp.float32),
            pltpu.VMEM((blocks * length, head_dim), jnp.float32),
        ],
        compiler_params=vmem(50),
        name="attend_back",
    )(parts, grad_context, log_total)


def project_out(context, weights, slots):
    heads, seqs, length, head_dim = context.shape
    span, width = weights.shape
    own = length // 4
    own_rows = seqs * own
    tile = width // 2

    def body(slots_ref, context_ref, weight_ref, rows_ref, *outs):
        @pl.when(pl.program_id(0) == 0)
        def _():
            for t in range(4):
                place = pl.ds(pl.multiple_of(slots_ref[t] * own, own), own)
                for h in range(heads):
                    rows_ref[
                        t * own_rows : (t + 1) * own_rows, h * head_dim : (h + 1) * head_dim
                    ] = context_ref[h, :, place].reshape(own_rows, head_dim)

        product = jnp.dot(rows_ref[...], weight_ref[...], preferred_element_type=jnp.float32)
        for t in range(4):
            outs[t][...] = product[t * own_rows : (t + 1) * own_rows].astype(LOW)

    return pl.pallas_call(
        body,
        grid_spec=pltpu.PrefetchScalarGridSpec(
            num_scalar_prefetch=1,
            grid=(2,),
            in_specs=[
                pl.BlockSpec(context.shape, lambda j, s: (0, 0, 0, 0)),
                pl.BlockSpec((span, tile), lambda j, s: (0, j)),
            ],
            out_specs=[pl.BlockSpec((4 * own_rows, span), lambda j, s: (0, 0))]
            + [pl.BlockSpec((own_rows, tile), lambda j, s: (0, j))] * 4,
        ),
        out_shape=[jax.ShapeDtypeStruct((4 * own_rows, span), LOW)]
        + [jax.ShapeDtypeStruct((own_rows, width), LOW)] * 4,
        compiler_params=vmem(50),
        name="project_out",
    )(slots, context, weights)


def project_out_back(grads, weights, heads, head_dim, seqs):
    rows, width = grads.shape
    own = rows // seqs
    span = heads * head_dim

    def body(grad_ref, weight_ref, out_ref):
        product = jnp.dot(grad_ref[...], weight_ref[...], preferred_element_type=jnp.float32)
        for h in range(heads):
            out_ref[h, 0] = (
                product[:, h * head_dim : (h + 1) * head_dim].astype(LOW).reshape(seqs, own, head_dim)
            )

    return pl.pallas_call(
        body,
        grid=(4,),
        in_specs=[
            pl.BlockSpec((rows, width), lambda j: (0, 0)),
            pl.BlockSpec((width, span), lambda j: (0, j)),
        ],
        out_specs=pl.BlockSpec((heads, 1, seqs, own, head_dim), lambda j: (0, j, 0, 0, 0)),
        out_shape=jax.ShapeDtypeStruct((heads, 4, seqs, own, head_dim), LOW),
        compiler_params=vmem(50),
        name="project_out_back",
    )(grads, weights)


def rows_of(pieces):
    own, width = pieces[0].shape

    def body(*refs):
        fill_slots(refs[7], refs[:7])

    return pl.pallas_call(
        body,
        out_shape=jax.ShapeDtypeStruct((4 * own, width), LOW),
        compiler_params=vmem(14),
        name="rows_of",
    )(*pieces)


def unprepare(grads, raw, squares, gains, cosines, sines, d_model):
    heads, _, seqs, length, head_dim = grads.shape
    own = length // 4
    rows = seqs * own
    span = heads * head_dim

    def body(
        grad_ref, raw_ref, square_ref, gain_ref, cos_ref, sin_ref, scaled_ref, dot_ref, sum_ref
    ):
        cosine = jnp.concatenate([cos_ref[...]] * seqs, axis=0)
        sine = -jnp.concatenate([sin_ref[...]] * seqs, axis=0)

        @pl.when(pl.program_id(0) == 0)
        def _():
            sum_ref[...] = jnp.zeros_like(sum_ref)

        for t in range(2):
            inv = inverse_norm(square_ref[t].reshape(rows, 1), d_model)
            total = jnp.zeros((rows, head_dim), jnp.float32)
            for h in range(heads):
                columns = slice(t * span + h * head_dim, t * span + (h + 1) * head_dim)
                back = turned(
                    grad_ref[h, t].reshape(rows, head_dim).astype(jnp.float32), cosine, sine
                )
                along = back * (raw_ref[:, :, columns].reshape(rows, head_dim) * inv)
                sum_ref[:, columns] += jnp.sum(along, axis=0, keepdims=True)
                scaled_ref[:, :, columns] = (back * gain_ref[:, columns]).reshape(
                    seqs, own, head_dim
                )
                total += along * gain_ref[:, columns]
            dot_ref[t] = jnp.sum(total, axis=-1, keepdims=True).reshape(seqs, own, 1)

    return pl.pallas_call(
        body,
        grid=(4,),
        in_specs=[
            pl.BlockSpec((heads, 3, seqs, own, head_dim), lambda t: (0, 0, 0, t, 0)),
            pl.BlockSpec((seqs, own, 3 * span), lambda t: (0, t, 0)),
            pl.BlockSpec((2, seqs, own, 1), lambda t: (0, 0, t, 0)),
            pl.BlockSpec((1, 2 * span), lambda t: (0, 0)),
            pl.BlockSpec((own, head_dim), lambda t: (t, 0)),
            pl.BlockSpec((own, head_dim), lambda t: (t, 0)),
        ],
        out_specs=[
            pl.BlockSpec((seqs, own, 2 * span), lambda t: (0, t, 0)),
            pl.BlockSpec((2, seqs, own, 1), lambda t: (0, 0, t, 0)),
            pl.BlockSpec((1, 2 * span), lambda t: (0, 0)),
        ],
        out_shape=[
            jax.ShapeDtypeStruct((seqs, length, 2 * span), jnp.float32),
            jax.ShapeDtypeStruct((2, seqs, length, 1), jnp.float32),
            jax.ShapeDtypeStruct((1, 2 * span), jnp.float32),
        ],
        compiler_params=vmem(14),
        name="unprepare",
    )(grads, raw, squares, gains, cosines, sines)


def project_in_back(grads, scaled, raw, squares, dots, weights, slots):
    heads, _, seqs, length, head_dim = grads.shape
    own = length // 4
    own_rows = seqs * own
    rows = seqs * length
    span = heads * head_dim
    d_model = weights.shape[0]
    tile = d_model // 4

    def body(
        slots_ref, grad_ref, scaled_ref, raw_ref, square_ref, dot_ref, weight_ref, rows_ref, *refs
    ):
        outs, product = refs[:4], refs[4]

        @pl.when(pl.program_id(0) == 0)
        def _():
            for k in range(2):
                columns = slice(k * span, (k + 1) * span)
                inv = inverse_norm(square_ref[k].reshape(rows, 1), d_model)
                mean = dot_ref[k].reshape(rows, 1) * (1.0 / d_model)
                unit = raw_ref[:, :, columns].reshape(rows, span) * inv
                rows_ref[:, columns] = (
                    inv * (scaled_ref[:, :, columns].reshape(rows, span) - unit * mean)
                ).astype(LOW)
            for h in range(heads):
                columns = slice(2 * span + h * head_dim, 2 * span + (h + 1) * head_dim)
                rows_ref[:, columns] = grad_ref[h, 0].reshape(rows, head_dim)

        product[...] = scores_of(rows_ref[...], weight_ref[...]).reshape(seqs, length, tile)
        for t in range(4):
            place = pl.ds(pl.multiple_of(slots_ref[t] * own, own), own)
            outs[t][...] = product[:, place].reshape(own_rows, tile).astype(LOW)

    flat = pl.BlockSpec((2, seqs, length, 1), lambda j, s: (0, 0, 0, 0))
    return pl.pallas_call(
        body,
        grid_spec=pltpu.PrefetchScalarGridSpec(
            num_scalar_prefetch=1,
            grid=(4,),
            in_specs=[
                pl.BlockSpec((heads, 1, seqs, length, head_dim), lambda j, s: (0, 2, 0, 0, 0)),
                pl.BlockSpec((seqs, length, 2 * span), lambda j, s: (0, 0, 0)),
                pl.BlockSpec((seqs, length, 2 * span), lambda j, s: (0, 0, 0)),
                flat,
                flat,
                pl.BlockSpec((tile, 3 * span), lambda j, s: (j, 0)),
            ],
            out_specs=[pl.BlockSpec((rows, 3 * span), lambda j, s: (0, 0))]
            + [pl.BlockSpec((own_rows, tile), lambda j, s: (0, j))] * 4,
            scratch_shapes=[pltpu.VMEM((seqs, length, tile), jnp.float32)],
        ),
        out_shape=[jax.ShapeDtypeStruct((rows, 3 * span), LOW)]
        + [jax.ShapeDtypeStruct((own_rows, d_model), LOW)] * 4,
        compiler_params=vmem(32),
        name="project_in_back",
    )(slots, grads, scaled, raw, squares, dots, weights)


def fill_slots(rows_ref, refs):
    own = refs[0].shape[0]
    seqs = len(refs) // 7
    for m in range(seqs):
        mine = refs[7 * m : 7 * m + 7]
        rows_ref[m * own : (m + 1) * own] = mine[0][...]
        for t in range(1, 4):
            first = (t * seqs + m) * own
            rows_ref[first : first + own] = mine[t][...] + mine[7 - t][...]


def attn_norm(parts, tokens, gains):
    rows, width = tokens.shape

    def body(own_ref, up_ref, down_ref, token_ref, gain_ref, hidden_ref, low_ref, unit_ref, inv_ref):
        total = (
            own_ref[...].astype(jnp.float32)
            + up_ref[...].astype(jnp.float32)
            + down_ref[...].astype(jnp.float32)
        )
        inv = lax.rsqrt(jnp.mean(total * total, axis=-1, keepdims=True) + NORM_EPS)
        unit = total * inv
        hidden = token_ref[...].astype(jnp.float32) + unit * gain_ref[...]
        hidden_ref[...] = hidden
        low_ref[...] = hidden.astype(LOW)
        unit_ref[...] = unit
        inv_ref[...] = inv

    full = jax.ShapeDtypeStruct((rows, width), jnp.float32)
    return pl.pallas_call(
        body,
        out_shape=[
            full,
            jax.ShapeDtypeStruct((rows, width), LOW),
            full,
            jax.ShapeDtypeStruct((rows, 1), jnp.float32),
        ],
        compiler_params=vmem(50),
        name="attn_norm",
    )(*parts, tokens, gains)


def mlp_norm(parts, hidden, cotangent, gains):
    rows, width = hidden.shape

    def body(own_ref, up_ref, down_ref, hidden_ref, grad_ref, gain_ref, out_ref, back_ref, sum_ref):
        total = (
            own_ref[...].astype(jnp.float32)
            + up_ref[...].astype(jnp.float32)
            + down_ref[...].astype(jnp.float32)
        )
        inv = lax.rsqrt(jnp.mean(total * total, axis=-1, keepdims=True) + NORM_EPS)
        unit = total * inv
        out_ref[...] = (hidden_ref[...] + unit * gain_ref[...]).astype(LOW)
        grad = grad_ref[...].astype(jnp.float32)
        sum_ref[...] = jnp.sum(grad * unit, axis=0, keepdims=True)
        scaled = grad * gain_ref[...]
        mean = jnp.mean(scaled * unit, axis=-1, keepdims=True)
        back_ref[...] = (inv * (scaled - unit * mean)).astype(LOW)

    return pl.pallas_call(
        body,
        out_shape=[jax.ShapeDtypeStruct((rows, width), LOW)] * 2
        + [jax.ShapeDtypeStruct((1, width), jnp.float32)],
        compiler_params=vmem(50),
        name="mlp_norm",
    )(*parts, hidden, cotangent, gains)


def attn_norm_back(parts, cotangent, unit, inv, gains):
    rows, width = unit.shape

    def body(
        own_ref, up_ref, down_ref, grad_ref, unit_ref, inv_ref, gain_ref, hidden_ref, back_ref, sum_ref
    ):
        grad = (
            grad_ref[...].astype(jnp.float32)
            + own_ref[...].astype(jnp.float32)
            + up_ref[...].astype(jnp.float32)
            + down_ref[...].astype(jnp.float32)
        )
        hidden_ref[...] = grad
        unit = unit_ref[...]
        sum_ref[...] = jnp.sum(grad * unit, axis=0, keepdims=True)
        scaled = grad * gain_ref[...]
        mean = jnp.mean(scaled * unit, axis=-1, keepdims=True)
        back_ref[...] = (inv_ref[...] * (scaled - unit * mean)).astype(LOW)

    return pl.pallas_call(
        body,
        out_shape=[
            jax.ShapeDtypeStruct((rows, width), jnp.float32),
            jax.ShapeDtypeStruct((rows, width), LOW),
            jax.ShapeDtypeStruct((1, width), jnp.float32),
        ],
        compiler_params=vmem(50),
        name="attn_norm_back",
    )(*parts, cotangent, unit, inv, gains)


def ff_totals(gate_up, down):
    height, units = down.shape
    steps = 4

    def body(gate_ref, up_ref, down_ref, gate_out, up_out, down_out):
        gate_out[...] = gate_ref[...].astype(jnp.float32)
        up_out[...] = up_ref[...].astype(jnp.float32)
        down_out[...] = down_ref[...].astype(jnp.float32).T

    tile = units // steps
    return pl.pallas_call(
        body,
        grid=(steps,),
        in_specs=[
            pl.BlockSpec((height, tile), lambda j: (0, j)),
            pl.BlockSpec((height, tile), lambda j: (0, steps + j)),
            pl.BlockSpec((height, tile), lambda j: (0, j)),
        ],
        out_specs=[pl.BlockSpec((height, tile), lambda j: (0, j))] * 2
        + [pl.BlockSpec((tile, height), lambda j: (j, 0))],
        out_shape=[jax.ShapeDtypeStruct((height, units), jnp.float32)] * 2
        + [jax.ShapeDtypeStruct((units, height), jnp.float32)],
        compiler_params=vmem(50),
        name="ff_totals",
    )(gate_up, gate_up, down)


def plane_totals(sums, span):
    height, width = sums[0].shape
    more = width - 4 * span

    def body(*refs):
        outs = refs[3:]
        for k in range(5):
            columns = slice(k * span, min((k + 1) * span, width))
            total = (
                refs[0][:, columns].astype(jnp.float32)
                + refs[1][:, columns].astype(jnp.float32)
                + refs[2][:, columns].astype(jnp.float32)
            )
            outs[k][...] = total.T if k == 3 else total

    return pl.pallas_call(
        body,
        out_shape=[jax.ShapeDtypeStruct((height, span), jnp.float32)] * 3
        + [
            jax.ShapeDtypeStruct((span, height), jnp.float32),
            jax.ShapeDtypeStruct((height, more), jnp.float32),
        ],
        compiler_params=vmem(50),
        name="plane_totals",
    )(*sums)


def weight_tiles(width, tile, tiles):
    return [pl.BlockSpec((width, tile), lambda j, k=k: (0, k * tiles + j)) for k in range(3)]


def feed_forward(pieces, weights):
    count = len(pieces)
    own, width = pieces[0].shape
    hidden_units = weights.shape[1] // 3
    tile = 512
    tiles = hidden_units // tile
    parts = 4 * count // 7
    rows = parts * own

    def body(*refs):
        ins, (gate_w, up_w, down_w) = refs[:count], refs[count : count + 3]
        rows_ref, gate_ref, up_ref, mixed_ref, *outs = refs[count + 3 : -1]
        total = refs[-1]

        @pl.when(pl.program_id(0) == 0)
        def _():
            fill_slots(rows_ref, ins)

        gate = jnp.dot(rows_ref[...], gate_w[...], preferred_element_type=jnp.float32)
        up = jnp.dot(rows_ref[...], up_w[...], preferred_element_type=jnp.float32)
        mixed = (gate * jax.nn.sigmoid(gate) * up).astype(LOW)
        gate_ref[...] = gate.astype(LOW)
        up_ref[...] = up.astype(LOW)
        mixed_ref[...] = mixed
        part = scores_of(mixed, down_w[...])

        @pl.when(pl.program_id(0) == 0)
        def _():
            total[...] = part

        @pl.when((pl.program_id(0) > 0) & (pl.program_id(0) < tiles - 1))
        def _():
            total[...] += part

        @pl.when(pl.program_id(0) == tiles - 1)
        def _():
            for t in range(parts):
                mine = slice(t * own, (t + 1) * own)
                outs[t][...] = (total[mine] + part[mine]).astype(LOW)

    fixed = pl.BlockSpec((own, width), lambda j: (0, 0))
    by_tile = pl.BlockSpec((rows, tile), lambda j: (0, j))
    return pl.pallas_call(
        body,
        grid=(tiles,),
        in_specs=[fixed] * count + weight_tiles(width, tile, tiles),
        out_specs=[pl.BlockSpec((rows, width), lambda j: (0, 0))] + [by_tile] * 3 + [fixed] * parts,
        out_shape=[jax.ShapeDtypeStruct((rows, width), LOW)]
        + [jax.ShapeDtypeStruct((rows, hidden_units), LOW)] * 3
        + [jax.ShapeDtypeStruct((own, width), LOW)] * parts,
        scratch_shapes=[pltpu.VMEM((rows, width), jnp.float32)],
        compiler_params=vmem(50),
        name="feed_forward",
    )(*pieces, weights, weights, weights)


def feed_forward_back(rows_low, gate, up, weights, parts):
    rows, width = rows_low.shape
    own = rows // parts
    hidden_units = gate.shape[1]
    tile = 512
    tiles = hidden_units // tile

    def body(rows_ref, gate_ref, up_ref, gate_w, up_w, down_w, grad_gate_ref, grad_up_ref, *refs):
        outs, total = refs[:parts], refs[parts]
        grad_mixed = jnp.dot(rows_ref[...], down_w[...], preferred_element_type=jnp.float32)
        gate = gate_ref[...].astype(jnp.float32)
        up = up_ref[...].astype(jnp.float32)
        sig = jax.nn.sigmoid(gate)
        grad_gate = (grad_mixed * up * sig * (1.0 + gate * (1.0 - sig))).astype(LOW)
        grad_up = (grad_mixed * gate * sig).astype(LOW)
        grad_gate_ref[...] = grad_gate
        grad_up_ref[...] = grad_up
        part = scores_of(grad_gate, gate_w[...]) + scores_of(grad_up, up_w[...])

        @pl.when(pl.program_id(0) == 0)
        def _():
            total[...] = part

        @pl.when((pl.program_id(0) > 0) & (pl.program_id(0) < tiles - 1))
        def _():
            total[...] += part

        @pl.when(pl.program_id(0) == tiles - 1)
        def _():
            for t in range(parts):
                mine = slice(t * own, (t + 1) * own)
                outs[t][...] = (total[mine] + part[mine]).astype(LOW)

    fixed = pl.BlockSpec((own, width), lambda j: (0, 0))
    by_tile = pl.BlockSpec((rows, tile), lambda j: (0, j))
    return pl.pallas_call(
        body,
        grid=(tiles,),
        in_specs=[pl.BlockSpec((rows, width), lambda j: (0, 0))]
        + [by_tile] * 2
        + weight_tiles(width, tile, tiles),
        out_specs=[by_tile] * 2 + [fixed] * parts,
        out_shape=[jax.ShapeDtypeStruct((rows, hidden_units), LOW)] * 2
        + [jax.ShapeDtypeStruct((own, width), LOW)] * parts,
        scratch_shapes=[pltpu.VMEM((rows, width), jnp.float32)],
        compiler_params=vmem(50),
        name="feed_forward_back",
    )(rows_low, gate, up, weights, weights, weights)


def down_grad(pieces, mixed):
    count = len(pieces)
    own, width = pieces[0].shape
    rows, columns = mixed.shape
    tile = 512

    def body(*refs):
        rows_ref, out_ref = refs[count + 1], refs[count + 2]

        @pl.when(pl.program_id(0) == 0)
        def _():
            fill_slots(rows_ref, refs[:count])

        place = pl.ds(pl.multiple_of(pl.program_id(0) * tile, tile), tile)
        out_ref[...] = contract(rows_ref[:, place], refs[count][...], 0, 0).astype(LOW)

    return pl.pallas_call(
        body,
        grid=(width // tile,),
        in_specs=[pl.BlockSpec((own, width), lambda j: (0, 0))] * count
        + [pl.BlockSpec((rows, columns), lambda j: (0, 0))],
        out_specs=[
            pl.BlockSpec((rows, width), lambda j: (0, 0)),
            pl.BlockSpec((tile, columns), lambda j: (j, 0)),
        ],
        out_shape=[
            jax.ShapeDtypeStruct((rows, width), LOW),
            jax.ShapeDtypeStruct((width, columns), LOW),
        ],
        compiler_params=vmem(50),
        name="down_grad",
    )(*pieces, mixed)


def weight_grad(left, right, all_columns, place, others=None):
    rows, width = left.shape
    columns = right.shape[1]
    tile = 512

    def body(left_ref, right_ref, *refs):
        refs[-1][...] = contract(left_ref[...], right_ref[...], 0, 0).astype(LOW)

    given = () if others is None else (others,)
    return pl.pallas_call(
        body,
        grid=(width // tile,),
        in_specs=[
            pl.BlockSpec((rows, tile), lambda j: (0, j)),
            pl.BlockSpec((rows, columns), lambda j: (0, 0)),
        ]
        + [pl.BlockSpec(memory_space=pl.ANY)] * len(given),
        out_specs=pl.BlockSpec((tile, columns), lambda j: (j, place)),
        out_shape=jax.ShapeDtypeStruct((width, all_columns), LOW),
        input_output_aliases={2: 0} if given else {},
        compiler_params=vmem(50),
        name="weight_grad",
    )(left, right, *given)


def on_plane(
    tokens,
    w_query,
    w_key,
    w_value,
    w_out,
    w_gate,
    w_up,
    w_down,
    q_gain,
    k_gain,
    attn_gain,
    mlp_gain,
    cotangent,
):
    seqs, length, d_model = tokens.shape
    rows = seqs * length
    tp_rank = lax.axis_index("tp")
    seq_rank = lax.axis_index("seq")
    heads = q_gain.shape[0]
    head_dim = q_gain.shape[1] * 8
    head_span = heads * head_dim
    own_length = length // 4
    own_rows = seqs * own_length
    order = (lax.axis_index("dp") * 4 + seq_rank) ^ jnp.arange(8, dtype=jnp.int32)
    slots = (tp_rank + 4 - jnp.arange(4, dtype=jnp.int32)) % 4

    gain_rows = jnp.concatenate([q_gain, k_gain, attn_gain, mlp_gain], axis=0)
    all_gains = lax.all_to_all(
        jnp.broadcast_to(gain_rows.reshape(1, -1), (8, gain_rows.size)), ("dp", "seq"), 0, 0, tiled=True
    )
    packed = jnp.concatenate([w_gate, w_up, w_down.T], axis=1)
    in_shard = jnp.concatenate([w_query, w_key, w_value], axis=1)
    in_pieces, (all_gains, packed) = gather_plane(
        in_shard, first_step(in_shard), (all_gains, packed)
    )
    all_gains = (
        jnp.transpose(all_gains.reshape((8,) + gain_rows.shape), (1, 0, 2))
        .reshape(gain_rows.shape[0], head_dim)
        .astype(jnp.float32)
    )
    qk_gain = all_gains[: 2 * heads].reshape(1, 2 * head_span)
    feature_rows = d_model // head_dim
    attn_gains = all_gains[2 * heads : 2 * heads + feature_rows].reshape(1, d_model)
    mlp_gains = all_gains[2 * heads + feature_rows :].reshape(1, d_model)
    positions = seq_rank * length + jnp.arange(length, dtype=jnp.int32)
    cosines, sines = rope_tables(positions, head_dim)
    cosines = jnp.concatenate([cosines[:, 0], cosines[:, 0]], axis=-1)
    sines = jnp.concatenate([-sines[:, 0], sines[:, 0]], axis=-1)
    own_tokens = lax.dynamic_slice_in_dim(tokens, tp_rank * own_length, own_length, 1).reshape(
        own_rows, d_model
    )
    grad_out = cotangent.reshape(own_rows, d_model)
    out_rows = lax.all_gather(w_out, "tp", axis=0, tiled=True)

    raw, in_weights = project_in(tokens.reshape(rows, d_model), in_pieces, order)
    out_firsts = first_step(after(w_out, in_pieces[3:5]))
    weights = lax.all_gather(after(packed, (in_pieces[3:5], out_rows)), ("dp", "seq"), axis=0, tiled=True)

    squares = jnp.stack(
        [
            jnp.sum(jnp.square(raw[:, :head_span]), axis=-1),
            jnp.sum(jnp.square(raw[:, head_span : 2 * head_span]), axis=-1),
        ]
    )
    raw, out_firsts = lax.optimization_barrier((raw, out_firsts))
    squares = sum_line(squares)
    squares = squares.reshape(2, seqs, length, 1)
    out_pieces, _ = gather_plane(w_out, out_firsts)
    raw = raw.reshape(seqs, length, 3 * head_span)
    parts = prepare(raw, squares, qk_gain, cosines, sines, heads, head_dim, d_model)
    parts, out_pieces[3:5] = lax.optimization_barrier((parts, out_pieces[3:5]))
    parts = lax.all_to_all(parts, "seq", 0, 0, tiled=True)
    parts, out_pieces = lax.optimization_barrier((parts, out_pieces))
    out_weights = assemble_columns(out_pieces, order)
    context, log_total = attend(parts)
    context = lax.all_to_all(context, "seq", 0, 0, tiled=True)
    context_rows, *attn_slots = project_out(context, out_weights, slots)
    hidden, hidden_low, attn_unit, attn_inv = attn_norm(
        scatter_line(attn_slots)[0], own_tokens, attn_gains
    )
    out_columns = after(out_rows, hidden_low).T
    out_columns = lax.all_gather(out_columns, ("dp", "seq"), axis=0, tiled=True)
    hidden_rows, gate, up, mixed, *mlp_slots = feed_forward(gather_line(hidden_low), weights)
    outputs, grad_mlp, grad_mgain = mlp_norm(
        scatter_line(mlp_slots)[0], hidden, grad_out, mlp_gains
    )
    grad_mlp, out_columns = lax.optimization_barrier((grad_mlp, out_columns))
    grad_mlp_rows, down_part = down_grad(gather_line(grad_mlp), mixed)
    grad_gate, grad_up, *hidden_slots = feed_forward_back(grad_mlp_rows, gate, up, weights, 4)
    units = mixed.shape[1]
    gate_part = weight_grad(hidden_rows, grad_gate, 2 * units, 0)
    gate_up_part = weight_grad(hidden_rows, grad_up, 2 * units, 1, gate_part)
    hidden_sum, (gate_part, gate_up_part) = scatter_line(hidden_slots, (gate_part, gate_up_part))

    def sum_plane(part):
        return lax.optimization_barrier(
            lax.psum_scatter(part, ("dp", "seq"), scatter_dimension=0, tiled=True)
        )

    down_sum = sum_plane(down_part)
    gate_up_sum = sum_plane(gate_up_part)
    ff_sums = ff_totals(gate_up_sum, down_sum)

    grad_hidden, grad_attn, grad_again = attn_norm_back(
        hidden_sum, grad_out, attn_unit, attn_inv, attn_gains
    )
    grad_context = project_out_back(grad_attn, out_columns, heads, head_dim, seqs)
    grad_context = lax.all_to_all(
        grad_context.reshape((16,) + grad_context.shape[2:]), ("seq", "tp"), 0, 0, tiled=True
    ).reshape(grad_context.shape)
    part_grads = attend_back(parts, grad_context, log_total)
    part_grads = lax.all_to_all(part_grads, "seq", 0, 0, tiled=True)
    grad_attn_rows = rows_of(gather_line(grad_attn))
    own_gains = lax.all_to_all(
        jnp.concatenate([grad_again.reshape(4, 4, -1), grad_mgain.reshape(4, 4, -1)], axis=1),
        "tp",
        0,
        0,
        tiled=True,
    )
    part_grads, grad_attn_rows, own_gains = lax.optimization_barrier(
        (part_grads, grad_attn_rows, own_gains)
    )
    own_gains = jnp.sum(own_gains, axis=0)
    scaled, dots, qk_sums = unprepare(part_grads, raw, squares, qk_gain, cosines, sines, d_model)
    dots = sum_line(dots.reshape(2, rows)).reshape(2, seqs, length, 1)
    grad_raw, *token_slots = project_in_back(
        part_grads, scaled, raw, squares, dots, in_weights, slots
    )
    gain_parts = jnp.concatenate([qk_sums.reshape(2, heads, 8, -1), own_gains.reshape(2, heads, 8, -1)])
    gain_parts = jnp.transpose(gain_parts, (2, 0, 1, 3)).reshape(8, -1, 128)
    gain_rows_used = gain_parts.shape[1]
    gain_parts = jnp.pad(
        gain_parts, ((0, 0), (0, d_model // 8 - gain_rows_used), (0, 0))
    ).reshape(d_model, 128)
    far_sent, near = sum_in_plane(
        (tokens.reshape(rows, d_model), grad_attn_rows),
        (grad_raw, context_rows),
        gain_parts,
        order,
    )
    token_sums, (_, near) = scatter_line(token_slots, (far_sent, near))
    in_sums = [near[2], to_neighbour(near[0], 1), to_neighbour(near[1], 2)]
    in_sums, ff_sums = lax.optimization_barrier((in_sums, ff_sums))
    *in_sums, gain_sums = plane_totals(in_sums, head_span)
    grad_tokens = grad_hidden
    for part in token_sums:
        grad_tokens = grad_tokens + part.astype(jnp.float32)

    gain_sums = gain_sums[:gain_rows_used].reshape(4, heads, -1)
    return (
        outputs.reshape(cotangent.shape),
        grad_tokens.reshape(cotangent.shape),
        *in_sums,
        ff_sums[0],
        ff_sums[1],
        ff_sums[2],
        gain_sums[0],
        gain_sums[1],
        gain_sums[2],
        gain_sums[3],
    )


def solution(mesh):
    by_plane = (mesh.shape["dp"], mesh.shape["seq"], mesh.shape["tp"]) == (2, 4, 4)
    return jax.shard_map(
        on_plane if by_plane else on_any_mesh,
        mesh=mesh,
        in_specs=(
            P("dp", "seq", None),
            P(("dp", "seq"), "tp"),
            P(("dp", "seq"), "tp"),
            P(("dp", "seq"), "tp"),
            P("tp", ("dp", "seq")),
            P(("dp", "seq"), "tp"),
            P(("dp", "seq"), "tp"),
            P("tp", ("dp", "seq")),
            P("tp", ("dp", "seq")),
            P("tp", ("dp", "seq")),
            P(None, ("dp", "seq")),
            P(None, ("dp", "seq")),
            P("dp", ("seq", "tp"), None),
        ),
        out_specs=(
            P("dp", ("seq", "tp"), None),
            P("dp", ("seq", "tp"), None),
            P(("dp", "seq"), "tp"),
            P(("dp", "seq"), "tp"),
            P(("dp", "seq"), "tp"),
            P("tp", ("dp", "seq")),
            P(("dp", "seq"), "tp"),
            P(("dp", "seq"), "tp"),
            P("tp", ("dp", "seq")),
            P("tp", ("dp", "seq")),
            P("tp", ("dp", "seq")),
            P("tp", ("dp", "seq")),
            P("tp", ("dp", "seq")),
        ),
        check_vma=False,
    )
```

```python
import math

import jax
import jax.numpy as jnp
from jax import lax
from jax.experimental import pallas as pl
from jax.experimental.pallas import tpu as pltpu
from jax.sharding import PartitionSpec as P

NORM_EPS = 1e-06
ROPE_BASE = 500000.0
MASKED = -1e30


def project(left, right):
    return jnp.dot(left, right, preferred_element_type=jnp.float32)


def project_back(left, right):
    return lax.dot_general(
        left, right, (((left.ndim - 1,), (1,)), ((), ())), preferred_element_type=jnp.float32
    )


def outer_sum(left, right):
    return lax.dot_general(
        left, right, (((0, 1), (0, 1)), ((), ())), preferred_element_type=jnp.float32
    )


def rope_tables(positions, head_dim):
    steps = jnp.arange(head_dim // 2, dtype=jnp.float32)
    freqs = jnp.exp(steps * (-2.0 * math.log(ROPE_BASE) / head_dim))
    angles = positions.astype(jnp.float32)[:, None] * freqs[None, :]
    return (jnp.cos(angles)[:, None, :], jnp.sin(angles)[:, None, :])


def rotate(values, cosines, sines):
    half = values.shape[-1] // 2
    first = values[..., :half]
    second = values[..., half:]
    return jnp.concatenate(
        [first * cosines - second * sines, second * cosines + first * sines], axis=-1
    )


def unrotate(grads, cosines, sines):
    half = grads.shape[-1] // 2
    first = grads[..., :half]
    second = grads[..., half:]
    return jnp.concatenate(
        [first * cosines + second * sines, second * cosines - first * sines], axis=-1
    )


def norm_back(normed, grad_normed, inv_scale, total_dot, d_model):
    return inv_scale * (grad_normed - normed * (total_dot / d_model)[..., None])


def on_any_mesh(
    tokens,
    w_query,
    w_key,
    w_value,
    w_out,
    w_gate,
    w_up,
    w_down,
    q_gain,
    k_gain,
    attn_gain,
    mlp_gain,
    cotangent,
):
    seq_count, local_len, d_model = tokens.shape
    seq_rank = lax.axis_index("seq")
    tp_rank = lax.axis_index("tp")
    own_rows = local_len // lax.axis_size("tp")
    weights_in = (
        lax.all_gather(w_query, ("dp", "seq"), axis=0, tiled=True),
        lax.all_gather(w_key, ("dp", "seq"), axis=0, tiled=True),
        lax.all_gather(w_value, ("dp", "seq"), axis=0, tiled=True),
        lax.all_gather(w_out, ("dp", "seq"), axis=1, tiled=True),
        lax.all_gather(w_gate, ("dp", "seq"), axis=0, tiled=True),
        lax.all_gather(w_up, ("dp", "seq"), axis=0, tiled=True),
        lax.all_gather(w_down, ("dp", "seq"), axis=1, tiled=True),
        lax.all_gather(q_gain, ("dp", "seq"), axis=1, tiled=True),
        lax.all_gather(k_gain, ("dp", "seq"), axis=1, tiled=True),
        lax.all_gather(attn_gain, ("dp", "seq"), axis=1, tiled=True),
        lax.all_gather(mlp_gain, ("dp", "seq"), axis=1, tiled=True),
    )
    (
        full_query,
        full_key,
        full_value,
        full_out,
        full_gate,
        full_up,
        full_down,
        full_qgain,
        full_kgain,
        full_again,
        full_mgain,
    ) = weights_in
    local_heads = full_qgain.shape[0]
    head_dim = full_qgain.shape[1]
    head_span = local_heads * head_dim
    score_scale = head_dim ** (-0.5)
    query_gain = full_qgain.astype(jnp.float32).reshape(head_span)
    key_gain = full_kgain.astype(jnp.float32).reshape(head_span)
    attn_scale_gain = full_again.astype(jnp.float32).reshape(d_model)
    mlp_scale_gain = full_mgain.astype(jnp.float32).reshape(d_model)
    query_raw = project(tokens, full_query)
    key_raw = project(tokens, full_key)
    value_raw = project(tokens, full_value)
    query_sq, key_sq = lax.psum(
        (jnp.sum(query_raw * query_raw, axis=-1), jnp.sum(key_raw * key_raw, axis=-1)), "tp"
    )
    query_inv = lax.rsqrt(query_sq / d_model + NORM_EPS)[..., None]
    key_inv = lax.rsqrt(key_sq / d_model + NORM_EPS)[..., None]
    query_unit = query_raw * query_inv
    key_unit = key_raw * key_inv
    positions = seq_rank * local_len + jnp.arange(local_len, dtype=jnp.int32)
    cosines, sines = rope_tables(positions, head_dim)
    heads_shape = (seq_count, local_len, local_heads, head_dim)
    queries = rotate((query_unit * query_gain).reshape(heads_shape), cosines, sines).astype(
        jnp.bfloat16
    )
    keys_local = (
        rotate((key_unit * key_gain).reshape(heads_shape), cosines, sines)
        .astype(jnp.bfloat16)
        .reshape(seq_count, local_len, head_span)
    )
    values_local = value_raw.astype(jnp.bfloat16)
    all_keys, all_values = (
        lax.all_gather(keys_local, "seq", axis=1, tiled=True),
        lax.all_gather(values_local, "seq", axis=1, tiled=True),
    )
    length = all_keys.shape[1]
    keys_full = all_keys.reshape(seq_count, length, local_heads, head_dim)
    values_full = all_values.reshape(seq_count, length, local_heads, head_dim)
    key_rows = min(512, length)
    block_ids = jnp.arange(length // key_rows, dtype=jnp.int32)

    def key_block(block_index):
        first_key = block_index * key_rows
        key_part = lax.dynamic_slice_in_dim(keys_full, first_key, key_rows, 1)
        value_part = lax.dynamic_slice_in_dim(values_full, first_key, key_rows, 1)
        scores = (
            jnp.einsum("mqhd,mkhd->mhqk", queries, key_part, preferred_element_type=jnp.float32)
            * score_scale
        )
        allowed = (first_key + jnp.arange(key_rows, dtype=jnp.int32))[None, :] <= positions[:, None]
        return (key_part, value_part, jnp.where(allowed, scores, MASKED), allowed)

    def max_step(state, block_index):
        running_max, running_sum = state
        key_part, value_part, scores, allowed = key_block(block_index)
        new_max = jnp.maximum(running_max, jnp.max(scores, axis=-1))
        weights_now = jnp.where(allowed, jnp.exp(scores - new_max[..., None]), 0.0)
        return (
            (new_max, running_sum * jnp.exp(running_max - new_max) + jnp.sum(weights_now, axis=-1)),
            None,
        )

    stat_shape = (seq_count, local_heads, local_len)
    final_state, unused = lax.scan(
        max_step,
        (jnp.full(stat_shape, MASKED, jnp.float32), jnp.zeros(stat_shape, jnp.float32)),
        block_ids,
    )
    log_total = (final_state[0] + jnp.log(final_state[1]))[..., None]

    def context_step(context, block_index):
        key_part, value_part, scores, allowed = key_block(block_index)
        probs = jnp.where(allowed, jnp.exp(scores - log_total), 0.0).astype(jnp.bfloat16)
        return (
            context
            + jnp.einsum("mhqk,mkhd->mqhd", probs, value_part, preferred_element_type=jnp.float32),
            None,
        )

    context, unused = lax.scan(context_step, jnp.zeros(heads_shape, jnp.float32), block_ids)
    context_low = context.astype(jnp.bfloat16).reshape(seq_count, local_len, head_span)
    attn_out = lax.psum_scatter(
        project(context_low, full_out), "tp", scatter_dimension=1, tiled=True
    )
    attn_inv = lax.rsqrt(jnp.mean(attn_out * attn_out, axis=-1, keepdims=True) + NORM_EPS)
    attn_unit = attn_out * attn_inv
    own_tokens = lax.dynamic_slice_in_dim(tokens, tp_rank * own_rows, own_rows, 1).astype(
        jnp.float32
    )
    hidden = own_tokens + attn_unit * attn_scale_gain
    hidden_all = lax.all_gather(hidden.astype(jnp.bfloat16), "tp", axis=1, tiled=True)
    gate_act = project(hidden_all, full_gate)
    up_act = project(hidden_all, full_up)
    gate_sig = jax.nn.sigmoid(gate_act)
    mixed = (gate_act * gate_sig * up_act).astype(jnp.bfloat16)
    mlp_out = lax.psum_scatter(project(mixed, full_down), "tp", scatter_dimension=1, tiled=True)
    mlp_inv = lax.rsqrt(jnp.mean(mlp_out * mlp_out, axis=-1, keepdims=True) + NORM_EPS)
    mlp_unit = mlp_out * mlp_inv
    outputs = (hidden + mlp_unit * mlp_scale_gain).astype(jnp.bfloat16)
    weights_back = (
        lax.all_gather(w_query, ("dp", "seq"), axis=0, tiled=True),
        lax.all_gather(w_key, ("dp", "seq"), axis=0, tiled=True),
        lax.all_gather(w_value, ("dp", "seq"), axis=0, tiled=True),
        lax.all_gather(w_out, ("dp", "seq"), axis=1, tiled=True),
        lax.all_gather(w_gate, ("dp", "seq"), axis=0, tiled=True),
        lax.all_gather(w_up, ("dp", "seq"), axis=0, tiled=True),
        lax.all_gather(w_down, ("dp", "seq"), axis=1, tiled=True),
    )
    back_query, back_key, back_value, back_out, back_gate, back_up, back_down = weights_back
    grad_out = cotangent.astype(jnp.float32)
    grad_mgain = jnp.sum(grad_out * mlp_unit, axis=(0, 1))
    mlp_scaled = grad_out * mlp_scale_gain
    grad_mlp = norm_back(
        mlp_unit, mlp_scaled, mlp_inv, jnp.sum(mlp_scaled * mlp_unit, axis=-1), d_model
    ).astype(jnp.bfloat16)
    grad_mlp_all = lax.all_gather(grad_mlp, "tp", axis=1, tiled=True)
    grad_wdown = outer_sum(mixed, grad_mlp_all)
    grad_mixed = project_back(grad_mlp_all, back_down)
    grad_gate = (grad_mixed * up_act * gate_sig * (1.0 + gate_act * (1.0 - gate_sig))).astype(
        jnp.bfloat16
    )
    grad_up = (grad_mixed * gate_act * gate_sig).astype(jnp.bfloat16)
    grad_wgate = outer_sum(hidden_all, grad_gate)
    grad_wup = outer_sum(hidden_all, grad_up)
    hidden_part = project_back(grad_gate, back_gate) + project_back(grad_up, back_up)
    hidden_sum, grad_mgain_part = (
        lax.psum_scatter(hidden_part, "tp", scatter_dimension=1, tiled=True),
        lax.psum_scatter(grad_mgain.reshape(-1, head_dim), "tp", scatter_dimension=0, tiled=True),
    )
    grad_hidden = grad_out + hidden_sum
    grad_again = jnp.sum(grad_hidden * attn_unit, axis=(0, 1))
    attn_scaled = grad_hidden * attn_scale_gain
    grad_attn = norm_back(
        attn_unit, attn_scaled, attn_inv, jnp.sum(attn_scaled * attn_unit, axis=-1), d_model
    ).astype(jnp.bfloat16)
    grad_attn_all = lax.all_gather(grad_attn, "tp", axis=1, tiled=True)
    grad_wout = outer_sum(context_low, grad_attn_all)
    grad_context = project_back(grad_attn_all, back_out).astype(jnp.bfloat16).reshape(heads_shape)

    def delta_step(delta, block_index):
        key_part, value_part, scores, allowed = key_block(block_index)
        probs = jnp.exp(scores - log_total)
        grad_probs = jnp.einsum(
            "mqhd,mkhd->mhqk", grad_context, value_part, preferred_element_type=jnp.float32
        )
        return (delta + jnp.sum(probs * grad_probs, axis=-1), None)

    delta, unused = lax.scan(delta_step, jnp.zeros(stat_shape, jnp.float32), block_ids)

    def score_grads(block_index):
        key_part, value_part, scores, allowed = key_block(block_index)
        probs = jnp.exp(scores - log_total)
        grad_probs = jnp.einsum(
            "mqhd,mkhd->mhqk", grad_context, value_part, preferred_element_type=jnp.float32
        )
        grad_scores = (probs * (grad_probs - delta[..., None])).astype(jnp.bfloat16)
        return (key_part, probs, grad_scores)

    def grad_step(grad_queries, block_index):
        key_part, probs, grad_scores = score_grads(block_index)
        grad_queries = grad_queries + jnp.einsum(
            "mhqk,mkhd->mqhd", grad_scores, key_part, preferred_element_type=jnp.float32
        )
        grad_keys = (
            jnp.einsum("mhqk,mqhd->kmhd", grad_scores, queries, preferred_element_type=jnp.float32)
            * score_scale
        )
        grad_values = jnp.einsum(
            "mhqk,mqhd->kmhd",
            probs.astype(jnp.bfloat16),
            grad_context,
            preferred_element_type=jnp.float32,
        )
        both_terms = jnp.concatenate(
            [
                grad_keys.reshape(key_rows, seq_count, head_span),
                grad_values.reshape(key_rows, seq_count, head_span),
            ],
            axis=-1,
        )
        return (grad_queries, both_terms)

    grad_queries, key_terms = lax.scan(grad_step, jnp.zeros(heads_shape, jnp.float32), block_ids)
    key_value_grads = lax.psum_scatter(
        key_terms.reshape(length, seq_count, 2 * head_span).astype(jnp.bfloat16),
        "seq",
        scatter_dimension=0,
        tiled=True,
    ).astype(jnp.float32)
    key_value_grads = jnp.transpose(key_value_grads, (1, 0, 2))
    grad_keys_own = key_value_grads[..., :head_span].reshape(heads_shape)
    grad_values_own = key_value_grads[..., head_span:].astype(jnp.bfloat16)
    query_grad_unit = unrotate(grad_queries * score_scale, cosines, sines).reshape(
        seq_count, local_len, head_span
    )
    key_grad_unit = unrotate(grad_keys_own, cosines, sines).reshape(seq_count, local_len, head_span)
    grad_qgain = jnp.sum(query_grad_unit * query_unit, axis=(0, 1))
    grad_kgain = jnp.sum(key_grad_unit * key_unit, axis=(0, 1))
    query_scaled = query_grad_unit * query_gain
    key_scaled = key_grad_unit * key_gain
    query_dot, key_dot = lax.psum(
        (jnp.sum(query_scaled * query_unit, axis=-1), jnp.sum(key_scaled * key_unit, axis=-1)), "tp"
    )
    grad_qraw = norm_back(query_unit, query_scaled, query_inv, query_dot, d_model).astype(
        jnp.bfloat16
    )
    grad_kraw = norm_back(key_unit, key_scaled, key_inv, key_dot, d_model).astype(jnp.bfloat16)
    grad_wquery = outer_sum(tokens, grad_qraw)
    grad_wkey = outer_sum(tokens, grad_kraw)
    grad_wvalue = outer_sum(tokens, grad_values_own)
    token_part = (
        project_back(grad_qraw, back_query)
        + project_back(grad_kraw, back_key)
        + project_back(grad_values_own, back_value)
    )
    token_sum, grad_again_part = (
        lax.psum_scatter(
            token_part.astype(jnp.bfloat16), "tp", scatter_dimension=1, tiled=True
        ).astype(jnp.float32),
        lax.psum_scatter(
            grad_again.reshape(-1, head_dim).astype(jnp.bfloat16),
            "tp",
            scatter_dimension=0,
            tiled=True,
        ).astype(jnp.float32),
    )
    grad_tokens = grad_hidden + token_sum
    summed = (
        lax.psum_scatter(
            grad_wquery.astype(jnp.bfloat16), ("dp", "seq"), scatter_dimension=0, tiled=True
        ).astype(jnp.float32),
        lax.psum_scatter(
            grad_wkey.astype(jnp.bfloat16), ("dp", "seq"), scatter_dimension=0, tiled=True
        ).astype(jnp.float32),
        lax.psum_scatter(
            grad_wvalue.astype(jnp.bfloat16), ("dp", "seq"), scatter_dimension=0, tiled=True
        ).astype(jnp.float32),
        lax.psum_scatter(
            grad_wout.astype(jnp.bfloat16), ("dp", "seq"), scatter_dimension=1, tiled=True
        ).astype(jnp.float32),
        lax.psum_scatter(
            grad_wgate.astype(jnp.bfloat16), ("dp", "seq"), scatter_dimension=0, tiled=True
        ).astype(jnp.float32),
        lax.psum_scatter(
            grad_wup.astype(jnp.bfloat16), ("dp", "seq"), scatter_dimension=0, tiled=True
        ).astype(jnp.float32),
        lax.psum_scatter(
            grad_wdown.astype(jnp.bfloat16), ("dp", "seq"), scatter_dimension=1, tiled=True
        ).astype(jnp.float32),
        lax.psum_scatter(
            grad_qgain.reshape(local_heads, head_dim).astype(jnp.bfloat16),
            ("dp", "seq"),
            scatter_dimension=1,
            tiled=True,
        ).astype(jnp.float32),
        lax.psum_scatter(
            grad_kgain.reshape(local_heads, head_dim).astype(jnp.bfloat16),
            ("dp", "seq"),
            scatter_dimension=1,
            tiled=True,
        ).astype(jnp.float32),
        lax.psum_scatter(
            grad_again_part.astype(jnp.bfloat16), ("dp", "seq"), scatter_dimension=1, tiled=True
        ).astype(jnp.float32),
        lax.psum_scatter(
            grad_mgain_part.astype(jnp.bfloat16), ("dp", "seq"), scatter_dimension=1, tiled=True
        ).astype(jnp.float32),
    )
    (
        sum_query,
        sum_key,
        sum_value,
        sum_out,
        sum_gate,
        sum_up,
        sum_down,
        sum_qgain,
        sum_kgain,
        sum_again,
        sum_mgain,
    ) = summed
    return (
        outputs,
        grad_tokens,
        sum_query,
        sum_key,
        sum_value,
        sum_out,
        sum_gate,
        sum_up,
        sum_down,
        sum_qgain,
        sum_kgain,
        sum_again,
        sum_mgain,
    )


LOW = jnp.bfloat16


def vmem(mebibytes):
    return pltpu.CompilerParams(vmem_limit_bytes=mebibytes * 1024 * 1024)


def to_neighbour(values, flip):
    return lax.ppermute(values, "seq", [(i, i ^ flip) for i in range(4)])


def to_core(values):
    return lax.ppermute(values, "dp", [(0, 1), (1, 0)])


def after(values, done):
    return lax.optimization_barrier((values, done))[0]


def first_step(shard):
    return to_neighbour(shard, 1), to_neighbour(shard, 2)


def gather_plane(shard, firsts, meanwhile=()):
    half = shard.shape[0] // 2
    (from_one, from_two), meanwhile = lax.optimization_barrier((firsts, meanwhile))
    far = [to_neighbour(from_two[:half], 1), to_neighbour(from_one[half:], 2)]
    near = [shard, from_one, from_two]
    far, other = lax.optimization_barrier((far, [to_core(piece) for piece in near]))
    return near + far + other + [to_core(piece) for piece in far], meanwhile


def place_piece(out_ref, order_ref, k, piece, axis):
    block = piece.shape[axis]
    if axis == 0 and k % 5 > 2:
        block *= 2
    first = piece.shape[0] if k % 5 == 4 else 0
    start = order_ref[(k // 5) * 4 + min(k % 5, 3)] * block
    if axis == 0:
        out_ref[pl.ds(pl.multiple_of(start + first, piece.shape[0]), piece.shape[0])] = piece
    else:
        out_ref[first : first + piece.shape[0], pl.ds(pl.multiple_of(start, block), block)] = piece


def assemble_columns(pieces, order):
    height, block = pieces[0].shape

    def body(order_ref, *refs):
        for k in range(10):
            place_piece(refs[10], order_ref, k, refs[k][...], 1)

    return pl.pallas_call(
        body,
        in_specs=[pl.BlockSpec(memory_space=pltpu.SMEM)]
        + [pl.BlockSpec(memory_space=pltpu.VMEM)] * 10,
        out_specs=pl.BlockSpec(memory_space=pltpu.VMEM),
        out_shape=jax.ShapeDtypeStruct((height, 8 * block), pieces[0].dtype),
        compiler_params=vmem(50),
        name="assemble_columns",
    )(order, *pieces)


def project_in(rows_low, pieces, order):
    rows, width = rows_low.shape
    columns = pieces[0].shape[1]
    tile = columns // 3

    def body(order_ref, rows_ref, *refs):
        for k in range(10):
            place_piece(refs[11], order_ref, k, refs[k][...], 0)
        refs[10][...] = jnp.dot(rows_ref[...], refs[11][...], preferred_element_type=jnp.float32)

    return pl.pallas_call(
        body,
        grid_spec=pltpu.PrefetchScalarGridSpec(
            num_scalar_prefetch=1,
            grid=(3,),
            in_specs=[pl.BlockSpec((rows, width), lambda j, o: (0, 0))]
            + [pl.BlockSpec((piece.shape[0], tile), lambda j, o: (0, j)) for piece in pieces],
            out_specs=[
                pl.BlockSpec((rows, tile), lambda j, o: (0, j)),
                pl.BlockSpec((width, tile), lambda j, o: (0, j)),
            ],
        ),
        out_shape=[
            jax.ShapeDtypeStruct((rows, columns), jnp.float32),
            jax.ShapeDtypeStruct((width, columns), LOW),
        ],
        compiler_params=vmem(50),
        name="project_in",
    )(order, rows_low, *pieces)


def grad_blocks(lefts, rights, extra, order, blocks, received=None, far=None):
    rows, d_model = lefts[0].shape
    block = d_model // 8
    half = block // 2
    count = len(blocks)
    width = sum(right.shape[1] for right in rights) + extra.shape[1]
    fresh = received is None

    def body(order_ref, *refs):
        left_refs, right_refs = refs[: len(lefts)], refs[len(lefts) : len(lefts) + len(rights)]
        extra_ref, rest = refs[len(lefts) + len(rights)], refs[len(lefts) + len(rights) + 1 :]
        first = 0
        for k in range(len(lefts) + 1):
            if k < len(lefts):
                total = contract(left_refs[k][...], right_refs[k][...], 0, 0)
            else:
                total = extra_ref[...]
            columns = slice(first, first + total.shape[1])
            first += total.shape[1]
            if fresh:
                rest[0][:, columns] = total.astype(LOW)
                continue
            total = total + rest[0][:, columns].astype(jnp.float32)
            if far is None:
                rest[1][:, columns] = total[:half].astype(LOW)
                rest[2][:, columns] = total[half:].astype(LOW)
                continue
            low, high, outs = rest[1], rest[2], rest[3:]

            @pl.when(pl.program_id(0) == 0)
            def _(total=total, columns=columns):
                outs[0][:half, columns] = total[:half].astype(LOW)
                outs[0][half:, columns] = (
                    total[half:] + high[:, columns].astype(jnp.float32)
                ).astype(LOW)

            @pl.when(pl.program_id(0) == 1)
            def _(total=total, columns=columns):
                outs[1][:half, columns] = (
                    total[:half] + low[:, columns].astype(jnp.float32)
                ).astype(LOW)
                outs[1][half:, columns] = total[half:].astype(LOW)

            @pl.when(pl.program_id(0) == 2)
            def _(total=total, columns=columns):
                outs[2][:, columns] = total.astype(LOW)

    def pick(j):
        value = blocks[0]
        for i, entry in enumerate(blocks[1:]):
            value = jnp.where(j > i, entry, value)
        return value

    def fixed(height):
        return pl.BlockSpec((height, width), lambda j, o: (0, 0))

    in_specs = [pl.BlockSpec((rows, block), lambda j, o: (0, o[pick(j)])) for _ in lefts]
    in_specs += [pl.BlockSpec(right.shape, lambda j, o: (0, 0)) for right in rights]
    in_specs.append(pl.BlockSpec((block, extra.shape[1]), lambda j, o: (o[pick(j)], 0)))
    more = ()
    if fresh:
        out_specs = [pl.BlockSpec((block, width), lambda j, o: (j, 0))]
        out_shape = [jax.ShapeDtypeStruct((count * block, width), LOW)]
    else:
        in_specs.append(pl.BlockSpec((block, width), lambda j, o: (pick(j), 0)))
        more = (received,)
        if far is None:
            out_specs = [fixed(half)] * 2
            out_shape = [jax.ShapeDtypeStruct((half, width), LOW)] * 2
        else:
            more += tuple(far)
            in_specs += [fixed(half)] * 2
            out_specs = [fixed(block)] * 3
            out_shape = [jax.ShapeDtypeStruct((block, width), LOW)] * 3
    return pl.pallas_call(
        body,
        grid_spec=pltpu.PrefetchScalarGridSpec(
            num_scalar_prefetch=1, grid=(count,), in_specs=in_specs, out_specs=out_specs
        ),
        out_shape=out_shape,
        compiler_params=vmem(24),
        cost_estimate=pl.CostEstimate(
            flops=2 * rows * block * count * width,
            bytes_accessed=4 * block * count * width + 2 * rows * (width + d_model),
            transcendentals=0,
        ),
        name="grad_blocks",
    )(order, *lefts, *rights, extra, *more)


def sum_in_plane(*parts):
    (sent,) = grad_blocks(*parts, (4, 5, 6, 7))
    received = to_core(sent)
    sent = grad_blocks(*parts, (3,), received)
    far = [to_neighbour(sent[0], 1), to_neighbour(sent[1], 2)]
    return sent, grad_blocks(*parts, (1, 2, 0), received, far)


def gather_line(own):
    up, down = own, own
    ups, downs = [], []
    for t in range(1, 4):
        up = lax.ppermute(up, "tp", [(i, i + 1) for i in range(t - 1, 3)])
        down = lax.ppermute(down, "tp", [(i, i - 1) for i in range(1, 5 - t)])
        ups.append(up)
        downs.append(down)
    return [own] + ups + downs


def scatter_line(slots, meanwhile=((), ())):
    meanwhile = list(meanwhile)
    def added(mine, got):
        return (mine.astype(jnp.float32) + got.astype(jnp.float32)).astype(LOW)

    up, down = slots[1], slots[3]
    for t in range(1, 4):
        up = lax.ppermute(up, "tp", [(i, i + 1) for i in range(t)])
        down = lax.ppermute(down, "tp", [(i, i - 1) for i in range(4 - t, 4)])
        if t < 3:
            up, down, meanwhile[t - 1] = lax.optimization_barrier((up, down, meanwhile[t - 1]))
            up = added(slots[t + 1], up)
            down = added(slots[3 - t], down)
    return (slots[0], up, down), meanwhile


def sum_line(values):
    flat = lax.optimization_barrier(values.reshape(1, -1, 128))
    flat = lax.all_to_all(jnp.broadcast_to(flat, (4,) + flat.shape[1:]), "tp", 0, 0, tiled=True)
    return jnp.sum(lax.optimization_barrier(flat), axis=0)


def contract(left, right, left_dim, right_dim):
    return lax.dot_general(
        left, right, (((left_dim,), (right_dim,)), ((), ())), preferred_element_type=jnp.float32
    )


def turned(values, cosines, sines):
    return values * cosines + pltpu.roll(values, values.shape[-1] // 2, axis=1) * sines


def inverse_norm(squares, d_model):
    return lax.rsqrt(squares * (1.0 / d_model) + NORM_EPS)


def prepare(raw, squares, gains, cosines, sines, heads, head_dim, d_model):
    seqs, length, _ = raw.shape
    own = length // 4
    rows = seqs * own
    span = heads * head_dim

    def body(raw_ref, square_ref, gain_ref, cos_ref, sin_ref, out_ref):
        cosine = jnp.concatenate([cos_ref[...]] * seqs, axis=0)
        sine = jnp.concatenate([sin_ref[...]] * seqs, axis=0)
        for t in range(2):
            inv = inverse_norm(square_ref[t].reshape(rows, 1), d_model)
            for h in range(heads):
                columns = slice(t * span + h * head_dim, t * span + (h + 1) * head_dim)
                normed = raw_ref[:, :, columns].reshape(rows, head_dim) * inv * gain_ref[:, columns]
                out_ref[h, t] = (
                    turned(normed, cosine, sine).astype(LOW).reshape(seqs, own, head_dim)
                )
        for h in range(heads):
            columns = slice(2 * span + h * head_dim, 2 * span + (h + 1) * head_dim)
            out_ref[h, 2] = raw_ref[:, :, columns].astype(LOW)

    return pl.pallas_call(
        body,
        grid=(4,),
        in_specs=[
            pl.BlockSpec((seqs, own, 3 * span), lambda t: (0, t, 0)),
            pl.BlockSpec((2, seqs, own, 1), lambda t: (0, 0, t, 0)),
            pl.BlockSpec((1, 2 * span), lambda t: (0, 0)),
            pl.BlockSpec((own, head_dim), lambda t: (t, 0)),
            pl.BlockSpec((own, head_dim), lambda t: (t, 0)),
        ],
        out_specs=pl.BlockSpec((heads, 3, seqs, own, head_dim), lambda t: (0, 0, 0, t, 0)),
        out_shape=jax.ShapeDtypeStruct((heads, 3, seqs, length, head_dim), LOW),
        compiler_params=vmem(50),
        name="prepare",
    )(raw, squares, gains, cosines, sines)


def scores_of(left, right):
    return lax.dot_general(
        left, right, (((1,), (1,)), ((), ())), preferred_element_type=jnp.float32
    )


def causal(scores, first):
    rows = lax.broadcasted_iota(jnp.int32, scores.shape, 0) + first
    columns = lax.broadcasted_iota(jnp.int32, scores.shape, 1)
    return columns <= rows


def attend(parts):
    blocks, _, seqs, length, head_dim = parts.shape
    score_scale = head_dim ** (-0.5)

    def body(parts_ref, out_ref, log_ref):
        for i in range(blocks):
            span = (i + 1) * length
            keys = parts_ref[: i + 1, 1, 0].reshape(span, head_dim)
            values = parts_ref[: i + 1, 2, 0].reshape(span, head_dim)
            scores = scores_of(parts_ref[i, 0, 0], keys) * score_scale
            scores = jnp.where(causal(scores, i * length), scores, MASKED)
            top = jnp.max(scores, axis=-1, keepdims=True)
            weights = jnp.exp(scores - top)
            total = jnp.sum(weights, axis=-1, keepdims=True)
            probs = (weights * (1.0 / total)).astype(LOW)
            out_ref[i, 0] = jnp.dot(probs, values, preferred_element_type=jnp.float32).astype(LOW)
            log_ref[i, 0] = top + jnp.log(total)

    return pl.pallas_call(
        body,
        grid=(seqs,),
        in_specs=[pl.BlockSpec((blocks, 3, 1, length, head_dim), lambda m: (0, 0, m, 0, 0))],
        out_specs=[
            pl.BlockSpec((blocks, 1, length, head_dim), lambda m: (0, m, 0, 0)),
            pl.BlockSpec((blocks, 1, length, 1), lambda m: (0, m, 0, 0)),
        ],
        out_shape=[
            jax.ShapeDtypeStruct((blocks, seqs, length, head_dim), LOW),
            jax.ShapeDtypeStruct((blocks, seqs, length, 1), jnp.float32),
        ],
        compiler_params=vmem(50),
        name="attend",
    )(parts)


def attend_back(parts, grad_context, log_total):
    blocks, _, seqs, length, head_dim = parts.shape
    score_scale = head_dim ** (-0.5)

    def body(parts_ref, grad_ref, log_ref, out_ref, keys_sum, values_sum):
        keys_sum[...] = jnp.zeros_like(keys_sum)
        values_sum[...] = jnp.zeros_like(values_sum)
        for i in range(blocks):
            span = (i + 1) * length
            queries = parts_ref[i, 0, 0]
            keys = parts_ref[: i + 1, 1, 0].reshape(span, head_dim)
            values = parts_ref[: i + 1, 2, 0].reshape(span, head_dim)
            grads = grad_ref[i, :, 0].reshape(length, head_dim)
            scores = scores_of(queries, keys) * score_scale
            probs = jnp.where(causal(scores, i * length), jnp.exp(scores - log_ref[i, 0]), 0.0)
            grad_probs = scores_of(grads, values)
            delta = jnp.sum(probs * grad_probs, axis=-1, keepdims=True)
            grad_scores = (probs * (grad_probs - delta)).astype(LOW)
            out_ref[i, 0, 0] = (
                jnp.dot(grad_scores, keys, preferred_element_type=jnp.float32) * score_scale
            ).astype(LOW)
            keys_sum[:span] += contract(grad_scores, queries, 0, 0)
            values_sum[:span] += contract(probs.astype(LOW), grads, 0, 0)
        out_ref[:, 1, 0] = (
            (keys_sum[...] * score_scale).astype(LOW).reshape(blocks, length, head_dim)
        )
        out_ref[:, 2, 0] = values_sum[...].astype(LOW).reshape(blocks, length, head_dim)

    whole = pl.BlockSpec((blocks, 3, 1, length, head_dim), lambda m: (0, 0, m, 0, 0))
    return pl.pallas_call(
        body,
        grid=(seqs,),
        in_specs=[
            whole,
            pl.BlockSpec((blocks, 4, 1, length // 4, head_dim), lambda m: (0, 0, m, 0, 0)),
            pl.BlockSpec((blocks, 1, length, 1), lambda m: (0, m, 0, 0)),
        ],
        out_specs=whole,
        out_shape=jax.ShapeDtypeStruct(parts.shape, LOW),
        scratch_shapes=[
            pltpu.VMEM((blocks * length, head_dim), jnp.float32),
            pltpu.VMEM((blocks * length, head_dim), jnp.float32),
        ],
        compiler_params=vmem(50),
        name="attend_back",
    )(parts, grad_context, log_total)


def project_out(context, weights, slots):
    heads, seqs, length, head_dim = context.shape
    span, width = weights.shape
    own = length // 4
    own_rows = seqs * own
    tile = width // 2

    def body(slots_ref, context_ref, weight_ref, rows_ref, *outs):
        @pl.when(pl.program_id(0) == 0)
        def _():
            for t in range(4):
                place = pl.ds(pl.multiple_of(slots_ref[t] * own, own), own)
                for h in range(heads):
                    rows_ref[
                        t * own_rows : (t + 1) * own_rows, h * head_dim : (h + 1) * head_dim
                    ] = context_ref[h, :, place].reshape(own_rows, head_dim)

        product = jnp.dot(rows_ref[...], weight_ref[...], preferred_element_type=jnp.float32)
        for t in range(4):
            outs[t][...] = product[t * own_rows : (t + 1) * own_rows].astype(LOW)

    return pl.pallas_call(
        body,
        grid_spec=pltpu.PrefetchScalarGridSpec(
            num_scalar_prefetch=1,
            grid=(2,),
            in_specs=[
                pl.BlockSpec(context.shape, lambda j, s: (0, 0, 0, 0)),
                pl.BlockSpec((span, tile), lambda j, s: (0, j)),
            ],
            out_specs=[pl.BlockSpec((4 * own_rows, span), lambda j, s: (0, 0))]
            + [pl.BlockSpec((own_rows, tile), lambda j, s: (0, j))] * 4,
        ),
        out_shape=[jax.ShapeDtypeStruct((4 * own_rows, span), LOW)]
        + [jax.ShapeDtypeStruct((own_rows, width), LOW)] * 4,
        compiler_params=vmem(50),
        name="project_out",
    )(slots, context, weights)


def project_out_back(grads, weights, heads, head_dim, seqs):
    rows, width = grads.shape
    own = rows // seqs
    span = heads * head_dim

    def body(grad_ref, weight_ref, out_ref):
        product = jnp.dot(grad_ref[...], weight_ref[...], preferred_element_type=jnp.float32)
        for h in range(heads):
            out_ref[h, 0] = (
                product[:, h * head_dim : (h + 1) * head_dim].astype(LOW).reshape(seqs, own, head_dim)
            )

    return pl.pallas_call(
        body,
        grid=(4,),
        in_specs=[
            pl.BlockSpec((rows, width), lambda j: (0, 0)),
            pl.BlockSpec((width, span), lambda j: (0, j)),
        ],
        out_specs=pl.BlockSpec((heads, 1, seqs, own, head_dim), lambda j: (0, j, 0, 0, 0)),
        out_shape=jax.ShapeDtypeStruct((heads, 4, seqs, own, head_dim), LOW),
        compiler_params=vmem(50),
        name="project_out_back",
    )(grads, weights)


def rows_of(pieces):
    own, width = pieces[0].shape

    def body(*refs):
        fill_slots(refs[7], refs[:7])

    return pl.pallas_call(
        body,
        out_shape=jax.ShapeDtypeStruct((4 * own, width), LOW),
        compiler_params=vmem(14),
        name="rows_of",
    )(*pieces)


def unprepare(grads, raw, squares, gains, cosines, sines, d_model):
    heads, _, seqs, length, head_dim = grads.shape
    own = length // 4
    rows = seqs * own
    span = heads * head_dim

    def body(
        grad_ref, raw_ref, square_ref, gain_ref, cos_ref, sin_ref, scaled_ref, dot_ref, sum_ref
    ):
        cosine = jnp.concatenate([cos_ref[...]] * seqs, axis=0)
        sine = -jnp.concatenate([sin_ref[...]] * seqs, axis=0)

        @pl.when(pl.program_id(0) == 0)
        def _():
            sum_ref[...] = jnp.zeros_like(sum_ref)

        for t in range(2):
            inv = inverse_norm(square_ref[t].reshape(rows, 1), d_model)
            total = jnp.zeros((rows, head_dim), jnp.float32)
            for h in range(heads):
                columns = slice(t * span + h * head_dim, t * span + (h + 1) * head_dim)
                back = turned(
                    grad_ref[h, t].reshape(rows, head_dim).astype(jnp.float32), cosine, sine
                )
                along = back * (raw_ref[:, :, columns].reshape(rows, head_dim) * inv)
                sum_ref[:, columns] += jnp.sum(along, axis=0, keepdims=True)
                scaled_ref[:, :, columns] = (back * gain_ref[:, columns]).reshape(
                    seqs, own, head_dim
                )
                total += along * gain_ref[:, columns]
            dot_ref[t] = jnp.sum(total, axis=-1, keepdims=True).reshape(seqs, own, 1)

    return pl.pallas_call(
        body,
        grid=(4,),
        in_specs=[
            pl.BlockSpec((heads, 3, seqs, own, head_dim), lambda t: (0, 0, 0, t, 0)),
            pl.BlockSpec((seqs, own, 3 * span), lambda t: (0, t, 0)),
            pl.BlockSpec((2, seqs, own, 1), lambda t: (0, 0, t, 0)),
            pl.BlockSpec((1, 2 * span), lambda t: (0, 0)),
            pl.BlockSpec((own, head_dim), lambda t: (t, 0)),
            pl.BlockSpec((own, head_dim), lambda t: (t, 0)),
        ],
        out_specs=[
            pl.BlockSpec((seqs, own, 2 * span), lambda t: (0, t, 0)),
            pl.BlockSpec((2, seqs, own, 1), lambda t: (0, 0, t, 0)),
            pl.BlockSpec((1, 2 * span), lambda t: (0, 0)),
        ],
        out_shape=[
            jax.ShapeDtypeStruct((seqs, length, 2 * span), jnp.float32),
            jax.ShapeDtypeStruct((2, seqs, length, 1), jnp.float32),
            jax.ShapeDtypeStruct((1, 2 * span), jnp.float32),
        ],
        compiler_params=vmem(14),
        name="unprepare",
    )(grads, raw, squares, gains, cosines, sines)


def project_in_back(grads, scaled, raw, squares, dots, weights, slots):
    heads, _, seqs, length, head_dim = grads.shape
    own = length // 4
    own_rows = seqs * own
    rows = seqs * length
    span = heads * head_dim
    d_model = weights.shape[0]
    tile = d_model // 4

    def body(
        slots_ref, grad_ref, scaled_ref, raw_ref, square_ref, dot_ref, weight_ref, rows_ref, *refs
    ):
        outs, product = refs[:4], refs[4]

        @pl.when(pl.program_id(0) == 0)
        def _():
            for k in range(2):
                columns = slice(k * span, (k + 1) * span)
                inv = inverse_norm(square_ref[k].reshape(rows, 1), d_model)
                mean = dot_ref[k].reshape(rows, 1) * (1.0 / d_model)
                unit = raw_ref[:, :, columns].reshape(rows, span) * inv
                rows_ref[:, columns] = (
                    inv * (scaled_ref[:, :, columns].reshape(rows, span) - unit * mean)
                ).astype(LOW)
            for h in range(heads):
                columns = slice(2 * span + h * head_dim, 2 * span + (h + 1) * head_dim)
                rows_ref[:, columns] = grad_ref[h, 0].reshape(rows, head_dim)

        product[...] = scores_of(rows_ref[...], weight_ref[...]).reshape(seqs, length, tile)
        for t in range(4):
            place = pl.ds(pl.multiple_of(slots_ref[t] * own, own), own)
            outs[t][...] = product[:, place].reshape(own_rows, tile).astype(LOW)

    flat = pl.BlockSpec((2, seqs, length, 1), lambda j, s: (0, 0, 0, 0))
    return pl.pallas_call(
        body,
        grid_spec=pltpu.PrefetchScalarGridSpec(
            num_scalar_prefetch=1,
            grid=(4,),
            in_specs=[
                pl.BlockSpec((heads, 1, seqs, length, head_dim), lambda j, s: (0, 2, 0, 0, 0)),
                pl.BlockSpec((seqs, length, 2 * span), lambda j, s: (0, 0, 0)),
                pl.BlockSpec((seqs, length, 2 * span), lambda j, s: (0, 0, 0)),
                flat,
                flat,
                pl.BlockSpec((tile, 3 * span), lambda j, s: (j, 0)),
            ],
            out_specs=[pl.BlockSpec((rows, 3 * span), lambda j, s: (0, 0))]
            + [pl.BlockSpec((own_rows, tile), lambda j, s: (0, j))] * 4,
            scratch_shapes=[pltpu.VMEM((seqs, length, tile), jnp.float32)],
        ),
        out_shape=[jax.ShapeDtypeStruct((rows, 3 * span), LOW)]
        + [jax.ShapeDtypeStruct((own_rows, d_model), LOW)] * 4,
        compiler_params=vmem(32),
        name="project_in_back",
    )(slots, grads, scaled, raw, squares, dots, weights)


def fill_slots(rows_ref, refs):
    own = refs[0].shape[0]
    seqs = len(refs) // 7
    for m in range(seqs):
        mine = refs[7 * m : 7 * m + 7]
        rows_ref[m * own : (m + 1) * own] = mine[0][...]
        for t in range(1, 4):
            first = (t * seqs + m) * own
            rows_ref[first : first + own] = mine[t][...] + mine[7 - t][...]


def attn_norm(parts, tokens, gains):
    rows, width = tokens.shape

    def body(own_ref, up_ref, down_ref, token_ref, gain_ref, hidden_ref, low_ref, unit_ref, inv_ref):
        total = (
            own_ref[...].astype(jnp.float32)
            + up_ref[...].astype(jnp.float32)
            + down_ref[...].astype(jnp.float32)
        )
        inv = lax.rsqrt(jnp.mean(total * total, axis=-1, keepdims=True) + NORM_EPS)
        unit = total * inv
        hidden = token_ref[...].astype(jnp.float32) + unit * gain_ref[...]
        hidden_ref[...] = hidden
        low_ref[...] = hidden.astype(LOW)
        unit_ref[...] = unit
        inv_ref[...] = inv

    full = jax.ShapeDtypeStruct((rows, width), jnp.float32)
    return pl.pallas_call(
        body,
        out_shape=[
            full,
            jax.ShapeDtypeStruct((rows, width), LOW),
            full,
            jax.ShapeDtypeStruct((rows, 1), jnp.float32),
        ],
        compiler_params=vmem(50),
        name="attn_norm",
    )(*parts, tokens, gains)


def mlp_norm(parts, hidden, cotangent, gains):
    rows, width = hidden.shape

    def body(own_ref, up_ref, down_ref, hidden_ref, grad_ref, gain_ref, out_ref, back_ref, sum_ref):
        total = (
            own_ref[...].astype(jnp.float32)
            + up_ref[...].astype(jnp.float32)
            + down_ref[...].astype(jnp.float32)
        )
        inv = lax.rsqrt(jnp.mean(total * total, axis=-1, keepdims=True) + NORM_EPS)
        unit = total * inv
        out_ref[...] = (hidden_ref[...] + unit * gain_ref[...]).astype(LOW)
        grad = grad_ref[...].astype(jnp.float32)
        sum_ref[...] = jnp.sum(grad * unit, axis=0, keepdims=True)
        scaled = grad * gain_ref[...]
        mean = jnp.mean(scaled * unit, axis=-1, keepdims=True)
        back_ref[...] = (inv * (scaled - unit * mean)).astype(LOW)

    return pl.pallas_call(
        body,
        out_shape=[jax.ShapeDtypeStruct((rows, width), LOW)] * 2
        + [jax.ShapeDtypeStruct((1, width), jnp.float32)],
        compiler_params=vmem(50),
        name="mlp_norm",
    )(*parts, hidden, cotangent, gains)


def attn_norm_back(parts, cotangent, unit, inv, gains):
    rows, width = unit.shape

    def body(
        own_ref, up_ref, down_ref, grad_ref, unit_ref, inv_ref, gain_ref, hidden_ref, back_ref, sum_ref
    ):
        grad = (
            grad_ref[...].astype(jnp.float32)
            + own_ref[...].astype(jnp.float32)
            + up_ref[...].astype(jnp.float32)
            + down_ref[...].astype(jnp.float32)
        )
        hidden_ref[...] = grad
        unit = unit_ref[...]
        sum_ref[...] = jnp.sum(grad * unit, axis=0, keepdims=True)
        scaled = grad * gain_ref[...]
        mean = jnp.mean(scaled * unit, axis=-1, keepdims=True)
        back_ref[...] = (inv_ref[...] * (scaled - unit * mean)).astype(LOW)

    return pl.pallas_call(
        body,
        out_shape=[
            jax.ShapeDtypeStruct((rows, width), jnp.float32),
            jax.ShapeDtypeStruct((rows, width), LOW),
            jax.ShapeDtypeStruct((1, width), jnp.float32),
        ],
        compiler_params=vmem(50),
        name="attn_norm_back",
    )(*parts, cotangent, unit, inv, gains)


def ff_totals(gate_up, down):
    height, units = down.shape
    steps = 4

    def body(gate_ref, up_ref, down_ref, gate_out, up_out, down_out):
        gate_out[...] = gate_ref[...].astype(jnp.float32)
        up_out[...] = up_ref[...].astype(jnp.float32)
        down_out[...] = down_ref[...].astype(jnp.float32).T

    tile = units // steps
    return pl.pallas_call(
        body,
        grid=(steps,),
        in_specs=[
            pl.BlockSpec((height, tile), lambda j: (0, j)),
            pl.BlockSpec((height, tile), lambda j: (0, steps + j)),
            pl.BlockSpec((height, tile), lambda j: (0, j)),
        ],
        out_specs=[pl.BlockSpec((height, tile), lambda j: (0, j))] * 2
        + [pl.BlockSpec((tile, height), lambda j: (j, 0))],
        out_shape=[jax.ShapeDtypeStruct((height, units), jnp.float32)] * 2
        + [jax.ShapeDtypeStruct((units, height), jnp.float32)],
        compiler_params=vmem(50),
        name="ff_totals",
    )(gate_up, gate_up, down)


def plane_totals(sums, span):
    height, width = sums[0].shape
    more = width - 4 * span

    def body(*refs):
        outs = refs[3:]
        for k in range(5):
            columns = slice(k * span, min((k + 1) * span, width))
            total = (
                refs[0][:, columns].astype(jnp.float32)
                + refs[1][:, columns].astype(jnp.float32)
                + refs[2][:, columns].astype(jnp.float32)
            )
            outs[k][...] = total.T if k == 3 else total

    return pl.pallas_call(
        body,
        out_shape=[jax.ShapeDtypeStruct((height, span), jnp.float32)] * 3
        + [
            jax.ShapeDtypeStruct((span, height), jnp.float32),
            jax.ShapeDtypeStruct((height, more), jnp.float32),
        ],
        compiler_params=vmem(50),
        name="plane_totals",
    )(*sums)


def weight_tiles(width, tile, tiles):
    return [pl.BlockSpec((width, tile), lambda j, k=k: (0, k * tiles + j)) for k in range(3)]


def feed_forward(pieces, weights):
    count = len(pieces)
    own, width = pieces[0].shape
    hidden_units = weights.shape[1] // 3
    tile = 512
    tiles = hidden_units // tile
    parts = 4 * count // 7
    rows = parts * own

    def body(*refs):
        ins, (gate_w, up_w, down_w) = refs[:count], refs[count : count + 3]
        rows_ref, gate_ref, up_ref, mixed_ref, *outs = refs[count + 3 : -1]
        total = refs[-1]

        @pl.when(pl.program_id(0) == 0)
        def _():
            fill_slots(rows_ref, ins)

        gate = jnp.dot(rows_ref[...], gate_w[...], preferred_element_type=jnp.float32)
        up = jnp.dot(rows_ref[...], up_w[...], preferred_element_type=jnp.float32)
        mixed = (gate * jax.nn.sigmoid(gate) * up).astype(LOW)
        gate_ref[...] = gate.astype(LOW)
        up_ref[...] = up.astype(LOW)
        mixed_ref[...] = mixed
        part = scores_of(mixed, down_w[...])

        @pl.when(pl.program_id(0) == 0)
        def _():
            total[...] = part

        @pl.when((pl.program_id(0) > 0) & (pl.program_id(0) < tiles - 1))
        def _():
            total[...] += part

        @pl.when(pl.program_id(0) == tiles - 1)
        def _():
            for t in range(parts):
                mine = slice(t * own, (t + 1) * own)
                outs[t][...] = (total[mine] + part[mine]).astype(LOW)

    fixed = pl.BlockSpec((own, width), lambda j: (0, 0))
    by_tile = pl.BlockSpec((rows, tile), lambda j: (0, j))
    return pl.pallas_call(
        body,
        grid=(tiles,),
        in_specs=[fixed] * count + weight_tiles(width, tile, tiles),
        out_specs=[pl.BlockSpec((rows, width), lambda j: (0, 0))] + [by_tile] * 3 + [fixed] * parts,
        out_shape=[jax.ShapeDtypeStruct((rows, width), LOW)]
        + [jax.ShapeDtypeStruct((rows, hidden_units), LOW)] * 3
        + [jax.ShapeDtypeStruct((own, width), LOW)] * parts,
        scratch_shapes=[pltpu.VMEM((rows, width), jnp.float32)],
        compiler_params=vmem(50),
        cost_estimate=pl.CostEstimate(
            flops=6 * rows * width * hidden_units,
            bytes_accessed=6 * width * hidden_units + 8 * rows * hidden_units,
            transcendentals=0,
        ),
        name="feed_forward",
    )(*pieces, weights, weights, weights)


def feed_forward_back(rows_low, gate, up, weights, parts):
    rows, width = rows_low.shape
    own = rows // parts
    hidden_units = gate.shape[1]
    tile = 512
    tiles = hidden_units // tile

    def body(rows_ref, gate_ref, up_ref, gate_w, up_w, down_w, grad_gate_ref, grad_up_ref, *refs):
        outs, total = refs[:parts], refs[parts]
        grad_mixed = jnp.dot(rows_ref[...], down_w[...], preferred_element_type=jnp.float32)
        gate = gate_ref[...].astype(jnp.float32)
        up = up_ref[...].astype(jnp.float32)
        sig = jax.nn.sigmoid(gate)
        grad_gate = (grad_mixed * up * sig * (1.0 + gate * (1.0 - sig))).astype(LOW)
        grad_up = (grad_mixed * gate * sig).astype(LOW)
        grad_gate_ref[...] = grad_gate
        grad_up_ref[...] = grad_up
        part = scores_of(grad_gate, gate_w[...]) + scores_of(grad_up, up_w[...])

        @pl.when(pl.program_id(0) == 0)
        def _():
            total[...] = part

        @pl.when((pl.program_id(0) > 0) & (pl.program_id(0) < tiles - 1))
        def _():
            total[...] += part

        @pl.when(pl.program_id(0) == tiles - 1)
        def _():
            for t in range(parts):
                mine = slice(t * own, (t + 1) * own)
                outs[t][...] = (total[mine] + part[mine]).astype(LOW)

    fixed = pl.BlockSpec((own, width), lambda j: (0, 0))
    by_tile = pl.BlockSpec((rows, tile), lambda j: (0, j))
    return pl.pallas_call(
        body,
        grid=(tiles,),
        in_specs=[pl.BlockSpec((rows, width), lambda j: (0, 0))]
        + [by_tile] * 2
        + weight_tiles(width, tile, tiles),
        out_specs=[by_tile] * 2 + [fixed] * parts,
        out_shape=[jax.ShapeDtypeStruct((rows, hidden_units), LOW)] * 2
        + [jax.ShapeDtypeStruct((own, width), LOW)] * parts,
        scratch_shapes=[pltpu.VMEM((rows, width), jnp.float32)],
        compiler_params=vmem(50),
        cost_estimate=pl.CostEstimate(
            flops=6 * rows * width * hidden_units,
            bytes_accessed=6 * width * hidden_units + 8 * rows * hidden_units,
            transcendentals=0,
        ),
        name="feed_forward_back",
    )(rows_low, gate, up, weights, weights, weights)


def down_grad(pieces, mixed):
    count = len(pieces)
    own, width = pieces[0].shape
    rows, columns = mixed.shape
    tile = 512

    def body(*refs):
        rows_ref, out_ref = refs[count + 1], refs[count + 2]

        @pl.when(pl.program_id(0) == 0)
        def _():
            fill_slots(rows_ref, refs[:count])

        place = pl.ds(pl.multiple_of(pl.program_id(0) * tile, tile), tile)
        out_ref[...] = contract(rows_ref[:, place], refs[count][...], 0, 0).astype(LOW)

    return pl.pallas_call(
        body,
        grid=(width // tile,),
        in_specs=[pl.BlockSpec((own, width), lambda j: (0, 0))] * count
        + [pl.BlockSpec((rows, columns), lambda j: (0, 0))],
        out_specs=[
            pl.BlockSpec((rows, width), lambda j: (0, 0)),
            pl.BlockSpec((tile, columns), lambda j: (j, 0)),
        ],
        out_shape=[
            jax.ShapeDtypeStruct((rows, width), LOW),
            jax.ShapeDtypeStruct((width, columns), LOW),
        ],
        compiler_params=vmem(50),
        cost_estimate=pl.CostEstimate(
            flops=2 * rows * width * columns,
            bytes_accessed=2 * (width * columns + rows * (width + columns)),
            transcendentals=0,
        ),
        name="down_grad",
    )(*pieces, mixed)


def weight_grad(left, right, all_columns, place, others=None):
    rows, width = left.shape
    columns = right.shape[1]
    tile = 512

    def body(left_ref, right_ref, *refs):
        refs[-1][...] = contract(left_ref[...], right_ref[...], 0, 0).astype(LOW)

    given = () if others is None else (others,)
    return pl.pallas_call(
        body,
        grid=(width // tile,),
        in_specs=[
            pl.BlockSpec((rows, tile), lambda j: (0, j)),
            pl.BlockSpec((rows, columns), lambda j: (0, 0)),
        ]
        + [pl.BlockSpec(memory_space=pl.ANY)] * len(given),
        out_specs=pl.BlockSpec((tile, columns), lambda j: (j, place)),
        out_shape=jax.ShapeDtypeStruct((width, all_columns), LOW),
        input_output_aliases={2: 0} if given else {},
        compiler_params=vmem(50),
        cost_estimate=pl.CostEstimate(
            flops=2 * rows * width * columns,
            bytes_accessed=2 * (width * columns + rows * (width + columns)),
            transcendentals=0,
        ),
        name="weight_grad",
    )(left, right, *given)


def on_plane(
    tokens,
    w_query,
    w_key,
    w_value,
    w_out,
    w_gate,
    w_up,
    w_down,
    q_gain,
    k_gain,
    attn_gain,
    mlp_gain,
    cotangent,
):
    seqs, length, d_model = tokens.shape
    rows = seqs * length
    tp_rank = lax.axis_index("tp")
    seq_rank = lax.axis_index("seq")
    heads = q_gain.shape[0]
    head_dim = q_gain.shape[1] * 8
    head_span = heads * head_dim
    own_length = length // 4
    own_rows = seqs * own_length
    order = (lax.axis_index("dp") * 4 + seq_rank) ^ jnp.arange(8, dtype=jnp.int32)
    slots = (tp_rank + 4 - jnp.arange(4, dtype=jnp.int32)) % 4

    gain_rows = jnp.concatenate([q_gain, k_gain, attn_gain, mlp_gain], axis=0)
    all_gains = lax.all_to_all(
        jnp.broadcast_to(gain_rows.reshape(1, -1), (8, gain_rows.size)), ("dp", "seq"), 0, 0, tiled=True
    )
    packed = jnp.concatenate([w_gate, w_up, w_down.T], axis=1)
    in_shard = jnp.concatenate([w_query, w_key, w_value], axis=1)
    in_pieces, (all_gains, packed) = gather_plane(
        in_shard, first_step(in_shard), (all_gains, packed)
    )
    all_gains = (
        jnp.transpose(all_gains.reshape((8,) + gain_rows.shape), (1, 0, 2))
        .reshape(gain_rows.shape[0], head_dim)
        .astype(jnp.float32)
    )
    qk_gain = all_gains[: 2 * heads].reshape(1, 2 * head_span)
    feature_rows = d_model // head_dim
    attn_gains = all_gains[2 * heads : 2 * heads + feature_rows].reshape(1, d_model)
    mlp_gains = all_gains[2 * heads + feature_rows :].reshape(1, d_model)
    positions = seq_rank * length + jnp.arange(length, dtype=jnp.int32)
    cosines, sines = rope_tables(positions, head_dim)
    cosines = jnp.concatenate([cosines[:, 0], cosines[:, 0]], axis=-1)
    sines = jnp.concatenate([-sines[:, 0], sines[:, 0]], axis=-1)
    own_tokens = lax.dynamic_slice_in_dim(tokens, tp_rank * own_length, own_length, 1).reshape(
        own_rows, d_model
    )
    grad_out = cotangent.reshape(own_rows, d_model)
    out_rows = lax.all_gather(w_out, "tp", axis=0, tiled=True)

    raw, in_weights = project_in(tokens.reshape(rows, d_model), in_pieces, order)
    out_firsts = first_step(after(w_out, in_pieces[3:5]))
    weights = lax.all_gather(after(packed, (in_pieces[3:5], out_rows)), ("dp", "seq"), axis=0, tiled=True)

    squares = jnp.stack(
        [
            jnp.sum(jnp.square(raw[:, :head_span]), axis=-1),
            jnp.sum(jnp.square(raw[:, head_span : 2 * head_span]), axis=-1),
        ]
    )
    raw, out_firsts = lax.optimization_barrier((raw, out_firsts))
    squares = sum_line(squares)
    squares = squares.reshape(2, seqs, length, 1)
    out_pieces, _ = gather_plane(w_out, out_firsts)
    raw = raw.reshape(seqs, length, 3 * head_span)
    parts = prepare(raw, squares, qk_gain, cosines, sines, heads, head_dim, d_model)
    parts, out_pieces[3:5] = lax.optimization_barrier((parts, out_pieces[3:5]))
    parts = lax.all_to_all(parts, "seq", 0, 0, tiled=True)
    parts, out_pieces = lax.optimization_barrier((parts, out_pieces))
    out_weights = assemble_columns(out_pieces, order)
    context, log_total = attend(parts)
    context = lax.all_to_all(context, "seq", 0, 0, tiled=True)
    context_rows, *attn_slots = project_out(context, out_weights, slots)
    hidden, hidden_low, attn_unit, attn_inv = attn_norm(
        scatter_line(attn_slots)[0], own_tokens, attn_gains
    )
    out_columns = after(out_rows, hidden_low).T
    out_columns = lax.all_gather(out_columns, ("dp", "seq"), axis=0, tiled=True)
    hidden_rows, gate, up, mixed, *mlp_slots = feed_forward(gather_line(hidden_low), weights)
    outputs, grad_mlp, grad_mgain = mlp_norm(
        scatter_line(mlp_slots)[0], hidden, grad_out, mlp_gains
    )
    grad_mlp, out_columns = lax.optimization_barrier((grad_mlp, out_columns))
    grad_mlp_rows, down_part = down_grad(gather_line(grad_mlp), mixed)
    grad_gate, grad_up, *hidden_slots = feed_forward_back(grad_mlp_rows, gate, up, weights, 4)
    units = mixed.shape[1]
    gate_part = weight_grad(hidden_rows, grad_gate, 2 * units, 0)
    gate_up_part = weight_grad(hidden_rows, grad_up, 2 * units, 1, gate_part)
    hidden_sum, (gate_part, gate_up_part) = scatter_line(hidden_slots, (gate_part, gate_up_part))

    def sum_plane(part):
        return lax.optimization_barrier(
            lax.psum_scatter(part, ("dp", "seq"), scatter_dimension=0, tiled=True)
        )

    down_sum = sum_plane(down_part)
    gate_up_sum = sum_plane(gate_up_part)
    ff_sums = ff_totals(gate_up_sum, down_sum)

    grad_hidden, grad_attn, grad_again = attn_norm_back(
        hidden_sum, grad_out, attn_unit, attn_inv, attn_gains
    )
    grad_context = project_out_back(grad_attn, out_columns, heads, head_dim, seqs)
    grad_context = lax.all_to_all(
        grad_context.reshape((16,) + grad_context.shape[2:]), ("seq", "tp"), 0, 0, tiled=True
    ).reshape(grad_context.shape)
    part_grads = attend_back(parts, grad_context, log_total)
    part_grads = lax.all_to_all(part_grads, "seq", 0, 0, tiled=True)
    grad_attn_rows = rows_of(gather_line(grad_attn))
    own_gains = lax.all_to_all(
        jnp.concatenate([grad_again.reshape(4, 4, -1), grad_mgain.reshape(4, 4, -1)], axis=1),
        "tp",
        0,
        0,
        tiled=True,
    )
    part_grads, grad_attn_rows, own_gains = lax.optimization_barrier(
        (part_grads, grad_attn_rows, own_gains)
    )
    own_gains = jnp.sum(own_gains, axis=0)
    scaled, dots, qk_sums = unprepare(part_grads, raw, squares, qk_gain, cosines, sines, d_model)
    dots = sum_line(dots.reshape(2, rows)).reshape(2, seqs, length, 1)
    grad_raw, *token_slots = project_in_back(
        part_grads, scaled, raw, squares, dots, in_weights, slots
    )
    gain_parts = jnp.concatenate([qk_sums.reshape(2, heads, 8, -1), own_gains.reshape(2, heads, 8, -1)])
    gain_parts = jnp.transpose(gain_parts, (2, 0, 1, 3)).reshape(8, -1, 128)
    gain_rows_used = gain_parts.shape[1]
    gain_parts = jnp.pad(
        gain_parts, ((0, 0), (0, d_model // 8 - gain_rows_used), (0, 0))
    ).reshape(d_model, 128)
    far_sent, near = sum_in_plane(
        (tokens.reshape(rows, d_model), grad_attn_rows),
        (grad_raw, context_rows),
        gain_parts,
        order,
    )
    token_sums, (_, near) = scatter_line(token_slots, (far_sent, near))
    in_sums = [near[2], to_neighbour(near[0], 1), to_neighbour(near[1], 2)]
    in_sums, ff_sums = lax.optimization_barrier((in_sums, ff_sums))
    *in_sums, gain_sums = plane_totals(in_sums, head_span)
    grad_tokens = grad_hidden
    for part in token_sums:
        grad_tokens = grad_tokens + part.astype(jnp.float32)

    gain_sums = gain_sums[:gain_rows_used].reshape(4, heads, -1)
    return (
        outputs.reshape(cotangent.shape),
        grad_tokens.reshape(cotangent.shape),
        *in_sums,
        ff_sums[0],
        ff_sums[1],
        ff_sums[2],
        gain_sums[0],
        gain_sums[1],
        gain_sums[2],
        gain_sums[3],
    )


def solution(mesh):
    by_plane = (mesh.shape["dp"], mesh.shape["seq"], mesh.shape["tp"]) == (2, 4, 4)
    return jax.shard_map(
        on_plane if by_plane else on_any_mesh,
        mesh=mesh,
        in_specs=(
            P("dp", "seq", None),
            P(("dp", "seq"), "tp"),
            P(("dp", "seq"), "tp"),
            P(("dp", "seq"), "tp"),
            P("tp", ("dp", "seq")),
            P(("dp", "seq"), "tp"),
            P(("dp", "seq"), "tp"),
            P("tp", ("dp", "seq")),
            P("tp", ("dp", "seq")),
            P("tp", ("dp", "seq")),
            P(None, ("dp", "seq")),
            P(None, ("dp", "seq")),
            P("dp", ("seq", "tp"), None),
        ),
        out_specs=(
            P("dp", ("seq", "tp"), None),
            P("dp", ("seq", "tp"), None),
            P(("dp", "seq"), "tp"),
            P(("dp", "seq"), "tp"),
            P(("dp", "seq"), "tp"),
            P("tp", ("dp", "seq")),
            P(("dp", "seq"), "tp"),
            P(("dp", "seq"), "tp"),
            P("tp", ("dp", "seq")),
            P("tp", ("dp", "seq")),
            P("tp", ("dp", "seq")),
            P("tp", ("dp", "seq")),
            P("tp", ("dp", "seq")),
        ),
        check_vma=False,
    )
```
